32 devices in a mesh: dp: 16 (over z, y, core), tensor: 2 (over x).
Axes of the slice: x: 2, y: 2, z: 4, core: 2. Of those that a mesh axis runs over, the one named last changes fastest.
Arguments:
- inputs: bfloat16 [32768, 768], P(('dp', 'tensor')), may hold values from -6 to 6
- gain_attn: bfloat16 [768], replicated, may hold values from 0.5 to 1.5
- w_query: bfloat16 [768, 768], P(None, 'tensor'), may hold values from -0.09375 to 0.09375
- w_key: bfloat16 [768, 768], P(None, 'tensor'), may hold values from -0.09375 to 0.09375
- w_value: bfloat16 [768, 768], P(None, 'tensor'), may hold values from -0.21875 to 0.21875
- w_output: bfloat16 [768, 768], P('tensor'), may hold values from -0.875 to 0.875
- relative_bias_table: bfloat16 [32, 12], P(None, 'tensor'), may hold values from -4 to 4
- gain_ffn: bfloat16 [768], replicated, may hold values from 0.5 to 1.5
- w_inner: bfloat16 [768, 3072], P(None, 'tensor'), may hold values from -0.21875 to 0.21875
- w_outer: bfloat16 [3072, 768], P('tensor'), may hold values from -0.109375 to 0.109375
- lengths: int32 [128], P('dp'), may hold values from 40 to 256, as said below
- cotangent: bfloat16 [32768, 768], P(('dp', 'tensor')), may hold values from -6 to 6
Outputs:
- layer_out: bfloat16 [32768, 768], P(('dp', 'tensor'))
- grad_input: float32 [32768, 768], P(('dp', 'tensor'))
- grad_gain_attn: float32 [768], replicated
- grad_query: float32 [768, 768], P('dp', 'tensor')
- grad_key: float32 [768, 768], P('dp', 'tensor')
- grad_value: float32 [768, 768], P('dp', 'tensor')
- grad_output: float32 [768, 768], P('tensor', 'dp')
- grad_table: float32 [32, 12], P(None, 'tensor')
- grad_gain_ffn: float32 [768], replicated
- grad_inner: float32 [768, 3072], P('dp', 'tensor')
- grad_outer: float32 [3072, 768], P('tensor', 'dp')
The draws below stay inside these ranges and needn't reach their ends.
Inputs may be any that keep to these rules, and one draw needn't show every extreme that they name: Each passage's valid keys are its first lengths slots; in every draw some passage has all 256 slots valid and some has the fewest.
All inputs are finite; a program needn't handle non-finite values.
Results may differ from the reference program's by a relative error of at most 0.013.
The reference program's roundings to bfloat16 on the way count: a program that leaves them out, or rounds other values in their place, can miss the bound.
Values may be sent and summed in bfloat16 or wider, within the bound.
No kernel may reach another device: no remote copies, remote signals or barrier semaphores. Data moves between devices by JAX's collectives and lax.ppermute only.
A program may use at most 192 MiB of HBM per device.

```python
import math
import jax
import jax.numpy as jnp
from jax import lax

D = 768
HEADS = 12
HEAD_DIM = 64
FF = 3072
BUCKETS = 32
SEQ = 256
PASSAGES = 128
TOKENS = 32768


def draw_lengths(key, part):
    key = jax.random.fold_in(key, 11)
    key_vals, key_first, key_second = jax.random.split(key, 3)
    shortest = SEQ * 5 // 32
    values = jax.random.randint(key_vals, (PASSAGES,), shortest, SEQ + 1, dtype=jnp.int32)
    first = jax.random.randint(key_first, (), 0, PASSAGES, dtype=jnp.int32)
    second = (first + 1 + jax.random.randint(key_second, (), 0, PASSAGES - 1, dtype=jnp.int32)) % PASSAGES
    values = values.at[first].set(SEQ)
    values = values.at[second].set(shortest)
    return values.astype(jnp.int32)


def steps_of(key, extent, cuts, least, top_value):
    level = 1.0
    for dim, parts in cuts:
        draws = jax.random.uniform(jax.random.fold_in(jax.random.fold_in(key, 6), dim), (parts,), jnp.float32, least / len(cuts), top_value / len(cuts))
        level = level * jnp.repeat(jnp.exp(draws), extent[dim] // parts).reshape((-1,) + (1,) * (len(extent) - 1 - dim))
    return level


def normal_values(rng, extent, width, most, shards=(), held_as=jnp.bfloat16):
    values = width * jax.random.normal(rng, extent, jnp.float32)
    if shards:
        values = values * steps_of(rng, extent, shards, -0.22, 0.18)
    return jnp.clip(values, -most, most).astype(held_as)


def setup_inputs(seed: int = 0) -> dict:
    streams_of = jax.random.split(jax.random.key(seed), 13)
    inputs = normal_values(streams_of[0], (TOKENS, D), 1.0, 6.0, ((0, 32),))
    gain_attn = jnp.clip(1.0 + 0.1 * jax.random.normal(streams_of[1], (D,), jnp.float32), 0.5, 1.5).astype(jnp.bfloat16)
    w_query = normal_values(streams_of[2], (D, D), (5 * D) ** -0.5, 0.09375, ((1, 2),))
    w_key = normal_values(streams_of[3], (D, D), (5 * D) ** -0.5, 0.09375, ((1, 2),))
    w_value = normal_values(streams_of[4], (D, D), D ** -0.5, 0.21875, ((1, 2),))
    w_output = normal_values(streams_of[5], (D, D), (D // 16) ** -0.5, 0.875, ((0, 2),))
    relative_bias_table = normal_values(streams_of[6], (BUCKETS, HEADS), 1.0, 4.0, ((1, 2),))
    gain_ffn = jnp.clip(1.0 + 0.1 * jax.random.normal(streams_of[7], (D,), jnp.float32), 0.5, 1.5).astype(jnp.bfloat16)
    w_inner = normal_values(streams_of[8], (D, FF), D ** -0.5, 0.21875, ((1, 2),))
    w_outer = normal_values(streams_of[9], (FF, D), FF ** -0.5, 0.109375, ((0, 2),))
    lengths = draw_lengths(jax.random.fold_in(streams_of[12], 71), 0)
    cotangent = normal_values(streams_of[11], (TOKENS, D), 1.0, 6.0, ((0, 32),))
    return {"inputs": inputs, "gain_attn": gain_attn, "w_query": w_query, "w_key": w_key, "w_value": w_value, "w_output": w_output, "relative_bias_table": relative_bias_table, "gain_ffn": gain_ffn, "w_inner": w_inner, "w_outer": w_outer, "lengths": lengths, "cotangent": cotangent}


@jax.custom_vjp
def low(v):
    return lax.optimization_barrier(v.astype(jnp.bfloat16)).astype(jnp.float32)

@jax.custom_vjp
def low_back(v):
    return v

def low_keep(v):
    return (low(v), None)

def low_pass(kept, grad):
    return (grad,)

def back_keep(v):
    return (v, None)

def back_low(kept, grad):
    return (low(grad),)
low.defvjp(low_keep, low_pass)
low_back.defvjp(back_keep, back_low)
PRECISE_MATMUL = lax.Precision.HIGHEST

def low_both(values):
    return low(low_back(values))

def matmul_hi(left, right):
    return jnp.dot(left, right, precision=PRECISE_MATMUL)

def rms_norm(values, gain):
    return values * lax.rsqrt(lax.optimization_barrier(jnp.mean(values * values, axis=-1, keepdims=True)) + 1e-06) * gain

def bucket_ids(seq_len):
    positions = jnp.arange(seq_len, dtype=jnp.int32)
    offsets = positions[None, :] - positions[:, None]
    distance = jnp.abs(offsets)
    far_bucket = jnp.full_like(distance, 8)
    for power in range(1, 8):
        far_bucket = far_bucket + (distance * distance >= 64 * 2 ** power).astype(jnp.int32)
    near_bucket = jnp.where(distance < 8, distance, far_bucket)
    return near_bucket + 16 * (offsets > 0).astype(jnp.int32)

def forward(inputs_f, gain_one, w_query_f, w_key_f, w_value_f, w_output_f, table_float, gain_two, w_inner_f, w_outer_f, key_mask, bucket_indicator):
    rows_one = low(rms_norm(inputs_f, gain_one))
    shape_five = (PASSAGES, SEQ, HEADS, HEAD_DIM)
    query = low_both(matmul_hi(rows_one, w_query_f)).reshape(shape_five)
    keyset = low_both(matmul_hi(rows_one, w_key_f)).reshape(shape_five)
    values = low_both(matmul_hi(rows_one, w_value_f)).reshape(shape_five)
    expanded_bias = jnp.einsum('utc,ul->ltc', bucket_indicator, table_float, precision=PRECISE_MATMUL)
    per_block = math.gcd(PASSAGES, max(1, 4096 // SEQ))
    block_count = PASSAGES // per_block

    def attend(pieces):
        part_q, part_k, part_v, part_m = pieces
        logits = low_back(jnp.einsum('pqhe,pkhe->phqk', part_q, part_k, precision=PRECISE_MATMUL) + expanded_bias)
        logits = jnp.where(part_m[:, None, None, :], logits, -1000000000.0)
        probs = jax.nn.softmax(logits, axis=-1)
        return jnp.einsum('phqk,pkhe->pqhe', low(probs), part_v, precision=PRECISE_MATMUL)

    def split_blocks(array):
        return array.reshape((block_count, per_block) + array.shape[1:])
    context = lax.map(jax.checkpoint(attend), (split_blocks(query), split_blocks(keyset), split_blocks(values), split_blocks(key_mask)))
    context = low_both(context.reshape(TOKENS, D))
    attn_out = low_back(matmul_hi(context, w_output_f))
    residual = inputs_f + attn_out
    rows_two = low(rms_norm(residual, gain_two))
    pre_act = low_back(matmul_hi(rows_two, w_inner_f))
    active = low(jax.nn.gelu(pre_act))
    ffn_out = low_back(matmul_hi(active, w_outer_f))
    return residual + ffn_out

def reference(inputs, gain_attn, w_query, w_key, w_value, w_output, relative_bias_table, gain_ffn, w_inner, w_outer, lengths, cotangent):
    key_mask = jnp.arange(SEQ, dtype=jnp.int32)[None, :] < lengths[:, None]
    bucket_indicator = (bucket_ids(SEQ)[None, :, :] == jnp.arange(BUCKETS, dtype=jnp.int32)[:, None, None]).astype(jnp.float32)

    def wrapped(inputs_f, gain_one, w_query_f, w_key_f, w_value_f, w_output_f, table_float, gain_two, w_inner_f, w_outer_f):
        return forward(inputs_f, gain_one, w_query_f, w_key_f, w_value_f, w_output_f, table_float, gain_two, w_inner_f, w_outer_f, key_mask, bucket_indicator)
    floats = [arg.astype(jnp.float32) for arg in (inputs, gain_attn, w_query, w_key, w_value, w_output, relative_bias_table, gain_ffn, w_inner, w_outer)]
    layer_out, pullback = jax.vjp(wrapped, *floats)
    grads = pullback(cotangent.astype(jnp.float32))
    return (layer_out.astype(jnp.bfloat16), grads[0], grads[1], grads[2], grads[3], grads[4], grads[5], grads[6], grads[7], grads[8], grads[9])
```

```python
import functools

import jax
import jax.numpy as jnp
from jax import lax
from jax.experimental import pallas as pl
from jax.experimental.pallas import tpu as pltpu
from jax.sharding import PartitionSpec as P

HEAD_DIM = 64
BUCKETS = 32
EPS = 1e-6
MASKED = -1e9
GELU_C = 0.7978845608028654
VMEM_BYTES = 60 * 1024 * 1024
F32 = jnp.float32
BF16 = jnp.bfloat16


def dot(left, right):
    return lax.dot_general(left, right, (((1,), (0,)), ((), ())), preferred_element_type=F32)


def dot_t(left, right):
    return lax.dot_general(left, right, (((1,), (1,)), ((), ())), preferred_element_type=F32)


def bucket_of(offsets):
    distance = jnp.abs(offsets)
    far = jnp.full_like(distance, 8)
    for power in range(1, 8):
        far = far + (distance * distance >= 64 * 2**power).astype(jnp.int32)
    near = jnp.where(distance < 8, distance, far)
    return near + jnp.where(offsets > 0, 16, 0)


def bucket_indicator(seq):
    lane = lax.broadcasted_iota(jnp.int32, (BUCKETS, 2 * seq), 1)
    offsets = jnp.where(lane < seq, -lane, 2 * seq - lane)
    ids = lax.broadcasted_iota(jnp.int32, (BUCKETS, 2 * seq), 0)
    return (bucket_of(offsets) == ids).astype(F32)


def fill_bias(table_ref, bias_ref):
    heads, seq, _ = bias_ref.shape
    base = dot(table_ref[...], bucket_indicator(seq).astype(BF16))
    for h in range(heads):
        wide = jnp.broadcast_to(base[h : h + 1, :], (seq, 2 * seq))
        bias_ref[h] = pltpu.roll(wide, 0, 1, stride=1, stride_axis=0)[:, :seq]


def head_mask(columns, parity):
    lane = lax.broadcasted_iota(jnp.int32, columns.shape, 1)
    keep = (lane < HEAD_DIM) if parity == 0 else (lane >= HEAD_DIM)
    return jnp.where(keep, columns, jnp.zeros_like(columns))


def rms_rows(values, gain):
    return values * lax.rsqrt(jnp.mean(values * values, axis=-1, keepdims=True) + EPS) * gain


def rms_back(values, gain, grads):
    scale = lax.rsqrt(jnp.mean(values * values, axis=-1, keepdims=True) + EPS)
    scaled = grads * gain
    mean = jnp.mean(scaled * values, axis=-1, keepdims=True)
    back = scale * scaled - values * (scale * scale * scale * mean)
    return back, jnp.sum(grads * values * scale, axis=0, keepdims=True)


def attend(length, rows, wq_ref, wk_ref, wv_ref, bias_ref, q_ref, k_ref, v_ref, lse_ref):
    seq = rows.shape[0]
    heads = bias_ref.shape[0]
    query = dot(rows, wq_ref[...]).astype(BF16)
    keys = dot(rows, wk_ref[...]).astype(BF16)
    vals = dot(rows, wv_ref[...]).astype(BF16)
    q_ref[...] = query
    k_ref[...] = keys
    v_ref[...] = vals
    query_t = query.T
    vals_t = vals.T
    valid = lax.broadcasted_iota(jnp.int32, (seq, 1), 0) < length
    parts = []
    for h in range(heads):
        lo = (h // 2) * 2 * HEAD_DIM
        key_h = head_mask(keys[:, lo : lo + 2 * HEAD_DIM], h % 2)
        logits = dot(key_h, query_t[lo : lo + 2 * HEAD_DIM, :]) + bias_ref[h]
        logits = jnp.where(valid, logits, MASKED)
        peak = jnp.max(logits, axis=0, keepdims=True)
        terms = jnp.exp(logits - peak)
        total = jnp.sum(terms, axis=0, keepdims=True)
        probs = (terms * (1.0 / total)).astype(BF16)
        lse_ref[0, h : h + 1, :] = peak + jnp.log(total)
        parts.append(dot(vals_t[h * HEAD_DIM : (h + 1) * HEAD_DIM, :], probs))
    return jnp.concatenate(parts, axis=0).astype(BF16).T


def attn_first_kernel(
    len_ref, x_ref, gain_ref, cot_ref, perm_ref, wq_ref, wk_ref, wv_ref, table_ref,
    rows_ref, rows_t_ref, cot_t_ref, q_ref, k_ref, v_ref, ctx_ref, lse_ref, bias_ref,
):
    p = pl.program_id(0)

    @pl.when(p == 0)
    def _():
        fill_bias(table_ref, bias_ref)

    rows = rms_rows(x_ref[...].astype(F32), gain_ref[...]).astype(BF16)
    rows_ref[...] = rows
    rows_t_ref[...] = dot_t(perm_ref[...], rows).astype(BF16)
    cot_t_ref[...] = dot_t(perm_ref[...], cot_ref[...]).astype(BF16)
    ctx_ref[...] = attend(
        len_ref[p], rows, wq_ref, wk_ref, wv_ref, bias_ref, q_ref, k_ref, v_ref, lse_ref
    )


def attn_second_kernel(
    len_ref, x_ref, gain_ref, rows_ref, ctx_first_ref, perm_ref, wq_ref, wk_ref, wv_ref,
    wo_first_ref, wo_ref, table_ref,
    q_ref, k_ref, v_ref, ctx_ref, lse_ref, resid_ref, rows_two_ref, rows_two_t_ref, bias_ref,
):
    p = pl.program_id(0)

    @pl.when(p == 0)
    def _():
        fill_bias(table_ref, bias_ref)

    context = attend(
        len_ref[p], rows_ref[...], wq_ref, wk_ref, wv_ref, bias_ref, q_ref, k_ref, v_ref, lse_ref
    )
    ctx_ref[...] = context
    branch = dot(ctx_first_ref[...], wo_first_ref[...]) + dot(context, wo_ref[...])
    residual = x_ref[...].astype(F32) + branch
    resid_ref[...] = residual
    rows_two = rms_rows(residual, gain_ref[...]).astype(BF16)
    rows_two_ref[...] = rows_two
    rows_two_t_ref[...] = dot_t(perm_ref[...], rows_two).astype(BF16)


def ffn_block(
    rows_ref, rows_t_ref, cot_ref, cot_t_ref, wi_ref, wo_ref, ffn_ref, back_ref,
    send_ref, keep_ref, act_ref, grad_ref, chunk,
):
    count = rows_ref.shape[0] // chunk

    def step(i, carry):
        at = pl.ds(i * chunk, chunk)
        v = dot(rows_ref[at, :], wi_ref[...])
        grad_act = dot_t(cot_ref[at, :], wo_ref[...])
        square = v * v
        tanh = jnp.tanh(GELU_C * v * (1.0 + 0.044715 * square))
        half = 0.5 + 0.5 * tanh
        act = (v * half).astype(BF16)
        slope = half + (0.5 * GELU_C) * v * (1.0 - tanh * tanh) * (1.0 + 0.134145 * square)
        grad = (grad_act * slope).astype(BF16)
        act_ref[at, :] = act
        grad_ref[at, :] = grad
        ffn_ref[at, :] += dot(act, wo_ref[...])
        back_ref[at, :] += dot_t(grad, wi_ref[...])
        return carry

    lax.fori_loop(0, count, step, 0)
    half_rows = keep_ref.shape[1]
    part = half_rows // 2

    def weights(i, carry):
        at = pl.ds(i * part, part)
        after = pl.ds(half_rows + i * part, part)
        keep_ref[0, at, :] = dot(rows_t_ref[at, :], grad_ref[...]).astype(BF16)
        keep_ref[1, at, :] = dot(cot_t_ref[at, :], act_ref[...]).astype(BF16)
        send_ref[0, at, :] = dot(rows_t_ref[after, :], grad_ref[...]).astype(BF16)
        send_ref[1, at, :] = dot(cot_t_ref[after, :], act_ref[...]).astype(BF16)
        return carry

    lax.fori_loop(0, 2, weights, 0)


def ffn_first_kernel(
    rows_ref, rows_t_ref, cot_ref, cot_t_ref, wi_ref, wo_ref,
    ffn_ref, back_ref, send_ref, keep_ref, act_ref, grad_ref, *, chunk,
):
    @pl.when(pl.program_id(0) == 0)
    def _():
        ffn_ref[...] = jnp.zeros_like(ffn_ref)
        back_ref[...] = jnp.zeros_like(back_ref)

    ffn_block(
        rows_ref, rows_t_ref, cot_ref, cot_t_ref, wi_ref, wo_ref, ffn_ref, back_ref,
        send_ref, keep_ref, act_ref, grad_ref, chunk,
    )


def ffn_second_kernel(
    rows_ref, rows_t_ref, cot_ref, cot_t_ref, wi_ref, wo_ref, ffn_in_ref, back_in_ref,
    resid_ref, gain_ref, perm_ref,
    layer_ref, grad_resid_ref, grad_attn_ref, grad_attn_t_ref, gain_grad_ref, send_ref, keep_ref,
    ffn_ref, back_ref, act_ref, grad_ref, *, chunk,
):
    @pl.when(pl.program_id(0) == 0)
    def _():
        ffn_ref[...] = ffn_in_ref[...]
        back_ref[...] = back_in_ref[...]

    ffn_block(
        rows_ref, rows_t_ref, cot_ref, cot_t_ref, wi_ref, wo_ref, ffn_ref, back_ref,
        send_ref, keep_ref, act_ref, grad_ref, chunk,
    )

    @pl.when(pl.program_id(0) == pl.num_programs(0) - 1)
    def _():
        gain_grad_ref[...] = jnp.zeros_like(gain_grad_ref)

        def step(i, carry):
            at = pl.ds(i * chunk, chunk)
            residual = resid_ref[at, :]
            layer_ref[at, :] = (residual + ffn_ref[at, :]).astype(BF16)
            back, gain_part = rms_back(residual, gain_ref[...], back_ref[at, :])
            gain_grad_ref[...] += gain_part
            grad_resid = cot_ref[at, :].astype(F32) + back
            grad_resid_ref[at, :] = grad_resid
            grad_attn_ref[at, :] = grad_resid.astype(BF16)
            return carry

        lax.fori_loop(0, rows_ref.shape[0] // chunk, step, 0)
        half_rows = perm_ref.shape[0] // 2

        def turn(i, carry):
            at = pl.ds(i * half_rows, half_rows)
            grad_attn_t_ref[at, :] = dot_t(perm_ref[at, :], grad_attn_ref[...]).astype(BF16)
            return carry

        lax.fori_loop(0, 2, turn, 0)


def attn_back_kernel(
    len_ref, grad_attn_ref, wo_ref, q_ref, k_ref, v_ref, ctx_ref, lse_ref, table_ref,
    rows_t_ref, grad_attn_t_ref,
    dqkv_ref, send_ref, keep_ref, table_grad_ref, bias_ref, sums_ref, ctx_all_ref, *, seq,
):
    p = pl.program_id(0)
    heads = bias_ref.shape[0]
    width = heads * HEAD_DIM

    @pl.when(p == 0)
    def _():
        fill_bias(table_ref, bias_ref)
        sums_ref[...] = jnp.zeros_like(sums_ref)

    here = pl.ds(p * seq, seq)
    ctx_all_ref[here, :] = ctx_ref[...]
    grad_ctx = dot_t(grad_attn_ref[...], wo_ref[...]).astype(BF16)
    grad_ctx_t = grad_ctx.T
    query = q_ref[...]
    query_t = query.T
    keys = k_ref[...]
    keys_t = keys.T
    vals = v_ref[...]
    valid = lax.broadcasted_iota(jnp.int32, (seq, 1), 0) < len_ref[p]
    first_head = lax.broadcasted_iota(jnp.int32, (seq, 2 * HEAD_DIM), 1) < HEAD_DIM
    dq_parts, dk_parts, dv_parts = [], [], []
    for pair in range(heads // 2):
        lo = pair * 2 * HEAD_DIM
        both = slice(lo, lo + 2 * HEAD_DIM)
        for parity in range(2):
            h = 2 * pair + parity
            own = slice(h * HEAD_DIM, (h + 1) * HEAD_DIM)
            logits = dot(head_mask(keys[:, both], parity), query_t[both, :]) + bias_ref[h]
            probs = jnp.where(valid, jnp.exp(logits - lse_ref[0, h : h + 1, :]), 0.0)
            grad_probs = dot(head_mask(vals[:, both], parity), grad_ctx_t[both, :])
            mixed = jnp.sum(probs * grad_probs, axis=0, keepdims=True)
            grads = (probs * (grad_probs - mixed)).astype(BF16)
            sums_ref[h] += grads.astype(F32)
            dq_parts.append(dot(keys_t[own, :], grads))
            dk_parts.append(dot(grads, query[:, both]))
            dv_parts.append(dot(probs.astype(BF16), grad_ctx[:, both]))
    dq = jnp.concatenate(dq_parts, axis=0).astype(BF16).T
    dqkv_ref[here, :width] = dq
    for pair in range(heads // 2):
        lo = pair * 2 * HEAD_DIM
        dk = jnp.where(first_head, dk_parts[2 * pair], dk_parts[2 * pair + 1])
        dv = jnp.where(first_head, dv_parts[2 * pair], dv_parts[2 * pair + 1])
        dqkv_ref[here, width + lo : width + lo + 2 * HEAD_DIM] = dk.astype(BF16)
        dqkv_ref[here, 2 * width + lo : 2 * width + lo + 2 * HEAD_DIM] = dv.astype(BF16)

    @pl.when(p == pl.num_programs(0) - 1)
    def _():
        half_rows = keep_ref.shape[0]
        part = half_rows // 2

        def weights(i, carry):
            at = pl.ds(i * part, part)
            after = pl.ds(half_rows + i * part, part)
            keep_ref[at, : 3 * width] = dot(rows_t_ref[at, :], dqkv_ref[...]).astype(BF16)
            keep_ref[at, 3 * width :] = dot(grad_attn_t_ref[at, :], ctx_all_ref[...]).astype(BF16)
            send_ref[at, : 3 * width] = dot(rows_t_ref[after, :], dqkv_ref[...]).astype(BF16)
            send_ref[at, 3 * width :] = dot(grad_attn_t_ref[after, :], ctx_all_ref[...]).astype(BF16)
            return carry

        lax.fori_loop(0, 2, weights, 0)
        indicator = bucket_indicator(seq)
        lane = lax.broadcasted_iota(jnp.int32, table_grad_ref.shape, 1)
        table_grad = jnp.zeros_like(table_grad_ref)
        for h in range(heads):
            folded = jnp.zeros((8, 2 * seq), F32)
            for a in range(0, seq, 8):
                wide = jnp.concatenate([sums_ref[h, a : a + 8, :], jnp.zeros((8, seq), F32)], axis=1)
                folded = folded + (pltpu.roll(wide, 2 * seq - a, 1) if a else wide)
            diagonals = folded[0:1, :]
            for b in range(1, 8):
                diagonals = diagonals + pltpu.roll(folded[b : b + 1, :], 2 * seq - b, 1)
            column = jnp.sum(indicator * diagonals, axis=1, keepdims=True)
            table_grad = jnp.where(lane == h, column, table_grad)
        table_grad_ref[...] = table_grad


def input_back_kernel(
    x_ref, gain_ref, grad_resid_ref, d_first_ref, d_second_ref,
    wq_first_ref, wk_first_ref, wv_first_ref, wq_ref, wk_ref, wv_ref,
    grad_input_ref, gain_grad_ref,
):
    @pl.when(pl.program_id(0) == 0)
    def _():
        gain_grad_ref[...] = jnp.zeros_like(gain_grad_ref)

    width = wq_ref.shape[1]
    total = None
    for d_ref, refs in (
        (d_first_ref, (wq_first_ref, wk_first_ref, wv_first_ref)),
        (d_second_ref, (wq_ref, wk_ref, wv_ref)),
    ):
        for n, ref in enumerate(refs):
            term = dot_t(d_ref[:, n * width : (n + 1) * width], ref[...])
            total = term if total is None else total + term
    back, gain_part = rms_back(x_ref[...].astype(F32), gain_ref[...], total)
    grad_input_ref[...] = grad_resid_ref[...] + back
    gain_grad_ref[...] += gain_part


def whole_spec(array_shape):
    return pl.BlockSpec(array_shape, lambda i: (0,) * len(array_shape), pipeline_mode=pl.Buffered(1))


def call(kernel, grid, ins, outs, scratch, cost, name):
    arrays = [a for a, _ in ins]
    return pl.pallas_call(
        kernel,
        grid=grid,
        in_specs=[s for _, s in ins],
        out_specs=[s for _, _, s in outs],
        out_shape=[jax.ShapeDtypeStruct(s, d) for s, d, _ in outs],
        scratch_shapes=scratch,
        compiler_params=pltpu.CompilerParams(
            dimension_semantics=("arbitrary",), vmem_limit_bytes=VMEM_BYTES
        ),
        cost_estimate=pl.CostEstimate(flops=cost, bytes_accessed=cost // 1000, transcendentals=0),
        name=name,
    )(*arrays)


def shards(
    inputs, gain_attn, w_query, w_key, w_value, w_output, relative_bias_table,
    gain_ffn, w_inner, w_outer, lengths, cotangent, *, dp, tp,
):
    rows_n, width = inputs.shape
    passages = lengths.shape[0] // tp
    seq = rows_n // passages
    cols = w_query.shape[1]
    heads = cols // HEAD_DIM
    hidden = w_inner.shape[1]
    me = lax.axis_index("dp")
    side = lax.axis_index("tensor")
    core = me % 2
    rest = dp // 4

    def across(value, distance):
        return lax.ppermute(value, "dp", [(i, i ^ distance) for i in range(dp)])

    def beside(value):
        return lax.ppermute(value, "tensor", [(i, tp - 1 - i) for i in range(tp)])

    def fetch(weight):
        half = weight.shape[0] // 2
        mine = lax.dynamic_slice_in_dim(weight, core * half, half, 0)
        got = beside(mine)
        other = across(got, 1)
        return jnp.where(
            core == 0,
            jnp.concatenate([got, other], axis=0),
            jnp.concatenate([other, got], axis=0),
        )

    table = jnp.pad(relative_bias_table.T, ((0, 16 - heads), (0, 0)))
    table_far = beside(table)
    qkv_far = fetch(jnp.concatenate([w_query, w_key, w_value], axis=1))
    wq_far, wk_far, wv_far = (qkv_far[:, n * cols : (n + 1) * cols] for n in range(3))
    wo_far = fetch(w_output)
    wi_far = fetch(w_inner)
    wout_far = fetch(w_outer)

    lens = lax.dynamic_slice_in_dim(lengths, side * passages, passages, 0)
    gain_one = gain_attn.astype(F32).reshape(1, width)
    gain_two = gain_ffn.astype(F32).reshape(1, width)

    block = width // dp
    index = lax.broadcasted_iota(jnp.int32, (width, width), 0)
    source = lax.broadcasted_iota(jnp.int32, (width, width), 1)
    rel = index // block
    rel_dp = (rel % rest) * 4 + ((rel // rest) % 2) * 2 + rel // (2 * rest)
    perm = (source == (rel_dp ^ me) * block + index % block).astype(BF16)

    smem = pl.BlockSpec(memory_space=pltpu.SMEM)
    by_passage = lambda c: pl.BlockSpec((seq, c), lambda p: (p, 0))
    by_passage_t = pl.BlockSpec((width, seq), lambda p: (0, p))
    lse_spec = pl.BlockSpec((1, 8, seq), lambda p: (p, 0, 0))
    weight_spec = whole_spec((width, cols))
    table_spec = whole_spec((16, BUCKETS))
    gain_spec = whole_spec((1, width))
    perm_spec = whole_spec((width, width))
    wo_spec = whole_spec((cols, width))
    qkv_outs = [((rows_n, cols), BF16, by_passage(cols))] * 4 + [((passages, 8, seq), F32, lse_spec)]
    bias_scratch = pltpu.VMEM((heads, seq, seq), F32)
    attn_cost = 2 * rows_n * (width * 3 * cols + seq * 4 * cols)

    rows_one, rows_one_t, cot_t, q_near, k_near, v_near, ctx_near, lse_near = call(
        attn_first_kernel, (passages,),
        [(lens, smem), (inputs, by_passage(width)), (gain_one, gain_spec), (cotangent, by_passage(width)),
         (perm, perm_spec), (w_query, weight_spec), (w_key, weight_spec), (w_value, weight_spec),
         (table, table_spec)],
        [((rows_n, width), BF16, by_passage(width)), ((width, rows_n), BF16, by_passage_t),
         ((width, rows_n), BF16, by_passage_t)] + qkv_outs,
        [bias_scratch], attn_cost, "attn_first",
    )
    q_far, k_far, v_far, ctx_far, lse_far, residual, rows_two, rows_two_t = call(
        attn_second_kernel, (passages,),
        [(lens, smem), (inputs, by_passage(width)), (gain_two, gain_spec), (rows_one, by_passage(width)),
         (ctx_near, by_passage(cols)), (perm, perm_spec), (wq_far, weight_spec), (wk_far, weight_spec),
         (wv_far, weight_spec), (w_output, wo_spec), (wo_far, wo_spec), (table_far, table_spec)],
        qkv_outs + [((rows_n, width), F32, by_passage(width)), ((rows_n, width), BF16, by_passage(width)),
                    ((width, rows_n), BF16, by_passage_t)],
        [bias_scratch], attn_cost, "attn_second",
    )

    block_hidden = 512 if hidden % 512 == 0 else hidden
    steps = hidden // block_hidden
    chunk = min(256, rows_n)
    full = whole_spec((rows_n, width))
    full_t = whole_spec((width, rows_n))
    wi_spec = pl.BlockSpec((width, block_hidden), lambda i: (0, i))
    wout_spec = pl.BlockSpec((block_hidden, width), lambda i: (i, 0))
    grad_spec = pl.BlockSpec((2, width // 2, block_hidden), lambda i: (0, 0, i))
    grad_out = ((2, width // 2, hidden), BF16, grad_spec)
    acc_out = ((rows_n, width), F32, full)
    hidden_scratch = [pltpu.VMEM((rows_n, block_hidden), BF16)] * 2
    ffn_cost = 12 * rows_n * width * hidden

    ffn_near, back_near, fg_send_near, fg_keep_near = call(
        functools.partial(ffn_first_kernel, chunk=chunk), (steps,),
        [(rows_two, full), (rows_two_t, full_t), (cotangent, full), (cot_t, full_t),
         (w_inner, wi_spec), (w_outer, wout_spec)],
        [acc_out, acc_out, grad_out, grad_out],
        hidden_scratch, ffn_cost, "ffn_first",
    )
    layer_out, grad_residual, grad_attn, grad_attn_t, gain_two_part, fg_send_far, fg_keep_far = call(
        functools.partial(ffn_second_kernel, chunk=chunk), (steps,),
        [(rows_two, full), (rows_two_t, full_t), (cotangent, full), (cot_t, full_t),
         (wi_far, wi_spec), (wout_far, wout_spec), (ffn_near, full), (back_near, full),
         (residual, full), (gain_two, gain_spec), (perm, perm_spec)],
        [((rows_n, width), BF16, full), acc_out, ((rows_n, width), BF16, full),
         ((width, rows_n), BF16, full_t), ((1, width), F32, gain_spec), grad_out, grad_out],
        [pltpu.VMEM((rows_n, width), F32)] * 2 + hidden_scratch, ffn_cost, "ffn_second",
    )

    def attn_back(wo, q, k, v, ctx, lse, tab, name):
        half_spec = whole_spec((width // 2, 4 * cols))
        half_out = ((width // 2, 4 * cols), BF16, half_spec)
        return call(
            functools.partial(attn_back_kernel, seq=seq), (passages,),
            [(lens, smem), (grad_attn, by_passage(width)), (wo, wo_spec), (q, by_passage(cols)),
             (k, by_passage(cols)), (v, by_passage(cols)), (ctx, by_passage(cols)), (lse, lse_spec),
             (tab, table_spec), (rows_one_t, full_t), (grad_attn_t, full_t)],
            [((rows_n, 3 * cols), BF16, whole_spec((rows_n, 3 * cols))), half_out, half_out,
             ((BUCKETS, 128), F32, whole_spec((BUCKETS, 128)))],
            [bias_scratch, pltpu.VMEM((heads, seq, seq), F32), pltpu.VMEM((rows_n, cols), BF16)],
            2 * rows_n * cols * (5 * width + 5 * seq), name,
        )

    d_far, ag_send_far, ag_keep_far, table_part_far = attn_back(
        wo_far, q_far, k_far, v_far, ctx_far, lse_far, table_far, "attn_back_far"
    )
    d_near, ag_send_near, ag_keep_near, table_part_near = attn_back(
        w_output, q_near, k_near, v_near, ctx_near, lse_near, table, "attn_back_near"
    )
    grad_input, gain_one_part = call(
        input_back_kernel, (passages,),
        [(inputs, by_passage(width)), (gain_one, gain_spec), (grad_residual, by_passage(width)),
         (d_near, by_passage(3 * cols)), (d_far, by_passage(3 * cols)),
         (w_query, weight_spec), (w_key, weight_spec), (w_value, weight_spec),
         (wq_far, weight_spec), (wk_far, weight_spec), (wv_far, weight_spec)],
        [((rows_n, width), F32, by_passage(width)), ((1, width), F32, gain_spec)],
        [], 12 * rows_n * width * cols, "input_back",
    )

    def plus(left, right):
        return (left.astype(F32) + right.astype(F32)).astype(BF16)

    def reduce_weights(send_near, keep_near, send_far, keep_far):
        near = plus(keep_near, across(send_near, 1))
        far = plus(keep_far, across(send_far, 1))
        mine = plus(near, beside(far))
        lead, tail = mine.shape[:-2], mine.shape[-1]
        halves = mine.reshape(lead + (2, mine.shape[-2] // 2, tail))
        mine = plus(halves[..., 0, :, :], across(halves[..., 1, :, :], 2))
        size, scale = rest, 4
        while size > 1:
            ways = min(4, size)
            rel_parts = mine.reshape(lead + (ways, mine.shape[-2] // ways, tail))
            low = scale * (size // ways)
            total = rel_parts[..., 0, :, :].astype(F32)
            for w in range(1, ways):
                total = total + across(rel_parts[..., w, :, :], w * low).astype(F32)
            size //= ways
            mine = total.astype(BF16) if size > 1 else total
        return mine.astype(F32)

    ffn_grads = reduce_weights(fg_send_near, fg_keep_near, fg_send_far, fg_keep_far)
    attn_grads = reduce_weights(ag_send_near, ag_keep_near, ag_send_far, ag_keep_far)
    grad_inner = ffn_grads[0]
    grad_outer = ffn_grads[1].T
    grad_query, grad_key, grad_value = (attn_grads[:, n * cols : (n + 1) * cols] for n in range(3))
    grad_output = attn_grads[:, 3 * cols :].T

    table_sum = table_part_near[:, :heads] + beside(table_part_far[:, :heads])
    small = jnp.concatenate([gain_one_part, gain_two_part], axis=1)
    small = small + beside(small)
    both = jnp.concatenate([small, table_sum.reshape(1, -1)], axis=1)
    distance = 1
    while distance < dp:
        both = both + across(both, distance)
        distance *= 2
    grad_gain_one = both[0, :width]
    grad_gain_two = both[0, width : 2 * width]
    grad_table = both[0, 2 * width :].reshape(BUCKETS, heads)
    return (
        layer_out, grad_input, grad_gain_one, grad_query, grad_key, grad_value, grad_output,
        grad_table, grad_gain_two, grad_inner, grad_outer,
    )


def solution(mesh):
    both = ("dp", "tensor")
    in_specs = (
        P(both, None), P(), P(None, "tensor"), P(None, "tensor"), P(None, "tensor"), P("tensor", None),
        P(None, "tensor"), P(), P(None, "tensor"), P("tensor", None), P("dp"), P(both, None),
    )
    out_specs = (
        P(both, None), P(both, None), P(), P("dp", "tensor"), P("dp", "tensor"), P("dp", "tensor"),
        P("tensor", "dp"), P(None, "tensor"), P(), P("dp", "tensor"), P("tensor", "dp"),
    )
    body = functools.partial(shards, dp=mesh.shape["dp"], tp=mesh.shape["tensor"])
    return jax.shard_map(body, mesh=mesh, in_specs=in_specs, out_specs=out_specs, check_vma=False)
```

```python
import functools

import jax
import jax.numpy as jnp
from jax import lax
from jax.experimental import pallas as pl
from jax.experimental.pallas import tpu as pltpu
from jax.sharding import PartitionSpec as P

HEAD_DIM = 64
BUCKETS = 32
EPS = 1e-6
MASKED = -1e9
GELU_C = 0.7978845608028654
VMEM_BYTES = 60 * 1024 * 1024
F32 = jnp.float32
BF16 = jnp.bfloat16


def dot(left, right):
    return lax.dot_general(left, right, (((1,), (0,)), ((), ())), preferred_element_type=F32)


def dot_t(left, right):
    return lax.dot_general(left, right, (((1,), (1,)), ((), ())), preferred_element_type=F32)


def dot_l(left, right):
    return lax.dot_general(left, right, (((0,), (0,)), ((), ())), preferred_element_type=F32)


def staggered(count, first, second, third):
    for n in range(count + 2):
        if n < count:
            first(n)
        if 0 <= n - 1 < count:
            second(n - 1)
        if 0 <= n - 2 < count:
            third(n - 2)


def bucket_of(offsets):
    distance = jnp.abs(offsets)
    far = jnp.full_like(distance, 8)
    for power in range(1, 8):
        far = far + (distance * distance >= 64 * 2**power).astype(jnp.int32)
    near = jnp.where(distance < 8, distance, far)
    return near + jnp.where(offsets > 0, 16, 0)


def bucket_indicator(seq):
    lane = lax.broadcasted_iota(jnp.int32, (BUCKETS, 2 * seq), 1)
    offsets = jnp.where(lane < seq, -lane, 2 * seq - lane)
    ids = lax.broadcasted_iota(jnp.int32, (BUCKETS, 2 * seq), 0)
    return (bucket_of(offsets) == ids).astype(F32)


def fill_bias(table_ref, bias_ref):
    heads, seq, _ = bias_ref.shape
    base = dot(table_ref[:, :BUCKETS], bucket_indicator(seq).astype(BF16))
    for h in range(heads):
        wide = jnp.broadcast_to(base[h : h + 1, :], (seq, 2 * seq))
        bias_ref[h] = pltpu.roll(wide, 0, 1, stride=1, stride_axis=0)[:, :seq]


def head_mask(columns, parity):
    lane = lax.broadcasted_iota(jnp.int32, columns.shape, 1)
    keep = (lane < HEAD_DIM) if parity == 0 else (lane >= HEAD_DIM)
    return jnp.where(keep, columns, jnp.zeros_like(columns))


def rms_rows(values, gain):
    return values * lax.rsqrt(jnp.mean(values * values, axis=-1, keepdims=True) + EPS) * gain


def rms_back(values, gain, grads):
    scale = lax.rsqrt(jnp.mean(values * values, axis=-1, keepdims=True) + EPS)
    scaled = grads * gain
    mean = jnp.mean(scaled * values, axis=-1, keepdims=True)
    back = scale * scaled - values * (scale * scale * scale * mean)
    return back, jnp.sum(grads * values * scale, axis=0, keepdims=True)


def fill_perm(perm_ref, me, dp):
    width = perm_ref.shape[0]
    block, bits = width // dp, dp.bit_length() - 1
    index = lax.broadcasted_iota(jnp.int32, (width, 128), 0)
    rel = lax.div(index, block)
    target = jnp.zeros_like(rel)
    for bit in range(bits):
        target = target + (((rel >> (bits - 1 - bit)) & 1) << bit)
    source = (target ^ me) * block + (index - rel * block)
    lane = lax.broadcasted_iota(jnp.int32, (width, 128), 1)
    for n in range(0, width, 128):
        perm_ref[:, n : n + 128] = jnp.where(source == lane + n, 1.0, 0.0).astype(BF16)


def gather_pieces(packets, quarter, sem, routes):
    copies = []
    for pieces, ways in zip(packets, routes, strict=True):
        for n, piece in enumerate(pieces):
            for rows, cols, target, count, at in ways:
                start = pl.multiple_of((quarter ^ n) * count, 16)
                copies.append(
                    pltpu.make_async_copy(piece.at[rows, cols], target.at[pl.ds(start, count), at], sem)
                )
    for copy in copies:
        copy.start()
    for copy in copies:
        copy.wait()


def attend(length, rows, wq_ref, wk_ref, wv_ref, bias_ref, q_ref, k_ref, v_ref, ctx_ref, lse_ref):
    seq = rows.shape[0]
    heads = bias_ref.shape[0]
    query = dot(rows, wq_ref[...]).astype(BF16)
    keys = dot(rows, wk_ref[...]).astype(BF16)
    vals = dot(rows, wv_ref[...]).astype(BF16)
    q_ref[...] = query
    k_ref[...] = keys
    v_ref[...] = vals
    query_t = query.T
    valid = lax.broadcasted_iota(jnp.int32, (seq, 1), 0) < length
    first_head = lax.broadcasted_iota(jnp.int32, (seq, 2 * HEAD_DIM), 1) < HEAD_DIM
    logits, probs, parts = {}, {}, {}

    def pair_of(h):
        lo = (h // 2) * 2 * HEAD_DIM
        return slice(lo, lo + 2 * HEAD_DIM)

    def score(h):
        logits[h] = dot(head_mask(keys[:, pair_of(h)], h % 2), query_t[pair_of(h), :])

    def normalise(h):
        biased = jnp.where(valid, logits.pop(h) + bias_ref[h], MASKED)
        peak = jnp.max(biased, axis=0, keepdims=True)
        terms = jnp.exp(biased - peak)
        total = jnp.sum(terms, axis=0, keepdims=True)
        probs[h] = (terms * (1.0 / total)).astype(BF16)
        lse_ref[0, h : h + 1, :] = peak + jnp.log(total)

    def combine(h):
        parts[h] = dot_l(probs.pop(h), vals[:, pair_of(h)])
        if h % 2:
            both = jnp.where(first_head, parts.pop(h - 1), parts.pop(h))
            ctx_ref[:, pair_of(h)] = both.astype(BF16)

    staggered(heads, score, normalise, combine)


def prepare_kernel(
    len_ref, x_ref, gain_ref, cot_ref, rows_ref, rows_t_ref, cot_t_ref, perm_ref, *, dp, info,
):
    @pl.when(pl.program_id(0) == 0)
    def _():
        fill_perm(perm_ref, len_ref[info], dp)

    rows = rms_rows(x_ref[...].astype(F32), gain_ref[...].astype(F32)).astype(BF16)
    rows_ref[...] = rows
    rows_t_ref[...] = dot_t(perm_ref[...], rows).astype(BF16)
    cot_t_ref[...] = dot_t(perm_ref[...], cot_ref[...]).astype(BF16)


def attn_first_kernel(
    len_ref, rows_ref, wq_ref, wk_ref, wv_ref, table_ref,
    q_ref, k_ref, v_ref, ctx_ref, lse_ref, bias_ref, *, info,
):
    p = pl.program_id(0)

    @pl.when(p == 0)
    def _():
        fill_bias(table_ref, bias_ref)

    attend(
        len_ref[len_ref[info + 1] + p], rows_ref[...], wq_ref, wk_ref, wv_ref, bias_ref, q_ref, k_ref,
        v_ref, ctx_ref, lse_ref,
    )


def pair_routes(piece_rows, cols, targets):
    rows = slice(0, piece_rows)
    return [
        (rows, slice(n * cols, (n + 1) * cols), target, piece_rows, slice(0, cols))
        for n, target in enumerate(targets)
    ]


def wo_routes(piece_rows, cols, target):
    half, lanes = piece_rows // 2, slice(cols, 2 * cols)
    return [
        (slice(0, half), lanes, target, half, slice(0, cols)),
        (slice(half, piece_rows), lanes, target, half, slice(cols, 2 * cols)),
    ]


def attn_second_kernel(
    len_ref, x_ref, gain_ref, rows_ref, ctx_first_ref, perm_ref, *refs, info,
):
    qk_pieces, vo_pieces = refs[:4], refs[4:8]
    (
        wo_first_ref, q_ref, k_ref, v_ref, ctx_ref, lse_ref, resid_ref, rows_two_ref,
        rows_two_t_ref, table_ref, bias_ref, wq_ref, wk_ref, wv_ref, wo_ref, sem, table_sem,
    ) = refs[8:]
    p = pl.program_id(0)

    @pl.when(p == 0)
    def _():
        rows, cols = vo_pieces[0].shape[0], wq_ref.shape[1]
        get_table = pltpu.make_async_copy(
            qk_pieces[0].at[rows : rows + 16, :128], table_ref, table_sem
        )
        get_table.start()
        get_table.wait()
        gather_pieces(
            (qk_pieces, vo_pieces), len_ref[info] & 3, sem,
            [
                pair_routes(rows, cols, (wq_ref, wk_ref)),
                pair_routes(rows, cols, (wv_ref,)) + wo_routes(rows, cols, wo_ref),
            ],
        )
        fill_bias(table_ref, bias_ref)

    attend(
        len_ref[len_ref[info + 1] + p], rows_ref[...], wq_ref, wk_ref, wv_ref, bias_ref, q_ref, k_ref,
        v_ref, ctx_ref, lse_ref,
    )
    branch = dot(ctx_first_ref[...], wo_first_ref[...]) + dot(ctx_ref[...], wo_ref[...])
    residual = x_ref[...].astype(F32) + branch
    resid_ref[...] = residual
    rows_two = rms_rows(residual, gain_ref[...].astype(F32)).astype(BF16)
    rows_two_ref[...] = rows_two
    rows_two_t_ref[...] = dot_t(perm_ref[...], rows_two).astype(BF16)


def ffn_block(
    rows_ref, rows_t_ref, cot_ref, cot_t_ref, wi_ref, wo_ref, ffn_ref, back_ref,
    weight_refs, act_ref, grad_ref, chunk,
):
    def first(i):
        at = slice(i * chunk, (i + 1) * chunk)
        v = dot(rows_ref[at, :], wi_ref[...])
        grad_act = dot_t(cot_ref[at, :], wo_ref[...])
        square = v * v
        tanh = jnp.tanh(GELU_C * v * (1.0 + 0.044715 * square))
        half = 0.5 + 0.5 * tanh
        act_ref[at, :] = (v * half).astype(BF16)
        slope = half + (0.5 * GELU_C) * v * (1.0 - tanh * tanh) * (1.0 + 0.134145 * square)
        grad_ref[at, :] = (grad_act * slope).astype(BF16)

    def second(i):
        at = slice(i * chunk, (i + 1) * chunk)
        ffn_ref[at, :] += dot(act_ref[at, :], wo_ref[...])
        back_ref[at, :] += dot_t(grad_ref[at, :], wi_ref[...])

    staggered(rows_ref.shape[0] // chunk, first, second, lambda i: None)
    send_in_ref, send_out_ref, keep_in_ref, keep_out_ref = weight_refs
    half_rows = keep_in_ref.shape[0]
    send_in_ref[...] = dot(rows_t_ref[half_rows:, :], grad_ref[...]).astype(BF16)
    send_out_ref[...] = dot(cot_t_ref[half_rows:, :], act_ref[...]).astype(BF16)
    keep_in_ref[...] = dot(rows_t_ref[:half_rows, :], grad_ref[...]).astype(BF16)
    keep_out_ref[...] = dot(cot_t_ref[:half_rows, :], act_ref[...]).astype(BF16)


def ffn_first_kernel(
    rows_ref, rows_t_ref, cot_ref, cot_t_ref, wi_ref, wo_ref,
    ffn_ref, back_ref, send_in_ref, send_out_ref, keep_in_ref, keep_out_ref, act_ref, grad_ref, *, chunk,
):
    @pl.when(pl.program_id(0) == 0)
    def _():
        ffn_ref[...] = jnp.zeros_like(ffn_ref)
        back_ref[...] = jnp.zeros_like(back_ref)

    ffn_block(
        rows_ref, rows_t_ref, cot_ref, cot_t_ref, wi_ref, wo_ref, ffn_ref, back_ref,
        (send_in_ref, send_out_ref, keep_in_ref, keep_out_ref), act_ref, grad_ref, chunk,
    )


def ffn_second_kernel(
    info_ref, rows_ref, rows_t_ref, cot_ref, cot_t_ref, *refs, chunk, info,
):
    inner_pieces, outer_pieces = refs[:4], refs[4:8]
    (
        ffn_in_ref, back_in_ref, resid_ref, gain_ref, perm_ref, layer_ref, grad_resid_ref, grad_attn_ref,
        grad_attn_t_ref, gain_grad_ref, send_in_ref, send_out_ref, keep_in_ref, keep_out_ref,
        ffn_ref, back_ref, act_ref, grad_ref, wi_all_ref, wo_all_ref, sem,
    ) = refs[8:]
    step = pl.program_id(0)
    block = act_ref.shape[1]

    @pl.when(step == 0)
    def _():
        width, hidden = wi_all_ref.shape
        wi_rows, wo_rows = width // 4, hidden // 4
        gather_pieces(
            (inner_pieces, outer_pieces), info_ref[info] & 3, sem,
            [
                [(slice(0, wi_rows), slice(0, hidden), wi_all_ref, wi_rows, slice(0, hidden))],
                [(slice(0, wo_rows), slice(0, width), wo_all_ref, wo_rows, slice(0, width))],
            ],
        )
        ffn_ref[...] = ffn_in_ref[...]
        back_ref[...] = back_in_ref[...]

    at_hidden = pl.ds(pl.multiple_of(step * block, block), block)
    wi_ref = wi_all_ref.at[:, at_hidden]
    wo_ref = wo_all_ref.at[at_hidden, :]

    ffn_block(
        rows_ref, rows_t_ref, cot_ref, cot_t_ref, wi_ref, wo_ref, ffn_ref, back_ref,
        (send_in_ref, send_out_ref, keep_in_ref, keep_out_ref), act_ref, grad_ref, chunk,
    )

    @pl.when(pl.program_id(0) == pl.num_programs(0) - 1)
    def _():
        gain_grad_ref[...] = jnp.zeros_like(gain_grad_ref)

        for i in range(rows_ref.shape[0] // chunk):
            at = slice(i * chunk, (i + 1) * chunk)
            residual = resid_ref[at, :]
            layer_ref[at, :] = (residual + ffn_ref[at, :]).astype(BF16)
            back, gain_part = rms_back(residual, gain_ref[...].astype(F32), back_ref[at, :])
            gain_grad_ref[...] += gain_part
            grad_resid = cot_ref[at, :].astype(F32) + back
            grad_resid_ref[at, :] = grad_resid
            grad_attn_ref[at, :] = grad_resid.astype(BF16)

        grad_attn_t_ref[...] = dot_t(perm_ref[...], grad_attn_ref[...]).astype(BF16)


def attn_back_far_kernel(len_ref, grad_attn_ref, *refs, seq, info):
    vo_pieces = refs[:4]
    (
        q_ref, k_ref, v_ref, lse_ref, table_ref, rows_t_ref, grad_attn_t_ref, ctx_far_ref, ctx_near_ref,
        dqkv_ref, send_ref, keep_ref, table_grad_ref, send_near_ref, keep_near_ref,
        bias_ref, sums_ref, wo_ref, sem,
    ) = refs[4:]

    @pl.when(pl.program_id(0) == 0)
    def _():
        gather_pieces(
            (vo_pieces,), len_ref[info] & 3, sem,
            [wo_routes(vo_pieces[0].shape[0], wo_ref.shape[0], wo_ref)],
        )

    attn_back_kernel(
        len_ref, grad_attn_ref, wo_ref, q_ref, k_ref, v_ref, lse_ref, table_ref, rows_t_ref,
        dqkv_ref, send_ref, keep_ref, table_grad_ref, bias_ref, sums_ref, seq=seq, info=info,
    )

    @pl.when(pl.program_id(0) == pl.num_programs(0) - 1)
    def _():
        half_rows = keep_ref.shape[0]
        taken = dqkv_ref.shape[1]
        for far, near, at in (
            (send_ref, send_near_ref, slice(half_rows, None)), (keep_ref, keep_near_ref, slice(half_rows)),
        ):
            far[:, taken:] = dot(grad_attn_t_ref[at, :], ctx_far_ref[...]).astype(BF16)
            near[...] = dot(grad_attn_t_ref[at, :], ctx_near_ref[...]).astype(BF16)


def attn_back_kernel(
    len_ref, grad_attn_ref, wo_ref, q_ref, k_ref, v_ref, lse_ref, table_ref, rows_t_ref,
    dqkv_ref, send_ref, keep_ref, table_grad_ref, bias_ref, sums_ref, *, seq, info,
):
    p = pl.program_id(0)
    heads = bias_ref.shape[0]
    width = heads * HEAD_DIM

    @pl.when(p == 0)
    def _():
        fill_bias(table_ref, bias_ref)
        sums_ref[...] = jnp.zeros_like(sums_ref)

    here = pl.ds(p * seq, seq)
    grad_ctx = dot_t(grad_attn_ref[...], wo_ref[...]).astype(BF16)
    grad_ctx_t = grad_ctx.T
    query = q_ref[...]
    query_t = query.T
    keys = k_ref[...]
    keys_t = keys.T
    vals = v_ref[...]
    valid = lax.broadcasted_iota(jnp.int32, (seq, 1), 0) < len_ref[len_ref[info + 1] + p]
    first_head = lax.broadcasted_iota(jnp.int32, (seq, 2 * HEAD_DIM), 1) < HEAD_DIM
    scores, weights, dq, dk, dv = {}, {}, {}, {}, {}

    def pair_of(h, offset=0):
        lo = (h // 2) * 2 * HEAD_DIM + offset
        return slice(lo, lo + 2 * HEAD_DIM)

    def score(h):
        both = pair_of(h)
        scores[h] = (
            dot(head_mask(keys[:, both], h % 2), query_t[both, :]),
            dot(head_mask(vals[:, both], h % 2), grad_ctx_t[both, :]),
        )

    def soften(h):
        logits, grad_probs = scores.pop(h)
        probs = jnp.exp(logits + bias_ref[h] - lse_ref[0, h : h + 1, :])
        probs = jnp.where(valid, probs, 0.0)
        mixed = jnp.sum(probs * grad_probs, axis=0, keepdims=True)
        grads = (probs * (grad_probs - mixed)).astype(BF16)
        sums_ref[h] += grads.astype(F32)
        weights[h] = (probs.astype(BF16), grads)

    def combine(h):
        probs, grads = weights.pop(h)
        dq[h] = dot(keys_t[h * HEAD_DIM : (h + 1) * HEAD_DIM, :], grads)
        dk[h] = dot(grads, query[:, pair_of(h)])
        dv[h] = dot(probs, grad_ctx[:, pair_of(h)])
        if h % 2:
            dk_both = jnp.where(first_head, dk.pop(h - 1), dk.pop(h)).astype(BF16)
            dv_both = jnp.where(first_head, dv.pop(h - 1), dv.pop(h)).astype(BF16)
            dqkv_ref[here, pair_of(h, width)] = dk_both
            dqkv_ref[here, pair_of(h, 2 * width)] = dv_both

    staggered(heads, score, soften, combine)
    dqkv_ref[here, :width] = jnp.concatenate([dq[h] for h in range(heads)], axis=0).astype(BF16).T

    @pl.when(p == pl.num_programs(0) - 1)
    def _():
        half_rows = keep_ref.shape[0]
        for ref, at in ((send_ref, slice(half_rows, None)), (keep_ref, slice(half_rows))):
            ref[:, : 3 * width] = dot(rows_t_ref[at, :], dqkv_ref[...]).astype(BF16)
        indicator = bucket_indicator(seq)
        lane = lax.broadcasted_iota(jnp.int32, table_grad_ref.shape, 1)
        table_grad = jnp.zeros_like(table_grad_ref)
        for h in range(heads):
            folded = jnp.zeros((8, 2 * seq), F32)
            for a in range(0, seq, 8):
                wide = jnp.concatenate([sums_ref[h, a : a + 8, :], jnp.zeros((8, seq), F32)], axis=1)
                folded = folded + (pltpu.roll(wide, 2 * seq - a, 1) if a else wide)
            diagonals = folded[0:1, :]
            for b in range(1, 8):
                diagonals = diagonals + pltpu.roll(folded[b : b + 1, :], 2 * seq - b, 1)
            column = jnp.sum(indicator * diagonals, axis=1, keepdims=True)
            table_grad = jnp.where(lane == h, column, table_grad)
        table_grad_ref[...] = table_grad


def input_back_kernel(
    info_ref, x_ref, gain_ref, grad_resid_ref, d_first_ref, d_second_ref,
    wq_first_ref, wk_first_ref, wv_first_ref, *refs, info,
):
    qk_pieces, vo_pieces = refs[:4], refs[4:8]
    grad_input_ref, gain_grad_ref, wq_ref, wk_ref, wv_ref, sem = refs[8:]

    @pl.when(pl.program_id(0) == 0)
    def _():
        gain_grad_ref[...] = jnp.zeros_like(gain_grad_ref)
        rows, cols = vo_pieces[0].shape[0], wq_ref.shape[1]
        gather_pieces(
            (qk_pieces, vo_pieces), info_ref[info] & 3, sem,
            [pair_routes(rows, cols, (wq_ref, wk_ref)), pair_routes(rows, cols, (wv_ref,))],
        )

    width = wq_ref.shape[1]
    total = None
    for d_ref, refs in (
        (d_first_ref, (wq_first_ref, wk_first_ref, wv_first_ref)),
        (d_second_ref, (wq_ref, wk_ref, wv_ref)),
    ):
        for n, ref in enumerate(refs):
            term = dot_t(d_ref[:, n * width : (n + 1) * width], ref[...])
            total = term if total is None else total + term
    back, gain_part = rms_back(x_ref[...].astype(F32), gain_ref[...].astype(F32), total)
    grad_input_ref[...] = grad_resid_ref[...] + back
    gain_grad_ref[...] += gain_part


def whole_spec(array_shape):
    return pl.BlockSpec(array_shape, lambda i: (0,) * len(array_shape), pipeline_mode=pl.Buffered(1))


def call(kernel, grid, ins, outs, scratch, cost, name):
    arrays = [a for a, _ in ins]
    return pl.pallas_call(
        kernel,
        grid=grid,
        in_specs=[s for _, s in ins],
        out_specs=[s for _, _, s in outs],
        out_shape=[jax.ShapeDtypeStruct(s, d) for s, d, _ in outs],
        scratch_shapes=scratch,
        compiler_params=pltpu.CompilerParams(
            dimension_semantics=("arbitrary",), vmem_limit_bytes=VMEM_BYTES
        ),
        cost_estimate=pl.CostEstimate(flops=1, bytes_accessed=1, transcendentals=0),
        name=name,
    )(*arrays)


def after(value, *others):
    return lax.optimization_barrier((value,) + others)[0]


def shards(
    inputs, gain_attn, w_query, w_key, w_value, w_output, relative_bias_table,
    gain_ffn, w_inner, w_outer, lengths, cotangent, *, dp, tp,
):
    rows_n, width = inputs.shape
    groups = lengths.shape[0]
    passages = groups // tp
    seq = rows_n // passages
    cols = w_query.shape[1]
    heads = cols // HEAD_DIM
    hidden = w_inner.shape[1]
    me = lax.axis_index("dp")
    side = lax.axis_index("tensor")
    rest = dp // 4

    def across(value, distance):
        return lax.ppermute(value, "dp", [(i, i ^ distance) for i in range(dp)])

    def beside(value):
        return lax.ppermute(value, "tensor", [(i, tp - 1 - i) for i in range(tp)])

    quarter = me & 3

    def part(weight, axis=0):
        count = weight.shape[axis] // 4
        return lax.dynamic_slice_in_dim(weight, quarter * count, count, axis)

    wo_part = part(w_output)
    qk_part = jnp.concatenate([part(w_query), part(w_key)], axis=1)
    vo_part = jnp.concatenate(
        [part(w_value), jnp.concatenate([wo_part[:, :cols], wo_part[:, cols:]], axis=0)], axis=1)
    table = jnp.pad(relative_bias_table.T, ((0, 16 - heads), (0, 128 - BUCKETS)))
    qk_part = jnp.concatenate([qk_part, jnp.pad(table, ((0, 0), (0, 2 * cols - 128)))], axis=0)
    qk_got = beside(qk_part)
    vo_part = after(vo_part, qk_part)
    vo_got = beside(vo_part)
    inner_part = part(after(w_inner, vo_part))
    outer_part = part(after(w_outer, inner_part))
    inner_got = beside(inner_part)
    outer_got = beside(outer_part)
    numbers = jnp.concatenate([lengths, jnp.stack([me, side * passages]).astype(jnp.int32)])
    info = groups
    gain_one = gain_attn.reshape(1, width)
    gain_two = gain_ffn.reshape(1, width)

    smem = pl.BlockSpec(memory_space=pltpu.SMEM)
    anywhere = pl.BlockSpec(memory_space=pl.ANY)
    by_passage = lambda c: pl.BlockSpec((seq, c), lambda p: (p, 0))
    by_passage_t = pl.BlockSpec((width, seq), lambda p: (0, p))
    lse_spec = pl.BlockSpec((1, 8, seq), lambda p: (p, 0, 0))
    weight_spec = whole_spec((width, cols))
    table_spec = whole_spec((16, 128))
    gain_spec = whole_spec((1, width))
    perm_spec = whole_spec((width, width))
    wo_spec = whole_spec((cols, width))
    qkv_outs = [((rows_n, cols), BF16, by_passage(cols))] * 4 + [((passages, 8, seq), F32, lse_spec)]
    bias_scratch = pltpu.VMEM((heads, seq, seq), F32)
    qkv_scratch = [pltpu.VMEM((width, cols), BF16)] * 3
    wo_scratch = pltpu.VMEM((cols, width), BF16)
    dma = pltpu.SemaphoreType.DMA
    attn_cost = 2 * rows_n * (width * 3 * cols + seq * 4 * cols)

    rows_one, rows_one_t, cot_t, perm = call(
        functools.partial(prepare_kernel, dp=dp, info=info), (passages,),
        [(after(numbers, vo_part), smem), (inputs, by_passage(width)), (gain_one, gain_spec),
         (cotangent, by_passage(width))],
        [((rows_n, width), BF16, by_passage(width)), ((width, rows_n), BF16, by_passage_t),
         ((width, rows_n), BF16, by_passage_t), ((width, width), BF16, perm_spec)],
        [], 4 * rows_n * width * width, "prepare",
    )
    qk_got = after(qk_got, rows_one)
    qk_second = across(qk_got, 2)
    qk_core = across(qk_got, 1)
    q_near, k_near, v_near, ctx_near, lse_near = call(
        functools.partial(attn_first_kernel, info=info), (passages,),
        [(after(numbers, qk_got, inner_part, outer_part), smem), (rows_one, by_passage(width)),
         (w_query, weight_spec), (w_key, weight_spec), (w_value, weight_spec), (table, table_spec)],
        qkv_outs, [bias_scratch], attn_cost, "attn_first",
    )
    vo_got = after(vo_got, q_near)
    vo_second = across(vo_got, 2)
    vo_core = across(vo_got, 1)
    qk_pieces = [qk_got, qk_core, qk_second, across(after(qk_second, q_near), 1)]
    vo_pieces = [vo_got, vo_core, vo_second, across(vo_second, 1)]
    attn_pieces = qk_pieces + vo_pieces
    inner_got = after(inner_got, q_near)
    inner_second = across(inner_got, 2)
    inner_core = across(inner_got, 1)
    q_far, k_far, v_far, ctx_far, lse_far, residual, rows_two, rows_two_t, table_far = call(
        functools.partial(attn_second_kernel, info=info), (passages,),
        [(after(numbers, inner_got), smem), (inputs, by_passage(width)), (gain_two, gain_spec),
         (rows_one, by_passage(width)), (ctx_near, by_passage(cols)), (perm, perm_spec)]
        + [(a, anywhere) for a in attn_pieces] + [(w_output, wo_spec)],
        qkv_outs + [((rows_n, width), F32, by_passage(width)), ((rows_n, width), BF16, by_passage(width)),
                    ((width, rows_n), BF16, by_passage_t), ((16, 128), BF16, table_spec)],
        [bias_scratch] + qkv_scratch + [wo_scratch, dma, dma], attn_cost, "attn_second",
    )

    block_hidden = 768 if hidden % 768 == 0 else hidden
    steps = hidden // block_hidden
    chunk = min(256, rows_n)
    full = whole_spec((rows_n, width))
    full_t = whole_spec((width, rows_n))
    wi_spec = pl.BlockSpec((width, block_hidden), lambda i: (0, i))
    wout_spec = pl.BlockSpec((block_hidden, width), lambda i: (i, 0))
    grad_spec = pl.BlockSpec((width // 2, block_hidden), lambda i: (0, i))
    grad_out = ((width // 2, hidden), BF16, grad_spec)
    acc_out = ((rows_n, width), F32, full)
    hidden_scratch = [pltpu.VMEM((rows_n, block_hidden), BF16)] * 2
    ffn_cost = 12 * rows_n * width * hidden

    outer_got = after(outer_got, rows_two)
    outer_second = across(outer_got, 2)
    outer_core = across(outer_got, 1)
    inner_last = across(after(inner_second, rows_two), 1)
    ffn_near, back_near, in_send_near, out_send_near, in_keep_near, out_keep_near = call(
        functools.partial(ffn_first_kernel, chunk=chunk), (steps,),
        [(after(rows_two, outer_got, inner_second), full), (rows_two_t, full_t), (cotangent, full), (cot_t, full_t),
         (w_inner, wi_spec), (w_outer, wout_spec)],
        [acc_out, acc_out] + [grad_out] * 4,
        hidden_scratch, ffn_cost, "ffn_first",
    )
    ffn_pieces = [inner_got, inner_core, inner_second, inner_last]
    ffn_pieces += [outer_got, outer_core, outer_second, across(after(outer_second, ffn_near), 1)]

    def plus(*values):
        return sum(v.astype(F32) for v in values).astype(BF16)

    def halves(values):
        count = values.shape[0] // 2
        return values[:count], values[count:]

    out_got_near = across(after(out_send_near, outer_second), 1)
    in_got_near = across(in_send_near, 1)
    outer_near = halves(plus(out_keep_near, out_got_near))
    outer_near_got = across(outer_near[1], 2)
    (
        layer_out, grad_residual, grad_attn, grad_attn_t, gain_two_part,
        in_send_far, out_send_far, in_keep_far, out_keep_far,
    ) = call(
        functools.partial(ffn_second_kernel, chunk=chunk, info=info), (steps,),
        [(after(numbers, outer_near[1]), smem), (rows_two, full), (rows_two_t, full_t), (cotangent, full),
         (cot_t, full_t)]
        + [(a, anywhere) for a in ffn_pieces] + [(ffn_near, full), (back_near, full),
         (residual, full), (gain_two, gain_spec), (perm, perm_spec)],
        [((rows_n, width), BF16, full), acc_out, ((rows_n, width), BF16, full),
         ((width, rows_n), BF16, full_t), ((1, width), F32, gain_spec)] + [grad_out] * 4,
        [pltpu.VMEM((rows_n, width), F32)] * 2 + hidden_scratch
        + [pltpu.VMEM((width, hidden), BF16), pltpu.VMEM((hidden, width), BF16), dma],
        ffn_cost, "ffn_second",
    )

    def attn_back(kernel, wo, q, k, v, lse, tab, order, ins, outs, columns, more, name):
        half_out = ((width // 2, columns), BF16, whole_spec((width // 2, columns)))
        return call(
            functools.partial(kernel, seq=seq, info=info), (passages,),
            [(after(numbers, *order), smem), (grad_attn, by_passage(width))] + wo + [(q, by_passage(cols)),
             (k, by_passage(cols)), (v, by_passage(cols)), (lse, lse_spec),
             (tab, table_spec), (rows_one_t, full_t)] + ins,
            [((rows_n, 3 * cols), BF16, whole_spec((rows_n, 3 * cols))), half_out, half_out,
             ((BUCKETS, 128), F32, whole_spec((BUCKETS, 128)))] + outs,
            [bias_scratch, pltpu.VMEM((heads, seq, seq), F32)] + more,
            2 * rows_n * cols * (5 * width + 5 * seq), name,
        )

    def finish(values, turn):
        distance = 4
        while distance < dp:
            kept, sent = halves(values)
            total = kept.astype(F32) + after(across(sent, distance), turn).astype(F32)
            distance *= 2
            values = total.astype(BF16) if distance < dp else total
        return values.astype(F32)

    outer_near_kept = plus(outer_near[0], after(outer_near_got, grad_attn))
    inner_near = plus(in_keep_near, after(in_got_near, grad_attn))
    out_got_far = across(after(out_send_far, outer_near_kept, inner_near), 1)
    in_got_far = across(after(in_send_far, outer_near_kept, inner_near), 1)
    outer_far = halves(plus(out_keep_far, out_got_far))
    outer_far_got = across(outer_far[1], 2)
    inner_far = plus(in_keep_far, in_got_far)
    split = hidden // 2
    inner_far_a, inner_far_b = inner_far[:, :split], inner_far[:, split:]
    inner_a_got = beside(inner_far_a)
    context_spec = whole_spec((rows_n, cols))
    wo_near_out = ((width // 2, cols), BF16, whole_spec((width // 2, cols)))
    d_far, ag_send_far, ag_keep_far, table_part_far, wo_send_near, wo_keep_near = attn_back(
        attn_back_far_kernel, [(a, anywhere) for a in vo_pieces], q_far, k_far, v_far,
        lse_far, table_far, (inner_far_a, outer_far[0], outer_far[1]),
        [(grad_attn_t, full_t), (ctx_far, context_spec), (ctx_near, context_spec)], [wo_near_out] * 2,
        4 * cols, [wo_scratch, dma], "attn_back_far",
    )
    inner_b_got = beside(inner_far_b)
    inner_a = halves(plus(inner_near[:, :split], after(inner_a_got, d_far)))
    inner_a_second = across(inner_a[1], 2)
    outer_far_kept = plus(outer_far[0], after(outer_far_got, d_far))
    outer_far_x = beside(outer_far_kept)
    ag_got_far = across(after(ag_send_far, inner_a[1], outer_far_kept), 1)
    wo_got_near = across(after(wo_send_near, inner_a[1], outer_far_kept), 1)
    attn_far = halves(jnp.concatenate(
        [plus(ag_keep_far, ag_got_far), plus(wo_keep_near, wo_got_near)], axis=1))
    attn_far_got = across(attn_far[1], 2)
    d_near, ag_send_near, ag_keep_near, table_part_near = attn_back(
        attn_back_kernel, [(w_output, wo_spec)], q_near, k_near, v_near, lse_near, table,
        (attn_far[1], inner_a[1], outer_far_kept), [], [], 3 * cols, [], "attn_back_near",
    )
    outer_mine = plus(outer_near_kept, after(outer_far_x, d_near))
    inner_b = halves(plus(inner_near[:, split:], after(inner_b_got, d_near)))
    inner_b_second = across(inner_b[1], 2)
    attn_both = plus(attn_far[0], after(attn_far_got, d_near))
    attn_far_x = beside(attn_both[:, : 4 * cols])
    ag_got_near = across(after(ag_send_near, outer_mine, inner_b[1], attn_both), 1)
    attn_near = halves(plus(ag_keep_near, ag_got_near))
    attn_near_got = across(attn_near[1], 2)
    grad_input, gain_one_part = call(
        functools.partial(input_back_kernel, info=info), (passages,),
        [(after(numbers, outer_mine, inner_b[1], attn_near[1], attn_both), smem),
         (inputs, by_passage(width)), (gain_one, gain_spec), (grad_residual, by_passage(width)),
         (d_near, by_passage(3 * cols)), (d_far, by_passage(3 * cols)),
         (w_query, weight_spec), (w_key, weight_spec), (w_value, weight_spec)]
        + [(a, anywhere) for a in attn_pieces],
        [((rows_n, width), F32, by_passage(width)), ((1, width), F32, gain_spec)],
        qkv_scratch + [dma], 12 * rows_n * width * cols, "input_back",
    )
    grad_outer = finish(outer_mine, gain_one_part).T
    inner_mine = jnp.concatenate(
        [plus(inner_a[0], after(inner_a_second, d_near)), plus(inner_b[0], after(inner_b_second, gain_one_part))],
        axis=1)
    grad_inner = finish(inner_mine, gain_one_part)
    attn_mine = jnp.concatenate(
        [plus(attn_near[0], after(attn_near_got, gain_one_part), attn_far_x[:, : 3 * cols]),
         plus(attn_both[:, 4 * cols :], attn_far_x[:, 3 * cols :])], axis=1)
    attn_grads = finish(attn_mine, gain_one_part)
    grad_query, grad_key, grad_value = (attn_grads[:, n * cols : (n + 1) * cols] for n in range(3))
    grad_output = attn_grads[:, 3 * cols :].T

    table_parts = jnp.stack([table_part_near[:, :heads], table_part_far[:, :heads]]).reshape(1, -1)
    small = jnp.concatenate([after(gain_one_part, attn_mine, inner_mine), gain_two_part, table_parts], axis=1)
    size, low = dp, 1
    while size > 1:
        ways = min(4, size)
        small = sum((across(small, w * low) for w in range(1, ways)), small)
        size, low = size // ways, low * ways
    small_got = beside(small)
    table_at = 2 * width
    table_count = BUCKETS * heads
    gains = small[0, :table_at] + small_got[0, :table_at]
    grad_gain_one = gains[:width]
    grad_gain_two = gains[width:]
    grad_table = (
        small[0, table_at : table_at + table_count] + small_got[0, table_at + table_count :]
    ).reshape(BUCKETS, heads)
    return (
        layer_out, grad_input, grad_gain_one, grad_query, grad_key, grad_value, grad_output,
        grad_table, grad_gain_two, grad_inner, grad_outer,
    )


def solution(mesh):
    both = ("dp", "tensor")
    in_specs = (
        P(both, None), P(), P(None, "tensor"), P(None, "tensor"), P(None, "tensor"), P("tensor", None),
        P(None, "tensor"), P(), P(None, "tensor"), P("tensor", None), P("dp"), P(both, None),
    )
    out_specs = (
        P(both, None), P(both, None), P(), P("dp", "tensor"), P("dp", "tensor"), P("dp", "tensor"),
        P("tensor", "dp"), P(None, "tensor"), P(), P("dp", "tensor"), P("tensor", "dp"),
    )
    body = functools.partial(shards, dp=mesh.shape["dp"], tp=mesh.shape["tensor"])
    return jax.shard_map(body, mesh=mesh, in_specs=in_specs, out_specs=out_specs, check_vma=False)
```

```python
import functools

import jax
import jax.numpy as jnp
from jax import lax
from jax.experimental import pallas as pl
from jax.experimental.pallas import tpu as pltpu
from jax.sharding import PartitionSpec as P

HEAD_DIM = 64
BUCKETS = 32
EPS = 1e-6
MASKED = -1e9
GELU_C = 0.7978845608028654
VMEM_BYTES = 60 * 1024 * 1024
F32 = jnp.float32
BF16 = jnp.bfloat16


def dot(left, right):
    return lax.dot_general(left, right, (((1,), (0,)), ((), ())), preferred_element_type=F32)


def dot_t(left, right):
    return lax.dot_general(left, right, (((1,), (1,)), ((), ())), preferred_element_type=F32)


def dot_l(left, right):
    return lax.dot_general(left, right, (((0,), (0,)), ((), ())), preferred_element_type=F32)


def staggered(count, first, second, third):
    for n in range(count + 2):
        if n < count:
            first(n)
        if 0 <= n - 1 < count:
            second(n - 1)
        if 0 <= n - 2 < count:
            third(n - 2)


def bucket_of(offsets):
    distance = jnp.abs(offsets)
    far = jnp.full_like(distance, 8)
    for power in range(1, 8):
        far = far + (distance * distance >= 64 * 2**power).astype(jnp.int32)
    near = jnp.where(distance < 8, distance, far)
    return near + jnp.where(offsets > 0, 16, 0)


def bucket_indicator(seq, count=BUCKETS):
    lane = lax.broadcasted_iota(jnp.int32, (count, 2 * seq), 1)
    offsets = jnp.where(lane < seq, -lane, 2 * seq - lane)
    ids = lax.broadcasted_iota(jnp.int32, (count, 2 * seq), 0)
    return (bucket_of(offsets) == ids).astype(F32)


def fill_bias(table_ref, bias_ref):
    heads, seq, _ = bias_ref.shape
    base = dot(table_ref[:, :BUCKETS], bucket_indicator(seq).astype(BF16))
    for h in range(heads):
        wide = jnp.broadcast_to(base[h : h + 1, :], (seq, 2 * seq))
        bias_ref[h] = pltpu.roll(wide, 0, 1, stride=1, stride_axis=0)[:, :seq]


def head_mask(columns, parity):
    lane = lax.broadcasted_iota(jnp.int32, columns.shape, 1)
    keep = (lane < HEAD_DIM) if parity == 0 else (lane >= HEAD_DIM)
    return jnp.where(keep, columns, jnp.zeros_like(columns))


def rms_rows(values, gain):
    return values * lax.rsqrt(jnp.mean(values * values, axis=-1, keepdims=True) + EPS) * gain


def add_row(ref, row):
    for n in range(row.shape[1] // 128):
        ref[n : n + 1, :] += row[:, n * 128 : (n + 1) * 128]


def rms_back(values, gain, grads):
    scale = lax.rsqrt(jnp.mean(values * values, axis=-1, keepdims=True) + EPS)
    scaled = grads * gain
    mean = jnp.mean(scaled * values, axis=-1, keepdims=True)
    back = scale * scaled - values * (scale * scale * scale * mean)
    return back, jnp.sum(grads * values * scale, axis=0, keepdims=True)


def fill_perm(perm_ref, me, dp, bits):
    width = perm_ref.shape[0]
    block = width // dp
    index = lax.broadcasted_iota(jnp.int32, (width, 128), 0)
    rel = lax.div(index, block)
    target = jnp.zeros_like(rel)
    for n, bit in enumerate(bits):
        target = target + ((rel >> (len(bits) - 1 - n)) & 1) * bit
    source = (target ^ me) * block + (index - rel * block)
    lane = lax.broadcasted_iota(jnp.int32, (width, 128), 1)
    for n in range(0, width, 128):
        perm_ref[:, n : n + 128] = jnp.where(source == lane + n, 1.0, 0.0).astype(BF16)


def piece_copies(packets, quarter, sem, routes):
    copies = []
    for pieces, ways in zip(packets, routes, strict=True):
        for n, piece in enumerate(pieces):
            for rows, cols, target, count, at in ways:
                start = pl.multiple_of((quarter ^ n) * count, 16)
                copies.append((piece.at[rows, cols], target.at[pl.ds(start, count), at], sem))
    return copies


def start_all(copies):
    for copy in copies:
        pltpu.make_async_copy(*copy).start()


def wait_all(copies):
    for copy in copies:
        pltpu.make_async_copy(*copy).wait()


def gather_pieces(packets, quarter, sem, routes):
    copies = piece_copies(packets, quarter, sem, routes)
    start_all(copies)
    wait_all(copies)


def attend(length, rows, wq_ref, wk_ref, wv_ref, bias_ref, q_ref, k_ref, v_ref, ctx_ref, lse_ref):
    seq = rows.shape[0]
    heads = bias_ref.shape[0]
    query = dot(rows, wq_ref[...]).astype(BF16)
    keys = dot(rows, wk_ref[...]).astype(BF16)
    vals = dot(rows, wv_ref[...]).astype(BF16)
    q_ref[...] = query
    k_ref[...] = keys
    v_ref[...] = vals
    query_t = query.T
    valid = lax.broadcasted_iota(jnp.int32, (seq, 1), 0) < length
    first_head = lax.broadcasted_iota(jnp.int32, (seq, 2 * HEAD_DIM), 1) < HEAD_DIM
    logits, probs, parts = {}, {}, {}

    def pair_of(h):
        lo = (h // 2) * 2 * HEAD_DIM
        return slice(lo, lo + 2 * HEAD_DIM)

    def score(h):
        logits[h] = dot(head_mask(keys[:, pair_of(h)], h % 2), query_t[pair_of(h), :])

    def normalise(h):
        biased = jnp.where(valid, logits.pop(h) + bias_ref[h], MASKED)
        peak = jnp.max(biased, axis=0, keepdims=True)
        terms = jnp.exp(biased - peak)
        total = jnp.sum(terms, axis=0, keepdims=True)
        probs[h] = (terms * (1.0 / total)).astype(BF16)
        lse_ref[0, h : h + 1, :] = peak + jnp.log(total)

    def combine(h):
        parts[h] = dot_l(probs.pop(h), vals[:, pair_of(h)])
        if h % 2:
            both = jnp.where(first_head, parts.pop(h - 1), parts.pop(h))
            ctx_ref[:, pair_of(h)] = both.astype(BF16)

    staggered(heads, score, normalise, combine)


def prepare_kernel(
    len_ref, x_ref, gain_ref, cot_ref, rows_ref, rows_t_ref, cot_t_ref, perm_ref, perm_in_ref,
    *, dp, info, orders,
):
    @pl.when(pl.program_id(0) == 0)
    def _():
        fill_perm(perm_ref, len_ref[info], dp, orders[0])
        fill_perm(perm_in_ref, len_ref[info], dp, orders[1])

    rows = rms_rows(x_ref[...].astype(F32), gain_ref[...].astype(F32)).astype(BF16)
    rows_ref[...] = rows
    rows_t_ref[...] = dot_t(perm_ref[...], rows).astype(BF16)
    cot_t_ref[...] = dot_t(perm_ref[...], cot_ref[...]).astype(BF16)


def attn_first_kernel(
    len_ref, rows_ref, wq_ref, wk_ref, wv_ref, table_ref,
    q_ref, k_ref, v_ref, ctx_ref, lse_ref, bias_ref, *, info,
):
    p = pl.program_id(0)

    @pl.when(p == 0)
    def _():
        fill_bias(table_ref, bias_ref)

    attend(
        len_ref[len_ref[info + 1] + p], rows_ref[...], wq_ref, wk_ref, wv_ref, bias_ref, q_ref, k_ref,
        v_ref, ctx_ref, lse_ref,
    )


def pair_routes(piece_rows, cols, targets):
    rows = slice(0, piece_rows)
    return [
        (rows, slice(n * cols, (n + 1) * cols), target, piece_rows, slice(0, cols))
        for n, target in enumerate(targets)
    ]


def wo_routes(piece_rows, cols, target):
    half, lanes = piece_rows // 2, slice(cols, 2 * cols)
    return [
        (slice(0, half), lanes, target, half, slice(0, cols)),
        (slice(half, piece_rows), lanes, target, half, slice(cols, 2 * cols)),
    ]


def attn_second_kernel(
    len_ref, x_ref, gain_ref, rows_ref, ctx_first_ref, perm_ref, *refs, info,
):
    qk_pieces, vo_pieces = refs[:4], refs[4:8]
    (
        wo_first_ref, q_ref, k_ref, v_ref, ctx_ref, lse_ref, resid_ref, rows_two_ref,
        rows_two_t_ref, table_ref, bias_ref, wq_ref, wk_ref, wv_ref, wo_ref, sem, table_sem,
    ) = refs[8:]
    p = pl.program_id(0)

    @pl.when(p == 0)
    def _():
        rows, cols = vo_pieces[0].shape[0], wq_ref.shape[1]
        get_table = pltpu.make_async_copy(
            qk_pieces[0].at[rows : rows + 16, :128], table_ref, table_sem
        )
        get_table.start()
        get_table.wait()
        gather_pieces(
            (qk_pieces, vo_pieces), len_ref[info] & 3, sem,
            [
                pair_routes(rows, cols, (wq_ref, wk_ref)),
                pair_routes(rows, cols, (wv_ref,)) + wo_routes(rows, cols, wo_ref),
            ],
        )
        fill_bias(table_ref, bias_ref)

    attend(
        len_ref[len_ref[info + 1] + p], rows_ref[...], wq_ref, wk_ref, wv_ref, bias_ref, q_ref, k_ref,
        v_ref, ctx_ref, lse_ref,
    )
    branch = dot(ctx_first_ref[...], wo_first_ref[...]) + dot(ctx_ref[...], wo_ref[...])
    residual = x_ref[...].astype(F32) + branch
    resid_ref[...] = residual
    rows_two = rms_rows(residual, gain_ref[...].astype(F32)).astype(BF16)
    rows_two_ref[...] = rows_two
    rows_two_t_ref[...] = dot_t(perm_ref[...], rows_two).astype(BF16)


def ffn_hidden(rows_ref, cot_ref, wi_ref, wo_ref, ffn_ref, back_ref, act_ref, grad_ref, chunk):
    def first(i):
        at = slice(i * chunk, (i + 1) * chunk)
        v = dot(rows_ref[at, :], wi_ref[...])
        grad_act = dot_t(cot_ref[at, :], wo_ref[...])
        square = v * v
        tanh = jnp.tanh(GELU_C * v * (1.0 + 0.044715 * square))
        half = 0.5 + 0.5 * tanh
        act_ref[at, :] = (v * half).astype(BF16)
        slope = half + (0.5 * GELU_C) * v * (1.0 - tanh * tanh) * (1.0 + 0.134145 * square)
        grad_ref[at, :] = (grad_act * slope).astype(BF16)

    def second(i):
        at = slice(i * chunk, (i + 1) * chunk)
        ffn_ref[at, :] += dot(act_ref[at, :], wo_ref[...])
        back_ref[at, :] += dot_t(grad_ref[at, :], wi_ref[...])

    staggered(rows_ref.shape[0] // chunk, first, second, lambda i: None)


def ffn_weights(rows_t_ref, cot_t_ref, weight_refs, act_ref, grad_ref, which):
    half_rows = weight_refs[0].shape[0]
    at = slice(half_rows, None) if which < 2 else slice(half_rows)
    left, right = ((rows_t_ref, grad_ref), (cot_t_ref, act_ref))[which % 2]
    weight_refs[which][...] = dot(left[at, :], right[...]).astype(BF16)


def ffn_first_kernel(
    rows_ref, cot_ref, wi_ref, wo_ref, rows_t_hbm, cot_t_hbm,
    ffn_hbm, back_hbm, send_in_ref, send_out_ref, keep_in_ref, keep_out_ref,
    rows_t_ref, cot_t_ref, ffn_ref, back_ref, act_ref, grad_ref, sems, *, chunk,
):
    step, last = pl.program_id(0), pl.num_programs(0) - 1
    turned = [(rows_t_hbm, rows_t_ref, sems.at[0]), (cot_t_hbm, cot_t_ref, sems.at[1])]
    out = [(ffn_ref, ffn_hbm, sems.at[2]), (back_ref, back_hbm, sems.at[3])]

    @pl.when(step == 0)
    def _():
        start_all(turned)
        ffn_ref[...] = jnp.zeros_like(ffn_ref)
        back_ref[...] = jnp.zeros_like(back_ref)

    ffn_hidden(rows_ref, cot_ref, wi_ref, wo_ref, ffn_ref, back_ref, act_ref, grad_ref, chunk)

    @pl.when(step == 0)
    def _():
        wait_all(turned)

    @pl.when(step == last)
    def _():
        start_all(out)

    weight_refs = (send_in_ref, send_out_ref, keep_in_ref, keep_out_ref)
    for which in range(4):
        ffn_weights(rows_t_ref, cot_t_ref, weight_refs, act_ref, grad_ref, which)

    @pl.when(step == last)
    def _():
        wait_all(out)


def ffn_second_kernel(
    info_ref, rows_ref, cot_ref, gain_ref, rows_t_hbm, cot_t_hbm, *refs, chunk, info,
):
    inner_pieces, outer_pieces = refs[:4], refs[4:8]
    (
        ffn_in_hbm, back_in_hbm, resid_hbm, perm_hbm,
        layer_hbm, grad_resid_hbm, grad_attn_hbm, grad_attn_t_hbm, gain_grad_ref,
        send_in_ref, send_out_ref, keep_in_ref, keep_out_ref,
        rows_t_ref, cot_t_ref, ffn_in_ref, back_in_ref, resid_ref, perm_ref,
        layer_ref, grad_resid_ref, grad_attn_ref, grad_attn_t_ref,
        ffn_ref, back_ref, act_ref, grad_ref, wi_all_ref, wo_all_ref, piece_sem, sems,
    ) = refs[8:]
    step, last = pl.program_id(0), pl.num_programs(0) - 1
    block = act_ref.shape[1]
    turned = [(rows_t_hbm, rows_t_ref, sems.at[0]), (cot_t_hbm, cot_t_ref, sems.at[1])]
    late = [
        (back_in_hbm, back_in_ref, sems.at[2]), (resid_hbm, resid_ref, sems.at[3]),
        (ffn_in_hbm, ffn_in_ref, sems.at[4]), (perm_hbm, perm_ref, sems.at[5]),
    ]

    @pl.when(step == 0)
    def _():
        width, hidden = wi_all_ref.shape
        wi_rows, wo_rows = width // 4, hidden // 4
        pieces = piece_copies(
            (inner_pieces, outer_pieces), info_ref[info] & 3, piece_sem,
            [
                [(slice(0, wi_rows), slice(0, hidden), wi_all_ref, wi_rows, slice(0, hidden))],
                [(slice(0, wo_rows), slice(0, width), wo_all_ref, wo_rows, slice(0, width))],
            ],
        )
        start_all(pieces)
        start_all(turned)
        start_all(late)
        ffn_ref[...] = jnp.zeros_like(ffn_ref)
        back_ref[...] = jnp.zeros_like(back_ref)
        wait_all(pieces)

    at_hidden = pl.ds(pl.multiple_of(step * block, block), block)
    ffn_hidden(
        rows_ref, cot_ref, wi_all_ref.at[:, at_hidden], wo_all_ref.at[at_hidden, :], ffn_ref, back_ref,
        act_ref, grad_ref, chunk,
    )
    weight_refs = (send_in_ref, send_out_ref, keep_in_ref, keep_out_ref)

    @pl.when(step == 0)
    def _():
        wait_all(turned)

    @pl.when(step < last)
    def _():
        for which in range(4):
            ffn_weights(rows_t_ref, cot_t_ref, weight_refs, act_ref, grad_ref, which)

    @pl.when(step == last)
    def _():
        wait_all(late)
        gain_grad_ref[...] = jnp.zeros_like(gain_grad_ref)
        count = rows_ref.shape[0] // chunk
        out = []
        for i in range(count):
            at = slice(i * chunk, (i + 1) * chunk)
            residual = resid_ref[at, :]
            back, gain_part = rms_back(
                residual, gain_ref[...].astype(F32), back_ref[at, :] + back_in_ref[at, :]
            )
            add_row(gain_grad_ref, gain_part)
            grad_resid = cot_ref[at, :].astype(F32) + back
            grad_resid_ref[at, :] = grad_resid
            grad_attn_ref[at, :] = grad_resid.astype(BF16)
            layer_ref[at, :] = (residual + (ffn_ref[at, :] + ffn_in_ref[at, :])).astype(BF16)
            if i < 4:
                ffn_weights(rows_t_ref, cot_t_ref, weight_refs, act_ref, grad_ref, i)
        for which in range(count, 4):
            ffn_weights(rows_t_ref, cot_t_ref, weight_refs, act_ref, grad_ref, which)
        out = [
            (grad_attn_ref, grad_attn_hbm, sems.at[6]), (grad_resid_ref, grad_resid_hbm, sems.at[7]),
            (layer_ref, layer_hbm, sems.at[8]), (grad_attn_t_ref, grad_attn_t_hbm, sems.at[9]),
        ]
        start_all(out[:3])
        grad_attn_t_ref[...] = dot_t(perm_ref[...], grad_attn_ref[...]).astype(BF16)
        start_all(out[3:])
        wait_all(out)


def gain_from_weights(me, bits, w_refs, grads, perm_ref, gain_ref, out_ref):
    width, cols = w_refs[0].shape
    block = width // (2 ** len(bits))
    if block % 16:
        weights = [dot(perm_ref[...], ref[...]) for ref in w_refs]
    else:
        weights = []
        for ref in w_refs:
            rows = []
            for n in range(width // block):
                target = sum(bit for m, bit in enumerate(bits) if (n >> (len(bits) - 1 - m)) & 1)
                rows.append(ref[pl.ds(pl.multiple_of((me ^ target) * block, 16), block), :])
            weights.append(jnp.concatenate(rows, axis=0).astype(F32))
    folded = None
    for n, weight in enumerate(weights):
        for lo in range(0, cols, 128):
            term = weight[:, lo : lo + 128] * grads[:, n * cols + lo : n * cols + lo + 128]
            folded = term if folded is None else folded + term
    ordered = jnp.sum(folded.T, axis=0, keepdims=True)
    high = ordered.astype(BF16)
    middle = (ordered - high.astype(F32)).astype(BF16)
    low = (ordered - high.astype(F32) - middle.astype(F32)).astype(BF16)
    parts = jnp.concatenate([high, middle, low, jnp.zeros((13, width), BF16)], axis=0)
    natural = jnp.sum(dot(parts, perm_ref[...]), axis=0, keepdims=True) / gain_ref[...].astype(F32)
    out_ref[...] = jnp.zeros_like(out_ref)
    add_row(out_ref, natural)


def attn_back_far_kernel(len_ref, grad_attn_ref, *refs, seq, info, bits):
    qk_pieces, vo_pieces = refs[:4], refs[4:8]
    *refs, wq_ref, wk_ref, wv_ref, wo_ref, sem = refs[8:]

    @pl.when(pl.program_id(0) == 0)
    def _():
        rows, cols = vo_pieces[0].shape[0], wq_ref.shape[1]
        gather_pieces(
            (qk_pieces, vo_pieces), len_ref[info] & 3, sem,
            [
                pair_routes(rows, cols, (wq_ref, wk_ref)),
                pair_routes(rows, cols, (wv_ref,)) + wo_routes(rows, cols, wo_ref),
            ],
        )

    attn_back_kernel(
        len_ref, grad_attn_ref, wq_ref, wk_ref, wv_ref, wo_ref, *refs, seq=seq, info=info, bits=bits
    )


def attn_back_kernel(
    len_ref, grad_attn_ref, wq_ref, wk_ref, wv_ref, wo_ref, q_ref, k_ref, v_ref, lse_ref, table_ref,
    rows_t_ref, grad_attn_t_ref, ctx_ref, perm_ref, gain_ref,
    dqkv_ref, send_ref, keep_ref, table_grad_ref, gain_grad_ref, bias_ref, sums_ref, grads_ref,
    *, seq, info, bits,
):
    p = pl.program_id(0)
    heads = bias_ref.shape[0]
    width = heads * HEAD_DIM

    @pl.when(p == 0)
    def _():
        fill_bias(table_ref, bias_ref)
        sums_ref[...] = jnp.zeros_like(sums_ref)

    here = pl.ds(p * seq, seq)
    grad_ctx = dot_t(grad_attn_ref[...], wo_ref[...]).astype(BF16)
    grad_ctx_t = grad_ctx.T
    query = q_ref[...]
    query_t = query.T
    keys = k_ref[...]
    keys_t = keys.T
    vals = v_ref[...]
    valid = lax.broadcasted_iota(jnp.int32, (seq, 1), 0) < len_ref[len_ref[info + 1] + p]
    first_head = lax.broadcasted_iota(jnp.int32, (seq, 2 * HEAD_DIM), 1) < HEAD_DIM
    scores, weights, dq, dk, dv = {}, {}, {}, {}, {}

    def pair_of(h, offset=0):
        lo = (h // 2) * 2 * HEAD_DIM + offset
        return slice(lo, lo + 2 * HEAD_DIM)

    def score(h):
        both = pair_of(h)
        scores[h] = (
            dot(head_mask(keys[:, both], h % 2), query_t[both, :]),
            dot(head_mask(vals[:, both], h % 2), grad_ctx_t[both, :]),
        )

    def soften(h):
        logits, grad_probs = scores.pop(h)
        probs = jnp.exp(logits + bias_ref[h] - lse_ref[0, h : h + 1, :])
        probs = jnp.where(valid, probs, 0.0)
        mixed = jnp.sum(probs * grad_probs, axis=0, keepdims=True)
        grads = (probs * (grad_probs - mixed)).astype(BF16)
        sums_ref[h] += grads.astype(F32)
        weights[h] = (probs.astype(BF16), grads)

    def combine(h):
        probs, grads = weights.pop(h)
        dq[h] = dot(keys_t[h * HEAD_DIM : (h + 1) * HEAD_DIM, :], grads)
        dk[h] = dot(grads, query[:, pair_of(h)])
        dv[h] = dot(probs, grad_ctx[:, pair_of(h)])
        if h % 2:
            dk_both = jnp.where(first_head, dk.pop(h - 1), dk.pop(h)).astype(BF16)
            dv_both = jnp.where(first_head, dv.pop(h - 1), dv.pop(h)).astype(BF16)
            dqkv_ref[here, pair_of(h, width)] = dk_both
            dqkv_ref[here, pair_of(h, 2 * width)] = dv_both

    staggered(heads, score, soften, combine)
    dqkv_ref[here, :width] = jnp.concatenate([dq[h] for h in range(heads)], axis=0).astype(BF16).T

    @pl.when(p == pl.num_programs(0) - 1)
    def _():
        half_rows = keep_ref.shape[0]
        for ref, at in ((send_ref, slice(half_rows, None)), (keep_ref, slice(half_rows))):
            grads_ref[at, :] = dot(rows_t_ref[at, :], dqkv_ref[...])
            ref[:, : 3 * width] = grads_ref[at, :].astype(BF16)
            ref[:, 3 * width :] = dot(grad_attn_t_ref[at, :], ctx_ref[...]).astype(BF16)
        gain_from_weights(
            len_ref[info], bits, (wq_ref, wk_ref, wv_ref), grads_ref, perm_ref, gain_ref, gain_grad_ref
        )
        rows = []
        for h in range(heads):
            folded = jnp.zeros((8, 2 * seq), F32)
            for a in range(0, seq, 8):
                wide = jnp.concatenate([sums_ref[h, a : a + 8, :], jnp.zeros((8, seq), F32)], axis=1)
                folded = folded + (pltpu.roll(wide, 2 * seq - a, 1) if a else wide)
            diagonals = folded[0:1, :]
            for b in range(1, 8):
                diagonals = diagonals + pltpu.roll(folded[b : b + 1, :], 2 * seq - b, 1)
            rows.append(diagonals)
        rows.append(jnp.zeros((8 - heads, 2 * seq), F32))
        table_grad_ref[...] = lax.dot_general(
            jnp.concatenate(rows, axis=0), bucket_indicator(seq, 128), (((1,), (1,)), ((), ())),
            precision=lax.Precision.HIGHEST, preferred_element_type=F32,
        )


def input_back_kernel(
    info_ref, x_ref, gain_ref, grad_resid_ref, d_first_ref, d_second_ref,
    wq_first_ref, wk_first_ref, wv_first_ref, *refs, info,
):
    qk_pieces, vo_pieces = refs[:4], refs[4:8]
    grad_input_ref, wq_ref, wk_ref, wv_ref, sem = refs[8:]

    @pl.when(pl.program_id(0) == 0)
    def _():
        rows, cols = vo_pieces[0].shape[0], wq_ref.shape[1]
        gather_pieces(
            (qk_pieces, vo_pieces), info_ref[info] & 3, sem,
            [pair_routes(rows, cols, (wq_ref, wk_ref)), pair_routes(rows, cols, (wv_ref,))],
        )

    width = wq_ref.shape[1]
    total = None
    for d_ref, refs in (
        (d_first_ref, (wq_first_ref, wk_first_ref, wv_first_ref)),
        (d_second_ref, (wq_ref, wk_ref, wv_ref)),
    ):
        for n, ref in enumerate(refs):
            term = dot_t(d_ref[:, n * width : (n + 1) * width], ref[...])
            total = term if total is None else total + term
    back, _ = rms_back(x_ref[...].astype(F32), gain_ref[...].astype(F32), total)
    grad_input_ref[...] = grad_resid_ref[...] + back


def whole_spec(array_shape):
    return pl.BlockSpec(array_shape, lambda i: (0,) * len(array_shape), pipeline_mode=pl.Buffered(1))


def call(kernel, grid, ins, outs, scratch, cost, name):
    arrays = [a for a, _ in ins]
    return pl.pallas_call(
        kernel,
        grid=grid,
        in_specs=[s for _, s in ins],
        out_specs=[s for _, _, s in outs],
        out_shape=[jax.ShapeDtypeStruct(s, d) for s, d, _ in outs],
        scratch_shapes=scratch,
        compiler_params=pltpu.CompilerParams(
            dimension_semantics=("arbitrary",), vmem_limit_bytes=VMEM_BYTES
        ),
        cost_estimate=pl.CostEstimate(flops=1, bytes_accessed=1, transcendentals=0),
        name=name,
    )(*arrays)


def after(value, *others):
    return lax.optimization_barrier((value,) + others)[0]


def shards(
    inputs, gain_attn, w_query, w_key, w_value, w_output, relative_bias_table,
    gain_ffn, w_inner, w_outer, lengths, cotangent, *, dp, tp,
):
    rows_n, width = inputs.shape
    groups = lengths.shape[0]
    passages = groups // tp
    seq = rows_n // passages
    cols = w_query.shape[1]
    heads = cols // HEAD_DIM
    hidden = w_inner.shape[1]
    me = lax.axis_index("dp")
    side = lax.axis_index("tensor")
    rest = dp // 4

    def across(value, distance):
        return lax.ppermute(value, "dp", [(i, i ^ distance) for i in range(dp)])

    def beside(value):
        return lax.ppermute(value, "tensor", [(i, tp - 1 - i) for i in range(tp)])

    def across_beside(value, distance):
        pairs = [(i * tp + t, (i ^ distance) * tp + tp - 1 - t) for i in range(dp) for t in range(tp)]
        return lax.ppermute(value, ("dp", "tensor"), pairs)

    quarter = me & 3

    def part(weight, axis=0):
        count = weight.shape[axis] // 4
        return lax.dynamic_slice_in_dim(weight, quarter * count, count, axis)

    wo_part = part(w_output)
    qk_part = jnp.concatenate([part(w_query), part(w_key)], axis=1)
    vo_part = jnp.concatenate(
        [part(w_value), jnp.concatenate([wo_part[:, :cols], wo_part[:, cols:]], axis=0)], axis=1)
    table = jnp.pad(relative_bias_table.T, ((0, 16 - heads), (0, 128 - BUCKETS)))
    qk_part = jnp.concatenate([qk_part, jnp.pad(table, ((0, 0), (0, 2 * cols - 128)))], axis=0)
    qk_got = beside(qk_part)
    vo_part = after(vo_part, qk_part)
    vo_got = beside(vo_part)
    inner_part = part(after(w_inner, vo_part))
    outer_part = part(after(w_outer, inner_part))
    inner_got = beside(inner_part)
    outer_got = beside(outer_part)
    numbers = jnp.concatenate([lengths, jnp.stack([me, side * passages]).astype(jnp.int32)])
    info = groups
    gain_one = gain_attn.reshape(1, width)
    gain_two = gain_ffn.reshape(1, width)

    smem = pl.BlockSpec(memory_space=pltpu.SMEM)
    anywhere = pl.BlockSpec(memory_space=pltpu.HBM)
    by_passage = lambda c: pl.BlockSpec((seq, c), lambda p: (p, 0))
    by_passage_t = pl.BlockSpec((width, seq), lambda p: (0, p))
    lse_spec = pl.BlockSpec((1, 8, seq), lambda p: (p, 0, 0))
    weight_spec = whole_spec((width, cols))
    table_spec = whole_spec((16, 128))
    gain_spec = whole_spec((1, width))
    perm_spec = whole_spec((width, width))
    small_rows = -(-width // 1024) * 8
    small_out = ((small_rows, 128), F32, whole_spec((small_rows, 128)))
    wo_spec = whole_spec((cols, width))
    qkv_outs = [((rows_n, cols), BF16, by_passage(cols))] * 4 + [((passages, 8, seq), F32, lse_spec)]
    bias_scratch = pltpu.VMEM((heads, seq, seq), F32)
    qkv_scratch = [pltpu.VMEM((width, cols), BF16)] * 3
    wo_scratch = pltpu.VMEM((cols, width), BF16)
    dma = pltpu.SemaphoreType.DMA
    attn_cost = 2 * rows_n * (width * 3 * cols + seq * 4 * cols)

    bits = [2**n for n in range(1, dp.bit_length() - 1)]
    upper = bits[1:]
    bits_in = upper[:2] + bits[:1] + upper[2:]
    rows_one, rows_one_t, cot_t, perm, perm_in = call(
        functools.partial(prepare_kernel, dp=dp, info=info, orders=([1] + bits, [1] + bits_in)), (passages,),
        [(after(numbers, vo_part), smem), (inputs, by_passage(width)), (gain_one, gain_spec),
         (cotangent, by_passage(width))],
        [((rows_n, width), BF16, by_passage(width)), ((width, rows_n), BF16, by_passage_t),
         ((width, rows_n), BF16, by_passage_t)] + [((width, width), BF16, perm_spec)] * 2,
        [], 4 * rows_n * width * width, "prepare",
    )
    qk_got = after(qk_got, rows_one)
    qk_second = across(qk_got, 2)
    qk_core = across(qk_got, 1)
    vo_got = after(vo_got, rows_one)
    vo_second = across(vo_got, 2)
    vo_core = across(vo_got, 1)
    q_near, k_near, v_near, ctx_near, lse_near = call(
        functools.partial(attn_first_kernel, info=info), (passages,),
        [(after(numbers, qk_got, vo_got, inner_part, outer_part), smem), (rows_one, by_passage(width)),
         (w_query, weight_spec), (w_key, weight_spec), (w_value, weight_spec), (table, table_spec)],
        qkv_outs, [bias_scratch], attn_cost, "attn_first",
    )
    qk_pieces = [qk_got, qk_core, qk_second, across(after(qk_second, q_near), 1)]
    vo_pieces = [vo_got, vo_core, vo_second, across(after(vo_second, q_near), 1)]
    attn_pieces = qk_pieces + vo_pieces
    inner_got = after(inner_got, q_near)
    inner_second = across(inner_got, 2)
    inner_core = across(inner_got, 1)
    q_far, k_far, v_far, ctx_far, lse_far, residual, rows_two, rows_two_t, table_far = call(
        functools.partial(attn_second_kernel, info=info), (passages,),
        [(after(numbers, inner_got), smem), (inputs, by_passage(width)), (gain_two, gain_spec),
         (rows_one, by_passage(width)), (ctx_near, by_passage(cols)), (perm_in, perm_spec)]
        + [(a, anywhere) for a in attn_pieces] + [(w_output, wo_spec)],
        qkv_outs + [((rows_n, width), F32, by_passage(width)), ((rows_n, width), BF16, by_passage(width)),
                    ((width, rows_n), BF16, by_passage_t), ((16, 128), BF16, table_spec)],
        [bias_scratch] + qkv_scratch + [wo_scratch, dma, dma], attn_cost, "attn_second",
    )

    block_hidden = 768 if hidden % 768 == 0 else hidden
    steps = hidden // block_hidden
    chunk = min(256, rows_n)
    full = whole_spec((rows_n, width))
    full_t = whole_spec((width, rows_n))
    wi_spec = pl.BlockSpec((width, block_hidden), lambda i: (0, i))
    wout_spec = pl.BlockSpec((block_hidden, width), lambda i: (i, 0))
    grad_spec = pl.BlockSpec((width // 2, block_hidden), lambda i: (0, i))
    grad_out = ((width // 2, hidden), BF16, grad_spec)
    hidden_scratch = [pltpu.VMEM((rows_n, block_hidden), BF16)] * 2
    ffn_cost = 12 * rows_n * width * hidden

    outer_got = after(outer_got, rows_two)
    outer_second = across(outer_got, 2)
    outer_core = across(outer_got, 1)
    inner_last = across(after(inner_second, rows_two), 1)
    acc_hbm = ((rows_n, width), F32, anywhere)
    rows_hbm = ((rows_n, width), BF16, anywhere)
    turned_hbm = ((width, rows_n), BF16, anywhere)
    acc_vmem = pltpu.VMEM((rows_n, width), F32)
    rows_vmem = pltpu.VMEM((rows_n, width), BF16)
    turned_vmem = pltpu.VMEM((width, rows_n), BF16)
    ffn_near, back_near, in_send_near, out_send_near, in_keep_near, out_keep_near = call(
        functools.partial(ffn_first_kernel, chunk=chunk), (steps,),
        [(after(rows_two, outer_got, inner_second), full), (cotangent, full),
         (w_inner, wi_spec), (w_outer, wout_spec), (rows_two_t, anywhere), (cot_t, anywhere)],
        [acc_hbm, acc_hbm] + [grad_out] * 4,
        [turned_vmem] * 2 + [acc_vmem] * 2 + hidden_scratch + [dma((4,))], ffn_cost, "ffn_first",
    )
    ffn_pieces = [inner_got, inner_core, inner_second, inner_last]
    ffn_pieces += [outer_got, outer_core, outer_second, across(after(outer_second, ffn_near), 1)]

    def whole(array):
        return (array, 0, array.shape[0])

    def part_of(term, n, ways):
        array, which, rows = term
        return (array, which * ways + n, rows // ways)

    def cut(terms, ways=2):
        return [part_of(t, 0, ways) for t in terms], [[part_of(t, n, ways) for t in terms] for n in range(1, ways)]

    def total(terms):
        return sum(array[which * rows : (which + 1) * rows].astype(F32) for array, which, rows in terms)

    def add_up(*groups):
        return [total(terms).astype(BF16) for terms in groups]

    def distances(low_bits):
        return low_bits if len(low_bits) < 2 else [low_bits[1], low_bits[0], low_bits[0] + low_bits[1]]

    out_got_near = across(after(out_send_near, outer_second), 1)
    in_got_near = across(after(in_send_near, outer_second), 1)
    outer_near, sent = cut([whole(out_keep_near), whole(out_got_near)])
    inner_near, sent_in = cut([whole(in_keep_near), whole(in_got_near)])
    (outer_near_sent,) = add_up(sent[0])
    (inner_near_sent,) = add_up(sent_in[0])
    outer_near_got = across(outer_near_sent, 2)
    inner_near_got = across(inner_near_sent, bits_in[0])
    (
        layer_out, grad_residual, grad_attn, grad_attn_t, gain_two_part,
        in_send_far, out_send_far, in_keep_far, out_keep_far,
    ) = call(
        functools.partial(ffn_second_kernel, chunk=chunk, info=info), (steps,),
        [(after(numbers, outer_near_sent, inner_near_sent), smem), (rows_two, full), (cotangent, full),
         (gain_two, gain_spec), (rows_two_t, anywhere), (cot_t, anywhere)]
        + [(a, anywhere) for a in ffn_pieces]
        + [(ffn_near, anywhere), (back_near, anywhere), (residual, anywhere), (perm, anywhere)],
        [rows_hbm, acc_hbm, rows_hbm, turned_hbm, small_out] + [grad_out] * 4,
        [turned_vmem] * 2 + [acc_vmem] * 3 + [pltpu.VMEM((width, width), BF16)]
        + [rows_vmem, acc_vmem, rows_vmem, turned_vmem] + [acc_vmem] * 2 + hidden_scratch
        + [pltpu.VMEM((width, hidden), BF16), pltpu.VMEM((hidden, width), BF16), dma, dma((10,))],
        ffn_cost, "ffn_second",
    )

    def attn_back(kernel, weights, q, k, v, lse, ctx, tab, order, more, name):
        half_out = ((width // 2, 4 * cols), BF16, whole_spec((width // 2, 4 * cols)))
        return call(
            functools.partial(kernel, seq=seq, info=info, bits=[1] + bits), (passages,),
            [(after(numbers, *order), smem), (grad_attn, by_passage(width))] + weights
            + [(q, by_passage(cols)), (k, by_passage(cols)), (v, by_passage(cols)), (lse, lse_spec),
               (tab, table_spec), (rows_one_t, full_t), (grad_attn_t, full_t), (ctx, whole_spec((rows_n, cols))),
               (perm, perm_spec), (gain_one, gain_spec)],
            [((rows_n, 3 * cols), BF16, whole_spec((rows_n, 3 * cols))), half_out, half_out,
             ((8, 128), F32, whole_spec((8, 128))), small_out],
            [bias_scratch, pltpu.VMEM((heads, seq, seq), F32), pltpu.VMEM((width, 3 * cols), F32)] + more,
            2 * rows_n * cols * (5 * width + 5 * seq), name,
        )

    def finish(terms, left, *order):
        for bit in left:
            terms, sent = cut(terms)
            terms = terms + [whole(after(across(total(sent[0]).astype(BF16), bit), *order))]
        return total(terms)

    outer_near_got = after(outer_near_got, grad_attn)
    inner_near_got = after(inner_near_got, grad_attn)
    outer_near = outer_near + [whole(outer_near_got)]
    out_got_far = across(after(out_send_far, outer_near_got, inner_near_got), 1)
    in_got_far = across(after(in_send_far, outer_near_got, inner_near_got), 1)
    inner_near, sent_near = cut(inner_near + [whole(inner_near_got)])
    outer_far, sent = cut([whole(out_keep_far), whole(out_got_far)])
    inner_far, sent_in = cut([whole(in_keep_far), whole(in_got_far)])
    outer_far_sent, inner_far_sent, inner_near_sent = add_up(sent[0], sent_in[0], sent_near[0])
    outer_far_got = across(outer_far_sent, 2)
    inner_far_got = across(inner_far_sent, bits_in[0])
    inner_near_got = across(inner_near_sent, bits_in[1])
    d_far, ag_send_far, ag_keep_far, table_part_far, gain_part_far = attn_back(
        attn_back_far_kernel, [(a, anywhere) for a in attn_pieces], q_far, k_far, v_far, lse_far, ctx_far,
        table_far, [outer_far_sent, inner_far_sent, inner_near_sent], qkv_scratch + [wo_scratch, dma],
        "attn_back_far",
    )
    outer_far_got = after(outer_far_got, d_far)
    inner_far_got = after(inner_far_got, d_far)
    inner_near_got = after(inner_near_got, d_far)
    ag_got_far = across(after(ag_send_far, outer_far_got, inner_far_got, inner_near_got), 1)
    outer_far = outer_far + [whole(outer_far_got)]
    inner_near = inner_near + [whole(inner_near_got)]
    inner_far, sent_in = cut(inner_far + [whole(inner_far_got)])
    outer_far_x, inner_far_sent = add_up(outer_far, sent_in[0])
    outer_x_got = beside(outer_far_x)
    inner_far_got = across(inner_far_sent, bits_in[1])
    attn_far, sent = cut([whole(ag_keep_far), whole(ag_got_far)])
    (attn_far_sent,) = add_up(sent[0])
    attn_far_got = across(attn_far_sent, 2)
    order = [outer_far_x, inner_far_sent, attn_far_sent]
    d_near, ag_send_near, ag_keep_near, table_part_near, gain_part_near = attn_back(
        attn_back_kernel,
        [(w_query, weight_spec), (w_key, weight_spec), (w_value, weight_spec), (w_output, wo_spec)], q_near, k_near, v_near, lse_near, ctx_near,
        table, order, [], "attn_back_near",
    )
    attn_far_got = after(attn_far_got, d_near)
    inner_far_got = after(inner_far_got, d_near)
    outer_x_got = after(outer_x_got, d_near)
    small = jnp.concatenate(
        [gain_part_near + gain_part_far, gain_two_part, table_part_near, table_part_far], axis=0)
    small_got = beside(after(small, attn_far_got, inner_far_got, outer_x_got))
    ag_got_near = across(after(ag_send_near, attn_far_got, inner_far_got, outer_x_got), 1)
    table_at = 2 * small_rows
    small = jnp.concatenate(
        [small[:table_at] + small_got[:table_at], small[table_at : table_at + 8] + small_got[table_at + 8 :]],
        axis=0)
    size, low = dp, 1
    while size > 1:
        ways = min(4, size)
        small = sum((across(small, w * low) for w in range(1, ways)), small)
        size, low = size // ways, low * ways
    outer, sent = cut(outer_near + [whole(outer_x_got)], 2 ** len(upper[:2]))
    outer_sent = add_up(*sent)
    outer_got = [across(v, d) for v, d in zip(outer_sent, distances(upper[:2]), strict=True)]
    far_x = jnp.concatenate(
        [total(attn_far + [whole(attn_far_got)]), total(inner_far + [whole(inner_far_got)])], axis=0).astype(BF16)
    far_x_got = beside(far_x)
    attn_near, sent = cut([whole(ag_keep_near), whole(ag_got_near)])
    (attn_near_sent,) = add_up(sent[0])
    attn_near_got = across(attn_near_sent, 2)
    order = [far_x, attn_near_sent, small] + outer_sent
    (grad_input,) = call(
        functools.partial(input_back_kernel, info=info), (passages,),
        [(after(numbers, *order), smem),
         (inputs, by_passage(width)), (gain_one, gain_spec), (grad_residual, by_passage(width)),
         (d_near, by_passage(3 * cols)), (d_far, by_passage(3 * cols)),
         (w_query, weight_spec), (w_key, weight_spec), (w_value, weight_spec)]
        + [(a, anywhere) for a in attn_pieces],
        [((rows_n, width), F32, by_passage(width))],
        qkv_scratch + [dma], 12 * rows_n * width * cols, "input_back",
    )
    far_x_got = after(far_x_got, grad_input)
    rows = attn_near_sent.shape[0]
    attn_near_got = after(attn_near_got, grad_input, far_x_got, *outer_got)
    attn, sent = cut(attn_near + [whole(attn_near_got), whole(far_x_got[:rows])], 2 ** len(upper[:2]))
    attn_sent = add_up(*sent)
    attn_got = [across(v, d) for v, d in zip(attn_sent, distances(upper[:2]), strict=True)]
    inner = inner_near + [whole(after(far_x_got, *attn_sent)[rows:])]
    grad_inner = finish(inner, bits_in[2:])
    outer = outer + [whole(after(got, *attn_sent)) for got in outer_got]
    grad_outer = finish(outer, upper[2:]).T
    attn_grads = finish(attn + [whole(got) for got in attn_got], upper[2:])
    grad_query, grad_key, grad_value = (attn_grads[:, n * cols : (n + 1) * cols] for n in range(3))
    grad_output = attn_grads[:, 3 * cols :].T

    grad_gain_one = small[: width // 128].reshape(width)
    grad_gain_two = small[small_rows : small_rows + width // 128].reshape(width)
    grad_table = small[table_at : table_at + heads, :BUCKETS].T
    return (
        layer_out, grad_input, grad_gain_one, grad_query, grad_key, grad_value, grad_output,
        grad_table, grad_gain_two, grad_inner, grad_outer,
    )


def solution(mesh):
    both = ("dp", "tensor")
    in_specs = (
        P(both, None), P(), P(None, "tensor"), P(None, "tensor"), P(None, "tensor"), P("tensor", None),
        P(None, "tensor"), P(), P(None, "tensor"), P("tensor", None), P("dp"), P(both, None),
    )
    out_specs = (
        P(both, None), P(both, None), P(), P("dp", "tensor"), P("dp", "tensor"), P("dp", "tensor"),
        P("tensor", "dp"), P(None, "tensor"), P(), P("dp", "tensor"), P("tensor", "dp"),
    )
    body = functools.partial(shards, dp=mesh.shape["dp"], tp=mesh.shape["tensor"])
    return jax.shard_map(body, mesh=mesh, in_specs=in_specs, out_specs=out_specs, check_vma=False)
```

```python
import functools

import jax
import jax.numpy as jnp
from jax import lax
from jax.experimental import pallas as pl
from jax.experimental.pallas import tpu as pltpu
from jax.sharding import PartitionSpec as P

HEAD_DIM = 64
BUCKETS = 32
EPS = 1e-6
MASKED = -1e9
GELU_C = 0.7978845608028654
VMEM_BYTES = 60 * 1024 * 1024
F32 = jnp.float32
BF16 = jnp.bfloat16


def dot(left, right):
    return lax.dot_general(left, right, (((1,), (0,)), ((), ())), preferred_element_type=F32)


def dot_t(left, right):
    return lax.dot_general(left, right, (((1,), (1,)), ((), ())), preferred_element_type=F32)


def dot_l(left, right):
    return lax.dot_general(left, right, (((0,), (0,)), ((), ())), preferred_element_type=F32)


def staggered(count, first, second, third):
    for n in range(count + 2):
        if n < count:
            first(n)
        if 0 <= n - 1 < count:
            second(n - 1)
        if 0 <= n - 2 < count:
            third(n - 2)


def bucket_of(offsets):
    distance = jnp.abs(offsets)
    far = jnp.full_like(distance, 8)
    for power in range(1, 8):
        far = far + (distance * distance >= 64 * 2**power).astype(jnp.int32)
    near = jnp.where(distance < 8, distance, far)
    return near + jnp.where(offsets > 0, 16, 0)


def bucket_indicator(seq, count=BUCKETS):
    lane = lax.broadcasted_iota(jnp.int32, (count, 2 * seq), 1)
    offsets = jnp.where(lane < seq, -lane, 2 * seq - lane)
    ids = lax.broadcasted_iota(jnp.int32, (count, 2 * seq), 0)
    return (bucket_of(offsets) == ids).astype(F32)


def fill_bias(table_ref, bias_ref):
    heads, seq, _ = bias_ref.shape
    base = dot(table_ref[:, :BUCKETS], bucket_indicator(seq).astype(BF16))
    for h in range(heads):
        wide = jnp.broadcast_to(base[h : h + 1, :], (seq, 2 * seq))
        bias_ref[h] = pltpu.roll(wide, 0, 1, stride=1, stride_axis=0)[:, :seq]


def head_mask(columns, parity):
    lane = lax.broadcasted_iota(jnp.int32, columns.shape, 1)
    keep = (lane < HEAD_DIM) if parity == 0 else (lane >= HEAD_DIM)
    return jnp.where(keep, columns, jnp.zeros_like(columns))


def rms_rows(values, gain):
    return values * lax.rsqrt(jnp.mean(values * values, axis=-1, keepdims=True) + EPS) * gain


def add_row(ref, row):
    for n in range(row.shape[1] // 128):
        ref[n : n + 1, :] += row[:, n * 128 : (n + 1) * 128]


def rms_back(values, gain, grads):
    scale = lax.rsqrt(jnp.mean(values * values, axis=-1, keepdims=True) + EPS)
    scaled = grads * gain
    mean = jnp.mean(scaled * values, axis=-1, keepdims=True)
    back = scale * scaled - values * (scale * scale * scale * mean)
    return back, jnp.sum(grads * values * scale, axis=0, keepdims=True)


def fill_perm(perm_ref, me, dp, bits):
    width = perm_ref.shape[0]
    block = width // dp
    index = lax.broadcasted_iota(jnp.int32, (width, 128), 0)
    rel = lax.div(index, block)
    target = jnp.zeros_like(rel)
    for n, bit in enumerate(bits):
        target = target + ((rel >> (len(bits) - 1 - n)) & 1) * bit
    source = (target ^ me) * block + (index - rel * block)
    lane = lax.broadcasted_iota(jnp.int32, (width, 128), 1)
    for n in range(0, width, 128):
        perm_ref[:, n : n + 128] = jnp.where(source == lane + n, 1.0, 0.0).astype(BF16)


def piece_copies(packets, quarter, sem, routes):
    copies = []
    for pieces, ways in zip(packets, routes, strict=True):
        for n, piece in enumerate(pieces):
            for rows, cols, target, count, at in ways:
                start = pl.multiple_of((quarter ^ n) * count, 16)
                copies.append((piece.at[rows, cols], target.at[pl.ds(start, count), at], sem))
    return copies


def start_all(copies):
    for copy in copies:
        pltpu.make_async_copy(*copy).start()


def wait_all(copies):
    for copy in copies:
        pltpu.make_async_copy(*copy).wait()


def gather_pieces(packets, quarter, sem, routes):
    copies = piece_copies(packets, quarter, sem, routes)
    start_all(copies)
    wait_all(copies)


class Heads:
    def __init__(self, seq, heads, lengths, bias_ref, q_ref, k_ref, v_ref, ctx_ref, lse_ref):
        self.seq, self.heads, self.lengths = seq, heads, lengths
        self.bias_ref, self.lse_ref = bias_ref, lse_ref
        self.q_ref, self.k_ref, self.v_ref, self.ctx_ref = q_ref, k_ref, v_ref, ctx_ref
        self.first_head = lax.broadcasted_iota(jnp.int32, (seq, 2 * HEAD_DIM), 1) < HEAD_DIM
        self.key_slot = lax.broadcasted_iota(jnp.int32, (seq, 1), 0)
        self.query_t, self.logits, self.probs, self.parts = {}, {}, {}, {}

    def rows_of(self, p):
        return slice(p * self.seq, (p + 1) * self.seq)

    def pair_of(self, h):
        lo = (h // 2) * 2 * HEAD_DIM
        return slice(lo, lo + 2 * HEAD_DIM)

    def project(self, p, rows, wq_ref, wk_ref, wv_ref):
        query = dot(rows, wq_ref[...]).astype(BF16)
        self.q_ref[self.rows_of(p), :] = query
        self.k_ref[self.rows_of(p), :] = dot(rows, wk_ref[...]).astype(BF16)
        self.v_ref[self.rows_of(p), :] = dot(rows, wv_ref[...]).astype(BF16)
        self.query_t[p] = query.T

    def score(self, n):
        p, h = divmod(n, self.heads)
        both = self.pair_of(h)
        keys = head_mask(self.k_ref[self.rows_of(p), both], h % 2)
        self.logits[n] = dot(keys, self.query_t[p][both, :])

    def normalise(self, n):
        p, h = divmod(n, self.heads)
        valid = self.key_slot < self.lengths[p]
        biased = jnp.where(valid, self.logits.pop(n) + self.bias_ref[h], MASKED)
        peak = jnp.max(biased, axis=0, keepdims=True)
        terms = jnp.exp(biased - peak)
        total = jnp.sum(terms, axis=0, keepdims=True)
        self.probs[n] = (terms * (1.0 / total)).astype(BF16)
        self.lse_ref[p, h : h + 1, :] = peak + jnp.log(total)

    def combine(self, n):
        p, h = divmod(n, self.heads)
        self.parts[n] = dot_l(self.probs.pop(n), self.v_ref[self.rows_of(p), self.pair_of(h)])
        if h % 2:
            both = jnp.where(self.first_head, self.parts.pop(n - 1), self.parts.pop(n))
            self.ctx_ref[self.rows_of(p), self.pair_of(h)] = both.astype(BF16)


def attn_first_kernel(
    len_ref, x_ref, gain_ref, wq_ref, wk_ref, wv_ref, table_ref,
    rows_ref, q_ref, k_ref, v_ref, ctx_ref, lse_ref, bias_ref, *, info,
):
    p = pl.program_id(0)
    seq = rows_ref.shape[0]

    @pl.when(p == 0)
    def _():
        fill_bias(table_ref, bias_ref)

    rows = rms_rows(x_ref[...].astype(F32), gain_ref[0:1, :].astype(F32)).astype(BF16)
    rows_ref[...] = rows
    lengths = [len_ref[len_ref[info + 1] + p]]
    work = Heads(seq, bias_ref.shape[0], lengths, bias_ref, q_ref, k_ref, v_ref, ctx_ref, lse_ref)
    work.project(0, rows, wq_ref, wk_ref, wv_ref)
    staggered(work.heads, work.score, work.normalise, work.combine)


def turn_kernel(
    len_ref, rows_ref, cot_ref, rows_t_ref, cot_t_ref, perm_ref, perm_in_ref, *, dp, info, orders,
):
    @pl.when(pl.program_id(0) == 0)
    def _():
        fill_perm(perm_ref, len_ref[info], dp, orders[0])
        fill_perm(perm_in_ref, len_ref[info], dp, orders[1])

    rows_t_ref[...] = dot_t(perm_ref[...], rows_ref[...]).astype(BF16)
    cot_t_ref[...] = dot_t(perm_ref[...], cot_ref[...]).astype(BF16)


def projection_routes(piece_rows, cols, targets):
    rows = slice(0, piece_rows)
    return [
        (rows, slice(n * cols, (n + 1) * cols), target, piece_rows, slice(0, cols))
        for n, target in enumerate(targets)
    ]


def output_routes(piece_rows, cols, target):
    half, lanes = piece_rows // 2, slice(cols, 2 * cols)
    return [
        (slice(0, half), lanes, target, half, slice(0, cols)),
        (slice(half, piece_rows), lanes, target, half, slice(cols, 2 * cols)),
    ]


def attn_second_kernel(len_ref, gain_ref, rows_hbm, x_hbm, ctx_first_hbm, perm_hbm, *refs, seq, info):
    qk_pieces, vo_pieces = refs[:4], refs[4:8]
    (
        wo_first_hbm, q_hbm, k_hbm, v_hbm, ctx_hbm, lse_ref, resid_hbm, rows_two_hbm, rows_two_t_hbm, table_ref,
        bias_ref, wq_ref, wk_ref, wv_ref, wo_ref, wo_first_ref, rows_ref, x_ref, ctx_first_ref, perm_ref,
        q_ref, k_ref, v_ref, ctx_ref, resid_ref, rows_two_ref, rows_two_t_ref, piece_sem, in_sems, out_sems,
    ) = refs[8:]
    rows, cols = wq_ref.shape[0] // 4, wq_ref.shape[1]
    heads = bias_ref.shape[0]
    passages = q_ref.shape[0] // seq
    quarter = len_ref[info] & 3
    get_table = [(qk_pieces[0].at[rows : rows + 16, :128], table_ref, in_sems.at[0])]
    projections = piece_copies(
        (qk_pieces, vo_pieces), quarter, piece_sem.at[0],
        [projection_routes(rows, cols, (wq_ref, wk_ref)), projection_routes(rows, cols, (wv_ref,))],
    )
    get_rows = [(rows_hbm, rows_ref, in_sems.at[1])]
    output = piece_copies((vo_pieces,), quarter, piece_sem.at[1], [output_routes(rows, cols, wo_ref)])
    output += [
        (wo_first_hbm, wo_first_ref, in_sems.at[2]), (ctx_first_hbm, ctx_first_ref, in_sems.at[3]),
        (x_hbm, x_ref, in_sems.at[4]), (perm_hbm, perm_ref, in_sems.at[5]),
    ]
    start_all(get_table + get_rows + projections + output)
    wait_all(get_table)
    fill_bias(table_ref, bias_ref)
    wait_all(get_rows + projections)
    lengths = [len_ref[len_ref[info + 1] + p] for p in range(passages)]
    work = Heads(seq, heads, lengths, bias_ref, q_ref, k_ref, v_ref, ctx_ref, lse_ref)
    out = []

    def put(ref, hbm, at, sem):
        copy = (ref.at[at], hbm.at[at], out_sems.at[sem])
        out.append(copy)
        start_all([copy])

    def project(p):
        here = work.rows_of(p)
        work.project(p, rows_ref[here, :], wq_ref, wk_ref, wv_ref)
        for n, (ref, hbm) in enumerate(((q_ref, q_hbm), (k_ref, k_hbm), (v_ref, v_hbm))):
            put(ref, hbm, (here, slice(None)), 7 * p + n)

    def branch(p):
        here = work.rows_of(p)
        if p == 0:
            wait_all(output)
        total = dot(ctx_first_ref[here, :], wo_first_ref[...]) + dot(ctx_ref[here, :], wo_ref[...])
        residual = x_ref[here, :].astype(F32) + total
        resid_ref[here, :] = residual
        rows_two_ref[here, :] = rms_rows(residual, gain_ref[1:2, :].astype(F32)).astype(BF16)
        pairs = ((ctx_ref, ctx_hbm), (resid_ref, resid_hbm), (rows_two_ref, rows_two_hbm))
        for n, (ref, hbm) in enumerate(pairs):
            put(ref, hbm, (here, slice(None)), 7 * p + 3 + n)

    def turn(p):
        here = work.rows_of(p)
        rows_two_t_ref[:, here] = dot_t(perm_ref[...], rows_two_ref[here, :]).astype(BF16)
        put(rows_two_t_ref, rows_two_t_hbm, (slice(None), here), 7 * p + 6)

    project(0)
    count = passages * heads
    for n in range(count + 2):
        if n < count:
            work.score(n)
            if n % heads == 2 and n // heads + 1 < passages:
                project(n // heads + 1)
        if 0 <= n - 1 < count:
            work.normalise(n - 1)
        if 0 <= n - 2 < count:
            work.combine(n - 2)
        done = (n - 2) // heads
        if n >= heads + 2 and n % heads == 2:
            branch(done - 1)
        if n >= heads + 4 and n % heads == 4:
            turn((n - 4) // heads - 1)
    branch(passages - 1)
    turn(passages - 1)
    wait_all(out)


def ffn_hidden(rows_ref, cot_ref, wi_ref, wo_ref, ffn_ref, back_ref, act_ref, grad_ref, chunk):
    def first(i):
        at = slice(i * chunk, (i + 1) * chunk)
        v = dot(rows_ref[at, :], wi_ref[...])
        grad_act = dot_t(cot_ref[at, :], wo_ref[...])
        square = v * v
        tanh = jnp.tanh(GELU_C * v * (1.0 + 0.044715 * square))
        half = 0.5 + 0.5 * tanh
        act_ref[at, :] = (v * half).astype(BF16)
        slope = half + (0.5 * GELU_C) * v * (1.0 - tanh * tanh) * (1.0 + 0.134145 * square)
        grad_ref[at, :] = (grad_act * slope).astype(BF16)

    def second(i):
        at = slice(i * chunk, (i + 1) * chunk)
        ffn_ref[at, :] += dot(act_ref[at, :], wo_ref[...])
        back_ref[at, :] += dot_t(grad_ref[at, :], wi_ref[...])

    staggered(rows_ref.shape[0] // chunk, first, second, lambda i: None)


def ffn_weights(rows_t_ref, cot_t_ref, weight_refs, act_ref, grad_ref, which):
    half_rows = weight_refs[0].shape[0]
    at = slice(half_rows, None) if which < 2 else slice(half_rows)
    left, right = ((rows_t_ref, grad_ref), (cot_t_ref, act_ref))[which % 2]
    weight_refs[which][...] = dot(left[at, :], right[...]).astype(BF16)


def ffn_first_kernel(
    rows_ref, cot_ref, wi_ref, wo_ref, rows_t_hbm, cot_t_hbm,
    ffn_hbm, back_hbm, send_in_ref, send_out_ref, keep_in_ref, keep_out_ref,
    rows_t_ref, cot_t_ref, ffn_ref, back_ref, act_ref, grad_ref, sems, *, chunk,
):
    step, last = pl.program_id(0), pl.num_programs(0) - 1
    turned = [(rows_t_hbm, rows_t_ref, sems.at[0]), (cot_t_hbm, cot_t_ref, sems.at[1])]
    out = [(ffn_ref, ffn_hbm, sems.at[2]), (back_ref, back_hbm, sems.at[3])]

    @pl.when(step == 0)
    def _():
        start_all(turned)
        ffn_ref[...] = jnp.zeros_like(ffn_ref)
        back_ref[...] = jnp.zeros_like(back_ref)

    ffn_hidden(rows_ref, cot_ref, wi_ref, wo_ref, ffn_ref, back_ref, act_ref, grad_ref, chunk)

    @pl.when(step == 0)
    def _():
        wait_all(turned)

    @pl.when(step == last)
    def _():
        start_all(out)

    weight_refs = (send_in_ref, send_out_ref, keep_in_ref, keep_out_ref)
    for which in range(4):
        ffn_weights(rows_t_ref, cot_t_ref, weight_refs, act_ref, grad_ref, which)

    @pl.when(step == last)
    def _():
        wait_all(out)


def ffn_second_kernel(
    info_ref, rows_ref, cot_ref, gain_ref, rows_t_hbm, cot_t_hbm, *refs, chunk, info,
):
    inner_pieces, outer_pieces = refs[:4], refs[4:8]
    (
        ffn_in_hbm, back_in_hbm, resid_hbm, perm_hbm,
        layer_hbm, grad_resid_hbm, grad_attn_hbm, grad_attn_t_hbm, gain_grad_ref,
        send_in_ref, send_out_ref, keep_in_ref, keep_out_ref,
        rows_t_ref, cot_t_ref, ffn_in_ref, back_in_ref, resid_ref, perm_ref,
        layer_ref, grad_resid_ref, grad_attn_ref, grad_attn_t_ref,
        ffn_ref, back_ref, act_ref, grad_ref, wi_all_ref, wo_all_ref, piece_sem, sems, out_sems,
    ) = refs[8:]
    step, last = pl.program_id(0), pl.num_programs(0) - 1
    block = act_ref.shape[1]
    turned = [(rows_t_hbm, rows_t_ref, sems.at[0]), (cot_t_hbm, cot_t_ref, sems.at[1])]
    late = [
        (back_in_hbm, back_in_ref, sems.at[2]), (resid_hbm, resid_ref, sems.at[3]),
        (ffn_in_hbm, ffn_in_ref, sems.at[4]), (perm_hbm, perm_ref, sems.at[5]),
    ]

    @pl.when(step == 0)
    def _():
        width, hidden = wi_all_ref.shape
        wi_rows, wo_rows = width // 4, hidden // 4
        pieces = piece_copies(
            (inner_pieces, outer_pieces), info_ref[info] & 3, piece_sem,
            [
                [(slice(0, wi_rows), slice(0, hidden), wi_all_ref, wi_rows, slice(0, hidden))],
                [(slice(0, wo_rows), slice(0, width), wo_all_ref, wo_rows, slice(0, width))],
            ],
        )
        start_all(pieces)
        ffn_ref[...] = jnp.zeros_like(ffn_ref)
        back_ref[...] = jnp.zeros_like(back_ref)
        wait_all(pieces)
        start_all(turned)

    @pl.when(step == last)
    def _():
        start_all(late)

    at_hidden = pl.ds(pl.multiple_of(step * block, block), block)
    ffn_hidden(
        rows_ref, cot_ref, wi_all_ref.at[:, at_hidden], wo_all_ref.at[at_hidden, :], ffn_ref, back_ref,
        act_ref, grad_ref, chunk,
    )
    weight_refs = (send_in_ref, send_out_ref, keep_in_ref, keep_out_ref)

    @pl.when(step == 0)
    def _():
        wait_all(turned)

    @pl.when(step < last)
    def _():
        for which in range(4):
            ffn_weights(rows_t_ref, cot_t_ref, weight_refs, act_ref, grad_ref, which)

    @pl.when(step == last)
    def _():
        wait_all(late)
        gain_grad_ref[...] = jnp.zeros_like(gain_grad_ref)
        count = rows_ref.shape[0] // chunk
        out = []

        def put(ref, hbm, at):
            out.append((ref.at[at], hbm.at[at], out_sems.at[len(out)]))
            start_all(out[-1:])

        for i in range(count):
            at = slice(i * chunk, (i + 1) * chunk)
            residual = resid_ref[at, :]
            back, gain_part = rms_back(
                residual, gain_ref[1:2, :].astype(F32), back_ref[at, :] + back_in_ref[at, :]
            )
            add_row(gain_grad_ref, gain_part)
            grad_resid = cot_ref[at, :].astype(F32) + back
            grad_resid_ref[at, :] = grad_resid
            grad_attn_ref[at, :] = grad_resid.astype(BF16)
            layer_ref[at, :] = (residual + (ffn_ref[at, :] + ffn_in_ref[at, :])).astype(BF16)
            if i < 3:
                ffn_weights(rows_t_ref, cot_t_ref, weight_refs, act_ref, grad_ref, i)
            for ref, hbm in (
                (grad_attn_ref, grad_attn_hbm), (grad_resid_ref, grad_resid_hbm), (layer_ref, layer_hbm)
            ):
                put(ref, hbm, (at, slice(None)))
        grad_attn_t_ref[...] = dot_t(perm_ref[...], grad_attn_ref[...]).astype(BF16)
        put(grad_attn_t_ref, grad_attn_t_hbm, (slice(None), slice(None)))
        for which in range(min(count, 3), 4):
            ffn_weights(rows_t_ref, cot_t_ref, weight_refs, act_ref, grad_ref, which)
        wait_all(out)


def gain_from_weights(me, bits, w_refs, grads, perm_ref, gain_ref, out_ref):
    width, cols = w_refs[0].shape
    block = width // (2 ** len(bits))
    if block % 16:
        weights = [dot(perm_ref[...], ref[...]) for ref in w_refs]
    else:
        weights = []
        for ref in w_refs:
            rows = []
            for n in range(width // block):
                target = sum(bit for m, bit in enumerate(bits) if (n >> (len(bits) - 1 - m)) & 1)
                rows.append(ref[pl.ds(pl.multiple_of((me ^ target) * block, 16), block), :])
            weights.append(jnp.concatenate(rows, axis=0).astype(F32))
    folded = None
    for n, weight in enumerate(weights):
        for lo in range(0, cols, 128):
            term = weight[:, lo : lo + 128] * grads[:, n * cols + lo : n * cols + lo + 128]
            folded = term if folded is None else folded + term
    ordered = jnp.sum(folded.T, axis=0, keepdims=True)
    high = ordered.astype(BF16)
    middle = (ordered - high.astype(F32)).astype(BF16)
    low = (ordered - high.astype(F32) - middle.astype(F32)).astype(BF16)
    parts = jnp.concatenate([high, middle, low, jnp.zeros((13, width), BF16)], axis=0)
    natural = jnp.sum(dot(parts, perm_ref[...]), axis=0, keepdims=True) / gain_ref[0:1, :].astype(F32)
    out_ref[...] = jnp.zeros_like(out_ref)
    add_row(out_ref, natural)


def attn_back_kernel(len_ref, *refs, seq, info, bits, far):
    if far:
        qk_pieces, vo_pieces, refs = refs[:4], refs[4:8], refs[8:]
    else:
        weights_hbm, refs = refs[:4], refs[4:]
    (
        grad_attn_hbm, q_hbm, k_hbm, v_hbm, lse_ref, table_ref, rows_t_hbm, grad_attn_t_hbm, ctx_hbm, perm_hbm,
        gain_ref, dqkv_hbm, send_hbm, keep_hbm, table_grad_ref, gain_grad_ref,
        wq_ref, wk_ref, wv_ref, wo_ref, grad_attn_ref, q_ref, k_ref, v_ref, rows_t_ref, grad_attn_t_ref, ctx_ref,
        perm_ref, dqkv_ref, send_ref, keep_ref, bias_ref, sums_ref, grads_ref, piece_sem, in_sems, out_sems,
    ) = refs
    heads = bias_ref.shape[0]
    cols = heads * HEAD_DIM
    passages = q_ref.shape[0] // seq
    half_rows = keep_ref.shape[0]

    def rows_of(p):
        return slice(p * seq, (p + 1) * seq)

    if far:
        rows = wq_ref.shape[0] // 4
        quarter = len_ref[info] & 3
        late_weights = piece_copies(
            (qk_pieces, vo_pieces), quarter, piece_sem.at[0],
            [projection_routes(rows, cols, (wq_ref, wk_ref)), projection_routes(rows, cols, (wv_ref,))],
        )
        output = piece_copies((vo_pieces,), quarter, piece_sem.at[1], [output_routes(rows, cols, wo_ref)])
    else:
        late_weights = [
            (hbm, ref, piece_sem.at[n])
            for n, (hbm, ref) in enumerate(zip(weights_hbm, (wq_ref, wk_ref, wv_ref), strict=False))
        ]
        output = [(weights_hbm[3], wo_ref, piece_sem.at[3])]
    start_all(output)
    by_passage = []
    for p in range(passages):
        pairs = ((grad_attn_hbm, grad_attn_ref), (q_hbm, q_ref), (k_hbm, k_ref), (v_hbm, v_ref))
        by_passage.append(
            [(hbm.at[rows_of(p), :], ref.at[rows_of(p), :], in_sems.at[4 * p + n]) for n, (hbm, ref) in enumerate(pairs)]
        )
    start_all(by_passage[0])
    at = 4 * passages
    turned = [(ctx_hbm, ctx_ref, in_sems.at[at]), (grad_attn_t_hbm, grad_attn_t_ref, in_sems.at[at + 1])]
    last = [(rows_t_hbm, rows_t_ref, in_sems.at[at + 2]), (perm_hbm, perm_ref, in_sems.at[at + 3])]
    fill_bias(table_ref, bias_ref)
    sums_ref[...] = jnp.zeros_like(sums_ref)
    wait_all(output)
    first_head = lax.broadcasted_iota(jnp.int32, (seq, 2 * HEAD_DIM), 1) < HEAD_DIM
    key_slot = lax.broadcasted_iota(jnp.int32, (seq, 1), 0)
    ready, scores, weights, dq, dk, dv = {}, {}, {}, {}, {}, {}

    def pair_of(h, offset=0):
        lo = (h // 2) * 2 * HEAD_DIM + offset
        return slice(lo, lo + 2 * HEAD_DIM)

    def prepare(p):
        wait_all(by_passage[p])
        grad_ctx = dot_t(grad_attn_ref[rows_of(p), :], wo_ref[...]).astype(BF16)
        valid = key_slot < len_ref[len_ref[info + 1] + p]
        ready[p] = (
            grad_ctx, grad_ctx.T, q_ref[rows_of(p), :].T, k_ref[rows_of(p), :].T, valid,
        )

    def score(n):
        p, h = divmod(n, heads)
        _, grad_ctx_t, query_t, _, _ = ready[p]
        both = pair_of(h)
        scores[n] = (
            dot(head_mask(k_ref[rows_of(p), both], h % 2), query_t[both, :]),
            dot(head_mask(v_ref[rows_of(p), both], h % 2), grad_ctx_t[both, :]),
        )

    def soften(n):
        p, h = divmod(n, heads)
        logits, grad_probs = scores.pop(n)
        probs = jnp.exp(logits + bias_ref[h] - lse_ref[p, h : h + 1, :])
        probs = jnp.where(ready[p][4], probs, 0.0)
        mixed = jnp.sum(probs * grad_probs, axis=0, keepdims=True)
        grads = (probs * (grad_probs - mixed)).astype(BF16)
        sums_ref[h] += grads.astype(F32)
        weights[n] = (probs.astype(BF16), grads)

    def combine(n):
        p, h = divmod(n, heads)
        grad_ctx, _, _, keys_t, _ = ready[p]
        probs, grads = weights.pop(n)
        dq[n] = dot(keys_t[h * HEAD_DIM : (h + 1) * HEAD_DIM, :], grads)
        dk[n] = dot(grads, q_ref[rows_of(p), pair_of(h)])
        dv[n] = dot(probs, grad_ctx[:, pair_of(h)])
        if h % 2:
            dqkv_ref[rows_of(p), pair_of(h, cols)] = jnp.where(first_head, dk.pop(n - 1), dk.pop(n)).astype(BF16)
            dqkv_ref[rows_of(p), pair_of(h, 2 * cols)] = jnp.where(first_head, dv.pop(n - 1), dv.pop(n)).astype(BF16)
        if h == heads - 1:
            parts = jnp.concatenate([dq.pop(m) for m in range(n - h, n + 1)], axis=0)
            dqkv_ref[rows_of(p), :cols] = parts.astype(BF16).T
            copy = (dqkv_ref.at[rows_of(p), :], dqkv_hbm.at[rows_of(p), :], out_sems.at[p])
            out.append(copy)
            start_all([copy])

    out = []
    count = passages * heads
    prepare(0)
    for p in range(1, passages):
        start_all(by_passage[p])
    start_all(turned)
    for n in range(count + 2):
        if n == heads:
            start_all(last + late_weights)
        if n < count:
            score(n)
            if n % heads == heads // 2 and n // heads + 1 < passages:
                prepare(n // heads + 1)
        if 0 <= n - 1 < count:
            soften(n - 1)
        if 0 <= n - 2 < count:
            combine(n - 2)
        if n == heads:
            wait_all(turned)
            send_ref[:, 3 * cols :] = dot(grad_attn_t_ref[half_rows:, :], ctx_ref[...]).astype(BF16)
        if n == heads + 2:
            keep_ref[:, 3 * cols :] = dot(grad_attn_t_ref[:half_rows, :], ctx_ref[...]).astype(BF16)
    wait_all(last)
    for ref, hbm, at, sem in (
        (send_ref, send_hbm, slice(half_rows, None), passages), (keep_ref, keep_hbm, slice(half_rows), passages + 1),
    ):
        grads_ref[at, :] = dot(rows_t_ref[at, :], dqkv_ref[...])
        ref[:, : 3 * cols] = grads_ref[at, :].astype(BF16)
        copy = (ref, hbm, out_sems.at[sem])
        out.append(copy)
        start_all([copy])
    wait_all(late_weights)
    gain_from_weights(
        len_ref[info], bits, (wq_ref, wk_ref, wv_ref), grads_ref, perm_ref, gain_ref, gain_grad_ref
    )
    rows = []
    for h in range(heads):
        folded = jnp.zeros((8, 2 * seq), F32)
        for a in range(0, seq, 8):
            wide = jnp.concatenate([sums_ref[h, a : a + 8, :], jnp.zeros((8, seq), F32)], axis=1)
            folded = folded + (pltpu.roll(wide, 2 * seq - a, 1) if a else wide)
        diagonals = folded[0:1, :]
        for b in range(1, 8):
            diagonals = diagonals + pltpu.roll(folded[b : b + 1, :], 2 * seq - b, 1)
        rows.append(diagonals)
    rows.append(jnp.zeros((8 - heads, 2 * seq), F32))
    table_grad_ref[...] = lax.dot_general(
        jnp.concatenate(rows, axis=0), bucket_indicator(seq, 128), (((1,), (1,)), ((), ())),
        precision=lax.Precision.HIGHEST, preferred_element_type=F32,
    )
    wait_all(out)


def input_back_kernel(
    info_ref, x_ref, gain_ref, grad_resid_ref, d_first_ref, d_second_ref,
    wq_first_ref, wk_first_ref, wv_first_ref, *refs, info,
):
    qk_pieces, vo_pieces = refs[:4], refs[4:8]
    grad_input_ref, wq_ref, wk_ref, wv_ref, sem = refs[8:]

    @pl.when(pl.program_id(0) == 0)
    def _():
        rows, cols = wq_ref.shape[0] // 4, wq_ref.shape[1]
        gather_pieces(
            (qk_pieces, vo_pieces), info_ref[info] & 3, sem,
            [projection_routes(rows, cols, (wq_ref, wk_ref)), projection_routes(rows, cols, (wv_ref,))],
        )

    width = wq_ref.shape[1]
    total = None
    for d_ref, refs in (
        (d_first_ref, (wq_first_ref, wk_first_ref, wv_first_ref)),
        (d_second_ref, (wq_ref, wk_ref, wv_ref)),
    ):
        for n, ref in enumerate(refs):
            term = dot_t(d_ref[:, n * width : (n + 1) * width], ref[...])
            total = term if total is None else total + term
    back, _ = rms_back(x_ref[...].astype(F32), gain_ref[0:1, :].astype(F32), total)
    grad_input_ref[...] = grad_resid_ref[...] + back


def whole_spec(array_shape):
    return pl.BlockSpec(array_shape, lambda i: (0,) * len(array_shape), pipeline_mode=pl.Buffered(1))


def call(kernel, grid, ins, outs, scratch, cost, name):
    arrays = [a for a, _ in ins]
    return pl.pallas_call(
        kernel,
        grid=grid,
        in_specs=[s for _, s in ins],
        out_specs=[s for _, _, s in outs],
        out_shape=[jax.ShapeDtypeStruct(s, d) for s, d, _ in outs],
        scratch_shapes=scratch,
        compiler_params=pltpu.CompilerParams(
            dimension_semantics=("arbitrary",), vmem_limit_bytes=VMEM_BYTES
        ),
        cost_estimate=pl.CostEstimate(flops=1, bytes_accessed=1, transcendentals=0),
        name=name,
    )(*arrays)


def after(value, *others):
    return lax.optimization_barrier((value,) + others)[0]


def shards(
    inputs, gain_attn, w_query, w_key, w_value, w_output, relative_bias_table,
    gain_ffn, w_inner, w_outer, lengths, cotangent, *, dp, tp,
):
    rows_n, width = inputs.shape
    groups = lengths.shape[0]
    passages = groups // tp
    seq = rows_n // passages
    cols = w_query.shape[1]
    heads = cols // HEAD_DIM
    hidden = w_inner.shape[1]
    me = lax.axis_index("dp")
    side = lax.axis_index("tensor")
    rest = dp // 4

    def across(value, distance):
        return lax.ppermute(value, "dp", [(i, i ^ distance) for i in range(dp)])

    def beside(value):
        return lax.ppermute(value, "tensor", [(i, tp - 1 - i) for i in range(tp)])

    def across_beside(value, distance):
        pairs = [(i * tp + t, (i ^ distance) * tp + tp - 1 - t) for i in range(dp) for t in range(tp)]
        return lax.ppermute(value, ("dp", "tensor"), pairs)

    quarter = me & 3

    def part(weight, axis=0):
        count = weight.shape[axis] // 4
        return lax.dynamic_slice_in_dim(weight, quarter * count, count, axis)

    wo_part = part(w_output)
    wo_part = jnp.concatenate([wo_part[:, :cols], wo_part[:, cols:]], axis=0)
    table = jnp.pad(relative_bias_table.T, ((0, 16 - heads), (0, 128 - BUCKETS)))
    qk_part = jnp.concatenate(
        [jnp.concatenate([part(w_query), part(w_key)], axis=1), jnp.pad(table, ((0, 0), (0, 2 * cols - 128)))], axis=0)
    vo_part = jnp.concatenate([part(w_value), wo_part], axis=1)
    qk_got, vo_got = beside(qk_part), beside(vo_part)
    numbers = jnp.concatenate([lengths, jnp.stack([me, side * passages]).astype(jnp.int32)])
    info = groups
    gains = jnp.stack([gain_attn, gain_ffn])

    smem = pl.BlockSpec(memory_space=pltpu.SMEM)
    anywhere = pl.BlockSpec(memory_space=pltpu.HBM)
    by_passage = lambda c: pl.BlockSpec((seq, c), lambda p: (p, 0))
    by_passage_t = pl.BlockSpec((width, seq), lambda p: (0, p))
    lse_spec = pl.BlockSpec((1, 8, seq), lambda p: (p, 0, 0))
    weight_spec = whole_spec((width, cols))
    table_spec = whole_spec((16, 128))
    gain_spec = whole_spec((2, width))
    perm_spec = whole_spec((width, width))
    small_rows = -(-width // 1024) * 8
    small_out = ((small_rows, 128), F32, whole_spec((small_rows, 128)))
    wo_spec = whole_spec((cols, width))
    qkv_outs = [((rows_n, cols), BF16, by_passage(cols))] * 4 + [((passages, 8, seq), F32, lse_spec)]
    bias_scratch = pltpu.VMEM((heads, seq, seq), F32)
    qkv_scratch = [pltpu.VMEM((width, cols), BF16)] * 3
    wo_scratch = pltpu.VMEM((cols, width), BF16)
    dma = pltpu.SemaphoreType.DMA
    cols_vmem = pltpu.VMEM((rows_n, cols), BF16)
    acc_hbm = ((rows_n, width), F32, anywhere)
    rows_hbm = ((rows_n, width), BF16, anywhere)
    turned_hbm = ((width, rows_n), BF16, anywhere)
    acc_vmem = pltpu.VMEM((rows_n, width), F32)
    rows_vmem = pltpu.VMEM((rows_n, width), BF16)
    turned_vmem = pltpu.VMEM((width, rows_n), BF16)
    attn_cost = 2 * rows_n * (width * 3 * cols + seq * 4 * cols)

    bits = [2**n for n in range(1, dp.bit_length() - 1)]
    upper = bits[1:]
    bits_in = upper[:2] + bits[:1] + upper[2:]
    rows_one, q_near, k_near, v_near, ctx_near, lse_near = call(
        functools.partial(attn_first_kernel, info=info), (passages,),
        [(after(numbers, qk_part, vo_part), smem), (inputs, by_passage(width)), (gains, gain_spec),
         (w_query, weight_spec), (w_key, weight_spec), (w_value, weight_spec), (table, table_spec)],
        [((rows_n, width), BF16, by_passage(width))] + qkv_outs, [bias_scratch], attn_cost, "attn_first",
    )
    qk_got, vo_got = after(qk_got, rows_one), after(vo_got, rows_one)
    qk_second, vo_second = across(qk_got, 2), across(vo_got, 2)
    qk_core, vo_core = across(qk_got, 1), across(vo_got, 1)
    inner_part = part(after(w_inner, qk_got, vo_got))
    outer_part = part(after(w_outer, inner_part))
    inner_got = beside(inner_part)
    rows_one_t, cot_t, perm, perm_in = call(
        functools.partial(turn_kernel, dp=dp, info=info, orders=([1] + bits, [1] + bits_in)), (passages,),
        [(after(numbers, inner_part, outer_part), smem), (rows_one, by_passage(width)), (cotangent, by_passage(width))],
        [((width, rows_n), BF16, by_passage_t)] * 2 + [((width, width), BF16, perm_spec)] * 2,
        [], 4 * rows_n * width * width, "turn",
    )
    attn_pieces = [qk_got, qk_core, qk_second, across(after(qk_second, perm), 1)]
    attn_pieces += [vo_got, vo_core, vo_second, across(after(vo_second, perm), 1)]
    outer_got = beside(outer_part)
    inner_got = after(inner_got, perm)
    inner_second = across(inner_got, 2)
    inner_core = across(inner_got, 1)
    q_far, k_far, v_far, ctx_far, lse_far, residual, rows_two, rows_two_t, table_far = call(
        functools.partial(attn_second_kernel, seq=seq, info=info), (1,),
        [(after(numbers, inner_got), smem), (gains, gain_spec), (rows_one, anywhere), (inputs, anywhere),
         (ctx_near, anywhere), (perm_in, anywhere)] + [(a, anywhere) for a in attn_pieces]
        + [(w_output, anywhere)],
        [((rows_n, cols), BF16, anywhere)] * 4 + [((passages, 8, seq), F32, whole_spec((passages, 8, seq)))]
        + [acc_hbm, rows_hbm, turned_hbm, ((16, 128), BF16, table_spec)],
        [bias_scratch] + qkv_scratch + [wo_scratch, wo_scratch, rows_vmem, rows_vmem, cols_vmem]
        + [pltpu.VMEM((width, width), BF16)] + [cols_vmem] * 4 + [acc_vmem, rows_vmem, turned_vmem]
        + [dma((2,)), dma((6,)), dma((7 * passages,))], attn_cost, "attn_second",
    )

    block_hidden = 768 if hidden % 768 == 0 else hidden
    steps = hidden // block_hidden
    chunk = min(256, rows_n)
    full = whole_spec((rows_n, width))
    full_t = whole_spec((width, rows_n))
    wi_spec = pl.BlockSpec((width, block_hidden), lambda i: (0, i))
    wout_spec = pl.BlockSpec((block_hidden, width), lambda i: (i, 0))
    grad_spec = pl.BlockSpec((width // 2, block_hidden), lambda i: (0, i))
    grad_out = ((width // 2, hidden), BF16, grad_spec)
    hidden_scratch = [pltpu.VMEM((rows_n, block_hidden), BF16)] * 2
    ffn_cost = 12 * rows_n * width * hidden

    outer_got = after(outer_got, rows_two)
    outer_second = across(outer_got, 2)
    outer_core = across(outer_got, 1)
    inner_last = across(after(inner_second, rows_two), 1)
    ffn_near, back_near, in_send_near, out_send_near, in_keep_near, out_keep_near = call(
        functools.partial(ffn_first_kernel, chunk=chunk), (steps,),
        [(after(rows_two, outer_got, inner_second, inner_core), full), (cotangent, full),
         (w_inner, wi_spec), (w_outer, wout_spec), (rows_two_t, anywhere), (cot_t, anywhere)],
        [acc_hbm, acc_hbm] + [grad_out] * 4,
        [turned_vmem] * 2 + [acc_vmem] * 2 + hidden_scratch + [dma((4,))], ffn_cost, "ffn_first",
    )
    ffn_pieces = [inner_got, inner_core, inner_second, inner_last]
    ffn_pieces += [outer_got, outer_core, outer_second, across(after(outer_second, ffn_near), 1)]

    def whole(array):
        return (array, 0, array.shape[0])

    def part_of(term, n, ways):
        array, which, rows = term
        return (array, which * ways + n, rows // ways)

    def cut(terms, ways=2):
        return [part_of(t, 0, ways) for t in terms], [[part_of(t, n, ways) for t in terms] for n in range(1, ways)]

    def total(terms):
        return sum(array[which * rows : (which + 1) * rows].astype(F32) for array, which, rows in terms)

    def add_up(*groups):
        return [total(terms).astype(BF16) for terms in groups]

    def distances(low_bits):
        return low_bits if len(low_bits) < 2 else [low_bits[1], low_bits[0], low_bits[0] + low_bits[1]]

    out_got_near = across(after(out_send_near, outer_second, inner_last, outer_core), 1)
    in_got_near = across(after(in_send_near, outer_second, inner_last, outer_core), 1)
    outer_near, sent = cut([whole(out_keep_near), whole(out_got_near)])
    inner_near, sent_in = cut([whole(in_keep_near), whole(in_got_near)])
    (outer_near_sent,) = add_up(sent[0])
    (inner_near_sent,) = add_up(sent_in[0])
    outer_near_got = across(outer_near_sent, 2)
    inner_near_got = across(inner_near_sent, bits_in[0])
    (
        layer_out, grad_residual, grad_attn, grad_attn_t, gain_two_part,
        in_send_far, out_send_far, in_keep_far, out_keep_far,
    ) = call(
        functools.partial(ffn_second_kernel, chunk=chunk, info=info), (steps,),
        [(after(numbers, outer_near_sent, inner_near_sent), smem), (rows_two, full), (cotangent, full),
         (gains, gain_spec), (rows_two_t, anywhere), (cot_t, anywhere)]
        + [(a, anywhere) for a in ffn_pieces]
        + [(ffn_near, anywhere), (back_near, anywhere), (residual, anywhere), (perm, anywhere)],
        [rows_hbm, acc_hbm, rows_hbm, turned_hbm, small_out] + [grad_out] * 4,
        [turned_vmem] * 2 + [acc_vmem] * 3 + [pltpu.VMEM((width, width), BF16)]
        + [rows_vmem, acc_vmem, rows_vmem, turned_vmem] + [acc_vmem] * 2 + hidden_scratch
        + [pltpu.VMEM((width, hidden), BF16), pltpu.VMEM((hidden, width), BF16), dma, dma((6,)), dma((3 * (rows_n // chunk) + 1,))],
        ffn_cost, "ffn_second",
    )

    def attn_back(weights, q, k, v, lse, ctx, tab, order, name):
        half_shape = (width // 2, 4 * cols)
        far = weights is attn_pieces
        return call(
            functools.partial(attn_back_kernel, seq=seq, info=info, bits=[1] + bits, far=far), (1,),
            [(after(numbers, *order), smem)] + [(w, anywhere) for w in weights]
            + [(grad_attn, anywhere), (q, anywhere), (k, anywhere), (v, anywhere),
               (lse, whole_spec((passages, 8, seq))), (tab, table_spec), (rows_one_t, anywhere),
               (grad_attn_t, anywhere), (ctx, anywhere), (perm, anywhere), (gains, gain_spec)],
            [((rows_n, 3 * cols), BF16, anywhere), (half_shape, BF16, anywhere), (half_shape, BF16, anywhere),
             ((8, 128), F32, whole_spec((8, 128))), small_out],
            qkv_scratch + [wo_scratch, rows_vmem] + [cols_vmem] * 3 + [turned_vmem] * 2
            + [cols_vmem, pltpu.VMEM((width, width), BF16), pltpu.VMEM((rows_n, 3 * cols), BF16)]
            + [pltpu.VMEM(half_shape, BF16)] * 2 + [bias_scratch, pltpu.VMEM((heads, seq, seq), F32)]
            + [pltpu.VMEM((width, 3 * cols), F32), dma((4,)), dma((4 * passages + 4,)), dma((passages + 2,))],
            2 * rows_n * cols * (5 * width + 5 * seq), name,
        )

    def finish(terms, left, *order):
        for bit in left:
            terms, sent = cut(terms)
            terms = terms + [whole(after(across(total(sent[0]).astype(BF16), bit), *order))]
        return total(terms)

    outer_near_got = after(outer_near_got, grad_attn)
    inner_near_got = after(inner_near_got, grad_attn)
    outer_near = outer_near + [whole(outer_near_got)]
    out_got_far = across(after(out_send_far, outer_near_got, inner_near_got), 1)
    in_got_far = across(after(in_send_far, outer_near_got, inner_near_got), 1)
    inner_near, sent_near = cut(inner_near + [whole(inner_near_got)])
    (inner_near_sent,) = add_up(sent_near[0])
    out_got_far = after(out_got_far, inner_near_sent)
    outer_far, sent = cut([whole(out_keep_far), whole(out_got_far)])
    inner_far, sent_in = cut([whole(in_keep_far), whole(in_got_far)])
    outer_far_sent, inner_far_sent = add_up(sent[0], sent_in[0])
    outer_far_got = across(outer_far_sent, 2)
    inner_far_got = across(inner_far_sent, bits_in[0])
    inner_near_got = across(inner_near_sent, bits_in[1])
    d_far, ag_send_far, ag_keep_far, table_part_far, gain_part_far = attn_back(
        attn_pieces, q_far, k_far, v_far, lse_far, ctx_far, table_far,
        [outer_far_sent, inner_far_sent, inner_near_sent], "attn_back_far",
    )
    outer_far_got = after(outer_far_got, d_far)
    inner_far_got = after(inner_far_got, d_far)
    inner_near_got = after(inner_near_got, d_far)
    ag_got_far = across(after(ag_send_far, outer_far_got, inner_far_got, inner_near_got), 1)
    outer_far = outer_far + [whole(outer_far_got)]
    inner_near = inner_near + [whole(inner_near_got)]
    inner_far, sent_in = cut(inner_far + [whole(inner_far_got)])
    outer_far_x, inner_far_sent = add_up(outer_far, sent_in[0])
    outer_x_got = beside(outer_far_x)
    inner_far_got = across(inner_far_sent, bits_in[1])
    attn_far, sent = cut([whole(ag_keep_far), whole(ag_got_far)])
    (attn_far_sent,) = add_up(sent[0])
    attn_far_got = across(attn_far_sent, 2)
    order = [outer_far_x, inner_far_sent, attn_far_sent]
    d_near, ag_send_near, ag_keep_near, table_part_near, gain_part_near = attn_back(
        [w_query, w_key, w_value, w_output], q_near, k_near, v_near, lse_near, ctx_near, table, order,
        "attn_back_near",
    )
    attn_far_got = after(attn_far_got, d_near)
    inner_far_got = after(inner_far_got, d_near)
    outer_x_got = after(outer_x_got, d_near)
    small = jnp.concatenate(
        [gain_part_near + gain_part_far, gain_two_part, table_part_near, table_part_far], axis=0)
    small_got = beside(after(small, attn_far_got, inner_far_got, outer_x_got))
    ag_got_near = across(after(ag_send_near, attn_far_got, inner_far_got, outer_x_got), 1)
    table_at = 2 * small_rows
    small = jnp.concatenate(
        [small[:table_at] + small_got[:table_at], small[table_at : table_at + 8] + small_got[table_at + 8 :]],
        axis=0)
    size, low = dp, 1
    while size > 1:
        ways = min(4, size)
        small = sum((across(small, w * low) for w in range(1, ways)), small)
        size, low = size // ways, low * ways
    outer, sent = cut(outer_near + [whole(outer_x_got)], 2 ** len(upper[:2]))
    outer_sent = add_up(*sent)
    outer_got = [across(v, d) for v, d in zip(outer_sent, distances(upper[:2]), strict=True)]
    far_x = jnp.concatenate(
        [total(attn_far + [whole(attn_far_got)]), total(inner_far + [whole(inner_far_got)])], axis=0).astype(BF16)
    far_x_got = beside(far_x)
    attn_near, sent = cut([whole(ag_keep_near), whole(ag_got_near)])
    (attn_near_sent,) = add_up(sent[0])
    attn_near_got = across(attn_near_sent, 2)
    order = [far_x, attn_near_sent, small] + outer_sent
    (grad_input,) = call(
        functools.partial(input_back_kernel, info=info), (passages,),
        [(after(numbers, *order), smem),
         (inputs, by_passage(width)), (gains, gain_spec), (grad_residual, by_passage(width)),
         (d_near, by_passage(3 * cols)), (d_far, by_passage(3 * cols)),
         (w_query, weight_spec), (w_key, weight_spec), (w_value, weight_spec)]
        + [(a, anywhere) for a in attn_pieces],
        [((rows_n, width), F32, by_passage(width))],
        qkv_scratch + [dma], 12 * rows_n * width * cols, "input_back",
    )
    far_x_got = after(far_x_got, grad_input)
    rows = attn_near_sent.shape[0]
    attn_near_got = after(attn_near_got, grad_input, far_x_got, *outer_got)
    attn, sent = cut(attn_near + [whole(attn_near_got), whole(far_x_got[:rows])], 2 ** len(upper[:2]))
    attn_sent = add_up(*sent)
    attn_got = [across(v, d) for v, d in zip(attn_sent, distances(upper[:2]), strict=True)]
    inner = inner_near + [whole(after(far_x_got, *attn_sent)[rows:])]
    grad_inner = finish(inner, bits_in[2:])
    outer = outer + [whole(after(got, *attn_sent)) for got in outer_got]
    grad_outer = finish(outer, upper[2:]).T
    attn_grads = finish(attn + [whole(after(got, grad_inner, grad_outer)) for got in attn_got], upper[2:])
    grad_query, grad_key, grad_value = (attn_grads[:, n * cols : (n + 1) * cols] for n in range(3))
    grad_output = attn_grads[:, 3 * cols :].T

    small = after(small, *attn_sent)
    grad_gain_one = small[: width // 128].reshape(width)
    grad_gain_two = small[small_rows : small_rows + width // 128].reshape(width)
    grad_table = small[table_at : table_at + heads, :BUCKETS].T
    return (
        layer_out, grad_input, grad_gain_one, grad_query, grad_key, grad_value, grad_output,
        grad_table, grad_gain_two, grad_inner, grad_outer,
    )


def solution(mesh):
    both = ("dp", "tensor")
    in_specs = (
        P(both, None), P(), P(None, "tensor"), P(None, "tensor"), P(None, "tensor"), P("tensor", None),
        P(None, "tensor"), P(), P(None, "tensor"), P("tensor", None), P("dp"), P(both, None),
    )
    out_specs = (
        P(both, None), P(both, None), P(), P("dp", "tensor"), P("dp", "tensor"), P("dp", "tensor"),
        P("tensor", "dp"), P(None, "tensor"), P(), P("dp", "tensor"), P("tensor", "dp"),
    )
    body = functools.partial(shards, dp=mesh.shape["dp"], tp=mesh.shape["tensor"])
    return jax.shard_map(body, mesh=mesh, in_specs=in_specs, out_specs=out_specs, check_vma=False)
```

```python
import functools

import jax
import jax.numpy as jnp
from jax import lax
from jax.experimental import pallas as pl
from jax.experimental.pallas import tpu as pltpu
from jax.sharding import PartitionSpec as P

HEAD_DIM = 64
BUCKETS = 32
EPS = 1e-6
MASKED = -1e9
GELU_C = 0.7978845608028654
VMEM_BYTES = 60 * 1024 * 1024
F32 = jnp.float32
BF16 = jnp.bfloat16


def dot(left, right):
    return lax.dot_general(left, right, (((1,), (0,)), ((), ())), preferred_element_type=F32)


def dot_t(left, right):
    return lax.dot_general(left, right, (((1,), (1,)), ((), ())), preferred_element_type=F32)


def dot_l(left, right):
    return lax.dot_general(left, right, (((0,), (0,)), ((), ())), preferred_element_type=F32)


def staggered(count, first, second, third):
    for n in range(count + 2):
        if n < count:
            first(n)
        if 0 <= n - 1 < count:
            second(n - 1)
        if 0 <= n - 2 < count:
            third(n - 2)


def bucket_of(offsets):
    distance = jnp.abs(offsets)
    far = jnp.full_like(distance, 8)
    for power in range(1, 8):
        far = far + (distance * distance >= 64 * 2**power).astype(jnp.int32)
    near = jnp.where(distance < 8, distance, far)
    return near + jnp.where(offsets > 0, 16, 0)


def bucket_indicator(seq, count=BUCKETS):
    lane = lax.broadcasted_iota(jnp.int32, (count, 2 * seq), 1)
    offsets = jnp.where(lane < seq, -lane, 2 * seq - lane)
    ids = lax.broadcasted_iota(jnp.int32, (count, 2 * seq), 0)
    return (bucket_of(offsets) == ids).astype(F32)


def fill_bias(table_ref, bias_ref):
    heads, seq, _ = bias_ref.shape
    base = dot(table_ref[:, :BUCKETS], bucket_indicator(seq).astype(BF16))
    for h in range(heads):
        wide = jnp.broadcast_to(base[h : h + 1, :], (seq, 2 * seq))
        bias_ref[h] = pltpu.roll(wide, 0, 1, stride=1, stride_axis=0)[:, :seq]


def head_mask(columns, parity):
    lane = lax.broadcasted_iota(jnp.int32, columns.shape, 1)
    keep = (lane < HEAD_DIM) if parity == 0 else (lane >= HEAD_DIM)
    return jnp.where(keep, columns, jnp.zeros_like(columns))


def rms_rows(values, gain):
    return values * lax.rsqrt(jnp.mean(values * values, axis=-1, keepdims=True) + EPS) * gain


def add_row(ref, row):
    for n in range(row.shape[1] // 128):
        ref[n : n + 1, :] += row[:, n * 128 : (n + 1) * 128]


def rms_back(values, gain, grads):
    scale = lax.rsqrt(jnp.mean(values * values, axis=-1, keepdims=True) + EPS)
    scaled = grads * gain
    mean = jnp.mean(scaled * values, axis=-1, keepdims=True)
    back = scale * scaled - values * (scale * scale * scale * mean)
    return back, jnp.sum(grads * values * scale, axis=0, keepdims=True)


def fill_perm(perm_ref, me, dp, bits):
    width = perm_ref.shape[0]
    block = width // dp
    index = lax.broadcasted_iota(jnp.int32, (width, 128), 0)
    rel = lax.div(index, block)
    target = jnp.zeros_like(rel)
    for n, bit in enumerate(bits):
        target = target + ((rel >> (len(bits) - 1 - n)) & 1) * bit
    source = (target ^ me) * block + (index - rel * block)
    lane = lax.broadcasted_iota(jnp.int32, (width, 128), 1)
    for n in range(0, width, 128):
        perm_ref[:, n : n + 128] = jnp.where(source == lane + n, 1.0, 0.0).astype(BF16)


def piece_copies(packets, quarter, sem, routes):
    copies = []
    for pieces, ways in zip(packets, routes, strict=True):
        for n, piece in enumerate(pieces):
            for rows, cols, target, count, at in ways:
                start = pl.multiple_of((quarter ^ n) * count, 16)
                copies.append((piece.at[rows, cols], target.at[pl.ds(start, count), at], sem))
    return copies


def start_all(copies):
    for copy in copies:
        pltpu.make_async_copy(*copy).start()


def wait_all(copies):
    for copy in copies:
        pltpu.make_async_copy(*copy).wait()


def gather_pieces(packets, quarter, sem, routes):
    copies = piece_copies(packets, quarter, sem, routes)
    start_all(copies)
    wait_all(copies)


class Heads:
    def __init__(self, seq, heads, lengths, bias_ref, q_ref, k_ref, v_ref, ctx_ref, lse_ref):
        self.seq, self.heads, self.lengths = seq, heads, lengths
        self.bias_ref, self.lse_ref = bias_ref, lse_ref
        self.q_ref, self.k_ref, self.v_ref, self.ctx_ref = q_ref, k_ref, v_ref, ctx_ref
        self.first_head = lax.broadcasted_iota(jnp.int32, (seq, 2 * HEAD_DIM), 1) < HEAD_DIM
        self.key_slot = lax.broadcasted_iota(jnp.int32, (seq, 1), 0)
        self.query_t, self.logits, self.probs, self.parts = {}, {}, {}, {}

    def rows_of(self, p):
        return slice(p * self.seq, (p + 1) * self.seq)

    def pair_of(self, h):
        lo = (h // 2) * 2 * HEAD_DIM
        return slice(lo, lo + 2 * HEAD_DIM)

    def project(self, p, rows, wq_ref, wk_ref, wv_ref):
        query = dot(rows, wq_ref[...]).astype(BF16)
        self.q_ref[self.rows_of(p), :] = query
        self.k_ref[self.rows_of(p), :] = dot(rows, wk_ref[...]).astype(BF16)
        self.v_ref[self.rows_of(p), :] = dot(rows, wv_ref[...]).astype(BF16)
        self.query_t[p] = query.T

    def score(self, n):
        p, h = divmod(n, self.heads)
        both = self.pair_of(h)
        keys = head_mask(self.k_ref[self.rows_of(p), both], h % 2)
        self.logits[n] = dot(keys, self.query_t[p][both, :])

    def normalise(self, n):
        p, h = divmod(n, self.heads)
        valid = self.key_slot < self.lengths[p]
        biased = jnp.where(valid, self.logits.pop(n) + self.bias_ref[h], MASKED)
        peak = jnp.max(biased, axis=0, keepdims=True)
        terms = jnp.exp(biased - peak)
        total = jnp.sum(terms, axis=0, keepdims=True)
        self.probs[n] = (terms * (1.0 / total)).astype(BF16)
        self.lse_ref[p, h : h + 1, :] = peak + jnp.log(total)

    def combine(self, n):
        p, h = divmod(n, self.heads)
        self.parts[n] = dot_l(self.probs.pop(n), self.v_ref[self.rows_of(p), self.pair_of(h)])
        if h % 2:
            both = jnp.where(self.first_head, self.parts.pop(n - 1), self.parts.pop(n))
            self.ctx_ref[self.rows_of(p), self.pair_of(h)] = both.astype(BF16)


def attn_first_kernel(
    len_ref, x_ref, gain_ref, wq_ref, wk_ref, wv_ref, table_ref,
    rows_ref, q_ref, k_ref, v_ref, ctx_ref, lse_ref, bias_ref, *, info,
):
    p = pl.program_id(0)
    seq = rows_ref.shape[0]

    @pl.when(p == 0)
    def _():
        fill_bias(table_ref, bias_ref)

    rows = rms_rows(x_ref[...].astype(F32), gain_ref[0:1, :].astype(F32)).astype(BF16)
    rows_ref[...] = rows
    lengths = [len_ref[len_ref[info + 1] + p]]
    work = Heads(seq, bias_ref.shape[0], lengths, bias_ref, q_ref, k_ref, v_ref, ctx_ref, lse_ref)
    work.project(0, rows, wq_ref, wk_ref, wv_ref)
    staggered(work.heads, work.score, work.normalise, work.combine)


def turn_kernel(
    len_ref, rows_ref, cot_ref, rows_t_ref, cot_t_ref, perm_ref, perm_in_ref, *, dp, info, orders,
):
    @pl.when(pl.program_id(0) == 0)
    def _():
        fill_perm(perm_ref, len_ref[info], dp, orders[0])
        fill_perm(perm_in_ref, len_ref[info], dp, orders[1])

    rows_t_ref[...] = dot_t(perm_ref[...], rows_ref[...]).astype(BF16)
    cot_t_ref[...] = dot_t(perm_ref[...], cot_ref[...]).astype(BF16)


def projection_routes(piece_rows, cols, targets):
    rows = slice(0, piece_rows)
    return [
        (rows, slice(n * cols, (n + 1) * cols), target, piece_rows, slice(0, cols))
        for n, target in enumerate(targets)
    ]


def output_routes(piece_rows, cols, target):
    half, lanes = piece_rows // 2, slice(cols, 2 * cols)
    return [
        (slice(0, half), lanes, target, half, slice(0, cols)),
        (slice(half, piece_rows), lanes, target, half, slice(cols, 2 * cols)),
    ]


def attn_second_kernel(len_ref, gain_ref, rows_hbm, x_hbm, ctx_first_hbm, perm_hbm, *refs, seq, info):
    qk_pieces, vo_pieces = refs[:4], refs[4:8]
    (
        wo_first_hbm, q_hbm, k_hbm, v_hbm, ctx_hbm, lse_ref, resid_hbm, rows_two_hbm, rows_two_t_hbm, table_ref,
        bias_ref, wq_ref, wk_ref, wv_ref, wo_ref, wo_first_ref, rows_ref, x_ref, ctx_first_ref, perm_ref,
        q_ref, k_ref, v_ref, ctx_ref, resid_ref, rows_two_ref, rows_two_t_ref, piece_sem, in_sems, out_sems,
    ) = refs[8:]
    rows, cols = wq_ref.shape[0] // 4, wq_ref.shape[1]
    heads = bias_ref.shape[0]
    passages = q_ref.shape[0] // seq
    quarter = len_ref[info] & 3
    get_table = [(qk_pieces[0].at[rows : rows + 16, :128], table_ref, in_sems.at[0])]
    projections = piece_copies(
        (qk_pieces, vo_pieces), quarter, piece_sem.at[0],
        [projection_routes(rows, cols, (wq_ref, wk_ref)), projection_routes(rows, cols, (wv_ref,))],
    )
    get_rows = [(rows_hbm, rows_ref, in_sems.at[1])]
    output = piece_copies((vo_pieces,), quarter, piece_sem.at[1], [output_routes(rows, cols, wo_ref)])
    output += [
        (wo_first_hbm, wo_first_ref, in_sems.at[2]), (ctx_first_hbm, ctx_first_ref, in_sems.at[3]),
        (x_hbm, x_ref, in_sems.at[4]), (perm_hbm, perm_ref, in_sems.at[5]),
    ]
    start_all(get_table + get_rows + projections + output)
    wait_all(get_table)
    fill_bias(table_ref, bias_ref)
    wait_all(get_rows + projections)
    lengths = [len_ref[len_ref[info + 1] + p] for p in range(passages)]
    work = Heads(seq, heads, lengths, bias_ref, q_ref, k_ref, v_ref, ctx_ref, lse_ref)
    out = []

    def put(ref, hbm, at, sem):
        copy = (ref.at[at], hbm.at[at], out_sems.at[sem])
        out.append(copy)
        start_all([copy])

    def project(p):
        here = work.rows_of(p)
        work.project(p, rows_ref[here, :], wq_ref, wk_ref, wv_ref)
        for n, (ref, hbm) in enumerate(((q_ref, q_hbm), (k_ref, k_hbm), (v_ref, v_hbm))):
            put(ref, hbm, (here, slice(None)), 7 * p + n)

    def branch(p):
        here = work.rows_of(p)
        if p == 0:
            wait_all(output)
        total = dot(ctx_first_ref[here, :], wo_first_ref[...]) + dot(ctx_ref[here, :], wo_ref[...])
        residual = x_ref[here, :].astype(F32) + total
        resid_ref[here, :] = residual
        rows_two_ref[here, :] = rms_rows(residual, gain_ref[1:2, :].astype(F32)).astype(BF16)
        pairs = ((ctx_ref, ctx_hbm), (resid_ref, resid_hbm), (rows_two_ref, rows_two_hbm))
        for n, (ref, hbm) in enumerate(pairs):
            put(ref, hbm, (here, slice(None)), 7 * p + 3 + n)

    def turn(p):
        here = work.rows_of(p)
        rows_two_t_ref[:, here] = dot_t(perm_ref[...], rows_two_ref[here, :]).astype(BF16)
        put(rows_two_t_ref, rows_two_t_hbm, (slice(None), here), 7 * p + 6)

    for p in range(passages):
        project(p)
    count = passages * heads
    for n in range(count + 2):
        if n < count:
            work.score(n)
        if 0 <= n - 1 < count:
            work.normalise(n - 1)
        if 0 <= n - 2 < count:
            work.combine(n - 2)
        done = (n - 2) // heads
    for p in range(passages):
        branch(p)
    for p in range(passages):
        turn(p)
    wait_all(out)


class Hidden:
    def __init__(self, refs, weight_refs, weight_hbms, sems, chunk, block):
        (
            self.rows_ref, self.cot_ref, self.wi_ref, self.wo_ref, self.rows_t_ref, self.cot_t_ref, self.ffn_ref,
            self.back_ref, self.act_ref, self.grad_ref,
        ) = refs
        self.weight_refs, self.weight_hbms, self.sems = weight_refs, weight_hbms, sems
        self.chunk, self.block = chunk, block
        self.chunks = self.rows_ref.shape[0] // chunk
        self.blocks = self.wi_ref.shape[1] // block
        self.out = []

    def rows_of(self, i):
        return slice(i * self.chunk, (i + 1) * self.chunk)

    def hidden(self, b, ready):
        units = slice(b * self.block, (b + 1) * self.block)

        def first(i):
            at = self.rows_of(i)
            ready(b, i, 0)
            v = dot(self.rows_ref[at, :], self.wi_ref[:, units])
            ready(b, i, 1)
            grad_act = dot_t(self.cot_ref[at, :], self.wo_ref[units, :])
            square = v * v
            tanh = jnp.tanh(GELU_C * v * (1.0 + 0.044715 * square))
            half = 0.5 + 0.5 * tanh
            self.act_ref[at, units] = (v * half).astype(BF16)
            slope = half + (0.5 * GELU_C) * v * (1.0 - tanh * tanh) * (1.0 + 0.134145 * square)
            self.grad_ref[at, units] = (grad_act * slope).astype(BF16)

        def second(i):
            at = self.rows_of(i)
            forward = dot(self.act_ref[at, units], self.wo_ref[units, :])
            backward = dot_t(self.grad_ref[at, units], self.wi_ref[:, units])
            if b:
                self.ffn_ref[at, :] += forward
                self.back_ref[at, :] += backward
            else:
                self.ffn_ref[at, :] = forward
                self.back_ref[at, :] = backward

        staggered(self.chunks, first, second, lambda i: None)

    def weights(self, b, which):
        units = slice(b * self.block, (b + 1) * self.block)
        ref = self.weight_refs[which]
        half_rows = ref.shape[0]
        at = slice(half_rows, None) if which < 2 else slice(half_rows)
        left, right = ((self.rows_t_ref, self.grad_ref), (self.cot_t_ref, self.act_ref))[which % 2]
        ref[:, units] = dot(left[at, :], right[:, units]).astype(BF16)
        self.put(ref, self.weight_hbms[which], (slice(None), units))

    def put(self, ref, hbm, at):
        self.out.append((ref.at[at], hbm.at[at], self.sems.at[len(self.out)]))
        start_all(self.out[-1:])


def ffn_first_kernel(rows_hbm, cot_hbm, wi_hbm, wo_hbm, rows_t_hbm, cot_t_hbm, ffn_hbm, back_hbm, *refs, chunk, block):
    weight_hbms, work_refs, weight_refs, in_sems, out_sems = refs[:4], refs[4:14], refs[14:18], refs[18], refs[19]
    work = Hidden(work_refs, weight_refs, weight_hbms, out_sems, chunk, block)
    copies = {}

    def get(key, hbm, ref, at):
        copies[key] = [(hbm.at[at], ref.at[at], in_sems.at[len(copies)])]
        start_all(copies[key])

    everything = slice(None)

    def get_weights(b):
        units = slice(b * block, (b + 1) * block)
        get(("weight", b, 0), wi_hbm, work.wi_ref, (everything, units))
        get(("weight", b, 1), wo_hbm, work.wo_ref, (units, everything))

    def get_rows(i):
        get(("rows", i, 0), rows_hbm, work.rows_ref, (work.rows_of(i), everything))
        get(("rows", i, 1), cot_hbm, work.cot_ref, (work.rows_of(i), everything))

    def ready(b, i, which):
        if i == 0:
            wait_all(copies["weight", b, which])
        if b == 0:
            wait_all(copies["rows", i, which])
        if b == 0 and i == 0 and which == 1:
            for n in range(1, work.blocks):
                get_weights(n)
            get("turned rows", rows_t_hbm, work.rows_t_ref, (everything, everything))
            get("turned cot", cot_t_hbm, work.cot_t_ref, (everything, everything))

    get_rows(0)
    get_weights(0)
    for i in range(1, work.chunks):
        get_rows(i)
    for b in range(work.blocks):
        work.hidden(b, ready)
        if b == 0:
            wait_all(copies["turned rows"] + copies["turned cot"])
        if b == work.blocks - 1:
            work.put(work.ffn_ref, ffn_hbm, (everything, everything))
            work.put(work.back_ref, back_hbm, (everything, everything))
        for which in range(4):
            work.weights(b, which)
    wait_all(work.out)


def ffn_second_kernel(
    info_ref, gain_ref, rows_hbm, cot_hbm, rows_t_hbm, cot_t_hbm, *refs, chunk, late_chunk, block, info,
):
    inner_pieces, outer_pieces = refs[:4], refs[4:8]
    (
        ffn_in_hbm, back_in_hbm, resid_hbm, perm_hbm,
        layer_hbm, grad_resid_hbm, grad_attn_hbm, grad_attn_t_hbm, gain_grad_ref,
    ) = refs[8:17]
    weight_hbms, work_refs, weight_refs = refs[17:21], refs[21:31], refs[31:35]
    (
        ffn_in_ref, back_in_ref, resid_ref, perm_ref, layer_ref, grad_resid_ref, grad_attn_ref, grad_attn_t_ref,
        piece_sems, in_sems, out_sems,
    ) = refs[35:]
    work = Hidden(work_refs, weight_refs, weight_hbms, out_sems, chunk, block)
    width, hidden = work.wi_ref.shape
    wi_rows, wo_rows = width // 4, hidden // 4
    quarter = info_ref[info] & 3
    everything = slice(None)
    inner = [
        piece_copies(
            (inner_pieces,), quarter, piece_sems.at[b],
            [[(slice(0, wi_rows), slice(b * block, (b + 1) * block), work.wi_ref, wi_rows,
               slice(b * block, (b + 1) * block))]],
        )
        for b in range(work.blocks)
    ]
    outer = piece_copies(
        (outer_pieces,), quarter, piece_sems.at[work.blocks],
        [[(slice(0, wo_rows), slice(0, width), work.wo_ref, wo_rows, slice(0, width))]],
    )
    rows_in = []
    for i in range(work.chunks):
        at = (work.rows_of(i), everything)
        rows_in.append([
            (rows_hbm.at[at], work.rows_ref.at[at], in_sems.at[2 * i]),
            (cot_hbm.at[at], work.cot_ref.at[at], in_sems.at[2 * i + 1]),
        ])
    base = 2 * work.chunks
    turned = [(rows_t_hbm, work.rows_t_ref, in_sems.at[base]), (cot_t_hbm, work.cot_t_ref, in_sems.at[base + 1])]
    late = [
        (back_in_hbm, back_in_ref, in_sems.at[base + 2]), (resid_hbm, resid_ref, in_sems.at[base + 3]),
        (ffn_in_hbm, ffn_in_ref, in_sems.at[base + 4]), (perm_hbm, perm_ref, in_sems.at[base + 5]),
    ]

    def ready(b, i, which):
        if i == 0 and which == 0:
            wait_all(inner[b])
        if i == 0 and b == 0 and which == 1:
            wait_all(outer)
        if b == 0:
            wait_all(rows_in[i][which : which + 1])
        if b == 0 and i == 0 and which == 1:
            for n in range(1, work.blocks):
                start_all(inner[n])
            start_all(turned)

    start_all(rows_in[0][:1] + inner[0] + rows_in[0][1:] + outer)
    for i in range(1, work.chunks):
        start_all(rows_in[i])
    last = work.blocks - 1
    for b in range(work.blocks):
        if b == last:
            start_all(late)
        work.hidden(b, ready)
        if b == 0:
            wait_all(turned)
        if b < last:
            for which in range(4):
                work.weights(b, which)
    wait_all(late)
    gain_grad_ref[...] = jnp.zeros_like(gain_grad_ref)
    count = resid_ref.shape[0] // late_chunk
    for i in range(count):
        at = slice(i * late_chunk, (i + 1) * late_chunk)
        residual = resid_ref[at, :]
        back, gain_part = rms_back(residual, gain_ref[1:2, :].astype(F32), work.back_ref[at, :] + back_in_ref[at, :])
        add_row(gain_grad_ref, gain_part)
        grad_resid = work.cot_ref[at, :].astype(F32) + back
        grad_resid_ref[at, :] = grad_resid
        grad_attn_ref[at, :] = grad_resid.astype(BF16)
        layer_ref[at, :] = (residual + (work.ffn_ref[at, :] + ffn_in_ref[at, :])).astype(BF16)
        if i < 3:
            work.weights(last, i)
        for ref, hbm in ((grad_attn_ref, grad_attn_hbm), (grad_resid_ref, grad_resid_hbm), (layer_ref, layer_hbm)):
            work.put(ref, hbm, (at, everything))
    grad_attn_t_ref[...] = dot_t(perm_ref[...], grad_attn_ref[...]).astype(BF16)
    work.put(grad_attn_t_ref, grad_attn_t_hbm, (everything, everything))
    for which in range(min(count, 3), 4):
        work.weights(last, which)
    wait_all(work.out)


def gain_from_weights(me, bits, w_refs, grads, perm_ref, gain_ref, out_ref):
    width, cols = w_refs[0].shape
    block = width // (2 ** len(bits))
    if block % 16:
        weights = [dot(perm_ref[...], ref[...]) for ref in w_refs]
    else:
        weights = []
        for ref in w_refs:
            rows = []
            for n in range(width // block):
                target = sum(bit for m, bit in enumerate(bits) if (n >> (len(bits) - 1 - m)) & 1)
                rows.append(ref[pl.ds(pl.multiple_of((me ^ target) * block, 16), block), :])
            weights.append(jnp.concatenate(rows, axis=0).astype(F32))
    folded = None
    for n, weight in enumerate(weights):
        for lo in range(0, cols, 128):
            term = weight[:, lo : lo + 128] * grads[:, n * cols + lo : n * cols + lo + 128]
            folded = term if folded is None else folded + term
    ordered = jnp.sum(folded.T, axis=0, keepdims=True)
    high = ordered.astype(BF16)
    middle = (ordered - high.astype(F32)).astype(BF16)
    low = (ordered - high.astype(F32) - middle.astype(F32)).astype(BF16)
    parts = jnp.concatenate([high, middle, low, jnp.zeros((13, width), BF16)], axis=0)
    natural = jnp.sum(dot(parts, perm_ref[...]), axis=0, keepdims=True) / gain_ref[0:1, :].astype(F32)
    out_ref[...] = jnp.zeros_like(out_ref)
    add_row(out_ref, natural)


def attn_back_kernel(len_ref, *refs, seq, info, bits, far):
    if far:
        qk_pieces, vo_pieces, refs = refs[:4], refs[4:8], refs[8:]
    else:
        weights_hbm, vector_refs, own_ref, block_ref = refs[:4], refs[4:7], refs[20], refs[-1]
        refs = refs[7:20] + refs[21:-1]
    (
        grad_attn_hbm, q_hbm, k_hbm, v_hbm, lse_ref, table_ref, rows_t_hbm, grad_attn_t_hbm, ctx_hbm, perm_hbm,
        gain_ref, dqkv_hbm, send_hbm, keep_hbm, table_grad_ref, gain_grad_ref,
        wq_ref, wk_ref, wv_ref, wo_ref, grad_attn_ref, q_ref, k_ref, v_ref, rows_t_ref, grad_attn_t_ref, ctx_ref,
        perm_ref, dqkv_ref, send_ref, keep_ref, bias_ref, sums_ref, grads_ref, piece_sem, in_sems, out_sems,
    ) = refs
    heads = bias_ref.shape[0]
    cols = heads * HEAD_DIM
    passages = q_ref.shape[0] // seq
    half_rows = keep_ref.shape[0]

    def rows_of(p):
        return slice(p * seq, (p + 1) * seq)

    if far:
        rows = wq_ref.shape[0] // 4
        quarter = len_ref[info] & 3
        late_weights = piece_copies(
            (qk_pieces, vo_pieces), quarter, piece_sem.at[0],
            [projection_routes(rows, cols, (wq_ref, wk_ref)), projection_routes(rows, cols, (wv_ref,))],
        )
        output = piece_copies((vo_pieces,), quarter, piece_sem.at[1], [output_routes(rows, cols, wo_ref)])
    else:
        late_weights = [
            (hbm, ref, piece_sem.at[n])
            for n, (hbm, ref) in enumerate(zip(weights_hbm, (wq_ref, wk_ref, wv_ref), strict=False))
        ]
        output = [(weights_hbm[3], wo_ref, piece_sem.at[3])]
    start_all(output)
    by_passage = []
    for p in range(passages):
        pairs = ((grad_attn_hbm, grad_attn_ref), (q_hbm, q_ref), (k_hbm, k_ref), (v_hbm, v_ref))
        by_passage.append(
            [(hbm.at[rows_of(p), :], ref.at[rows_of(p), :], in_sems.at[4 * p + n]) for n, (hbm, ref) in enumerate(pairs)]
        )
    start_all(by_passage[0])
    at = 4 * passages
    turned = [(ctx_hbm, ctx_ref, in_sems.at[at]), (grad_attn_t_hbm, grad_attn_t_ref, in_sems.at[at + 1])]
    last = [(rows_t_hbm, rows_t_ref, in_sems.at[at + 2]), (perm_hbm, perm_ref, in_sems.at[at + 3])]
    fill_bias(table_ref, bias_ref)
    sums_ref[...] = jnp.zeros_like(sums_ref)
    wait_all(output)
    first_head = lax.broadcasted_iota(jnp.int32, (seq, 2 * HEAD_DIM), 1) < HEAD_DIM
    key_slot = lax.broadcasted_iota(jnp.int32, (seq, 1), 0)
    ready, scores, weights, dq, dk, dv = {}, {}, {}, {}, {}, {}

    def pair_of(h, offset=0):
        lo = (h // 2) * 2 * HEAD_DIM + offset
        return slice(lo, lo + 2 * HEAD_DIM)

    def prepare(p):
        wait_all(by_passage[p])
        grad_ctx = dot_t(grad_attn_ref[rows_of(p), :], wo_ref[...]).astype(BF16)
        valid = key_slot < len_ref[len_ref[info + 1] + p]
        ready[p] = (
            grad_ctx, grad_ctx.T, q_ref[rows_of(p), :].T, k_ref[rows_of(p), :].T, valid,
        )

    def score(n):
        p, h = divmod(n, heads)
        _, grad_ctx_t, query_t, _, _ = ready[p]
        both = pair_of(h)
        scores[n] = (
            dot(head_mask(k_ref[rows_of(p), both], h % 2), query_t[both, :]),
            dot(head_mask(v_ref[rows_of(p), both], h % 2), grad_ctx_t[both, :]),
        )

    def soften(n):
        p, h = divmod(n, heads)
        logits, grad_probs = scores.pop(n)
        probs = jnp.exp(logits + bias_ref[h] - lse_ref[p, h : h + 1, :])
        probs = jnp.where(ready[p][4], probs, 0.0)
        mixed = jnp.sum(probs * grad_probs, axis=0, keepdims=True)
        grads = (probs * (grad_probs - mixed)).astype(BF16)
        sums_ref[h] += grads.astype(F32)
        weights[n] = (probs.astype(BF16), grads)

    def combine(n):
        p, h = divmod(n, heads)
        grad_ctx, _, _, keys_t, _ = ready[p]
        probs, grads = weights.pop(n)
        dq[n] = dot(keys_t[h * HEAD_DIM : (h + 1) * HEAD_DIM, :], grads)
        dk[n] = dot(grads, q_ref[rows_of(p), pair_of(h)])
        dv[n] = dot(probs, grad_ctx[:, pair_of(h)])
        if h % 2:
            dqkv_ref[rows_of(p), pair_of(h, cols)] = jnp.where(first_head, dk.pop(n - 1), dk.pop(n)).astype(BF16)
            dqkv_ref[rows_of(p), pair_of(h, 2 * cols)] = jnp.where(first_head, dv.pop(n - 1), dv.pop(n)).astype(BF16)
        if h == heads - 1:
            parts = jnp.concatenate([dq.pop(m) for m in range(n - h, n + 1)], axis=0)
            dqkv_ref[rows_of(p), :cols] = parts.astype(BF16).T
            copy = (dqkv_ref.at[rows_of(p), :], dqkv_hbm.at[rows_of(p), :], out_sems.at[p])
            out.append(copy)
            start_all([copy])

    out = []
    count = passages * heads
    for p in range(1, passages):
        start_all(by_passage[p])
    start_all(turned)
    for p in range(passages):
        prepare(p)
    for n in range(count + 2):
        if n == heads:
            start_all(last + late_weights)
        if n < count:
            score(n)
        if 0 <= n - 1 < count:
            soften(n - 1)
        if 0 <= n - 2 < count:
            combine(n - 2)
        if n == heads:
            wait_all(turned)
            send_ref[:, 3 * cols :] = dot(grad_attn_t_ref[half_rows:, :], ctx_ref[...]).astype(BF16)
        if n == heads + 2:
            keep_ref[:, 3 * cols :] = dot(grad_attn_t_ref[:half_rows, :], ctx_ref[...]).astype(BF16)
    wait_all(last)
    for ref, hbm, at, sem in (
        (send_ref, send_hbm, slice(half_rows, None), passages), (keep_ref, keep_hbm, slice(half_rows), passages + 1),
    ):
        grads_ref[at, :] = dot(rows_t_ref[at, :], dqkv_ref[...])
        ref[:, : 3 * cols] = grads_ref[at, :].astype(BF16)
        copy = (ref, hbm.at[:, : 4 * cols], out_sems.at[sem])
        out.append(copy)
        start_all([copy])
    wait_all(late_weights)
    gain_from_weights(
        len_ref[info], bits, (wq_ref, wk_ref, wv_ref), grads_ref, perm_ref, gain_ref, gain_grad_ref
    )
    rows = []
    for h in range(heads):
        folded = jnp.zeros((8, 2 * seq), F32)
        for a in range(0, seq, 8):
            wide = jnp.concatenate([sums_ref[h, a : a + 8, :], jnp.zeros((8, seq), F32)], axis=1)
            folded = folded + (pltpu.roll(wide, 2 * seq - a, 1) if a else wide)
        diagonals = folded[0:1, :]
        for b in range(1, 8):
            diagonals = diagonals + pltpu.roll(folded[b : b + 1, :], 2 * seq - b, 1)
        rows.append(diagonals)
    rows.append(jnp.zeros((8 - heads, 2 * seq), F32))
    table_grad_ref[...] = lax.dot_general(
        jnp.concatenate(rows, axis=0), bucket_indicator(seq, 128), (((1,), (1,)), ((), ())),
        precision=lax.Precision.HIGHEST, preferred_element_type=F32,
    )
    if not far:
        gain_two_ref, gain_far_ref, table_far_ref = vector_refs
        own = jnp.concatenate(
            [gain_grad_ref[...] + gain_far_ref[...], gain_two_ref[...], table_grad_ref[...], table_far_ref[...]], axis=0)
        own_ref[...] = own
        high = own.astype(BF16)
        middle = (own - high.astype(F32)).astype(BF16)
        low = (own - high.astype(F32) - middle.astype(F32)).astype(BF16)
        block_ref[...] = jnp.concatenate(
            [jnp.concatenate([high, middle], axis=1), jnp.concatenate([low, jnp.zeros_like(low)], axis=1)], axis=0)
        rows, lanes = block_ref.shape
        out.append(
            (block_ref, send_hbm.at[:rows, 4 * cols : 4 * cols + lanes], out_sems.at[passages + 2])
        )
        start_all(out[-1:])
    wait_all(out)


def input_back_kernel(
    info_ref, x_ref, gain_ref, grad_resid_ref, d_first_ref, d_second_ref,
    wq_first_ref, wk_first_ref, wv_first_ref, *refs, info,
):
    qk_pieces, vo_pieces = refs[:4], refs[4:8]
    grad_input_ref, wq_ref, wk_ref, wv_ref, sem = refs[8:]

    @pl.when(pl.program_id(0) == 0)
    def _():
        rows, cols = wq_ref.shape[0] // 4, wq_ref.shape[1]
        gather_pieces(
            (qk_pieces, vo_pieces), info_ref[info] & 3, sem,
            [projection_routes(rows, cols, (wq_ref, wk_ref)), projection_routes(rows, cols, (wv_ref,))],
        )

    width = wq_ref.shape[1]
    total = None
    for d_ref, refs in (
        (d_first_ref, (wq_first_ref, wk_first_ref, wv_first_ref)),
        (d_second_ref, (wq_ref, wk_ref, wv_ref)),
    ):
        for n, ref in enumerate(refs):
            term = dot_t(d_ref[:, n * width : (n + 1) * width], ref[...])
            total = term if total is None else total + term
    back, _ = rms_back(x_ref[...].astype(F32), gain_ref[0:1, :].astype(F32), total)
    grad_input_ref[...] = grad_resid_ref[...] + back


def whole_spec(array_shape):
    return pl.BlockSpec(array_shape, lambda i: (0,) * len(array_shape), pipeline_mode=pl.Buffered(1))


def call(kernel, grid, ins, outs, scratch, cost, name):
    arrays = [a for a, _ in ins]
    return pl.pallas_call(
        kernel,
        grid=grid,
        in_specs=[s for _, s in ins],
        out_specs=[s for _, _, s in outs],
        out_shape=[jax.ShapeDtypeStruct(s, d) for s, d, _ in outs],
        scratch_shapes=scratch,
        compiler_params=pltpu.CompilerParams(
            dimension_semantics=("arbitrary",), vmem_limit_bytes=VMEM_BYTES
        ),
        cost_estimate=pl.CostEstimate(flops=1, bytes_accessed=1, transcendentals=0),
        name=name,
    )(*arrays)


def after(value, *others):
    return lax.optimization_barrier((value,) + others)[0]


def shards(
    inputs, gain_attn, w_query, w_key, w_value, w_output, relative_bias_table,
    gain_ffn, w_inner, w_outer, lengths, cotangent, *, dp, tp,
):
    rows_n, width = inputs.shape
    groups = lengths.shape[0]
    passages = groups // tp
    seq = rows_n // passages
    cols = w_query.shape[1]
    heads = cols // HEAD_DIM
    hidden = w_inner.shape[1]
    me = lax.axis_index("dp")
    side = lax.axis_index("tensor")
    rest = dp // 4

    def across(value, distance):
        return lax.ppermute(value, "dp", [(i, i ^ distance) for i in range(dp)])

    def beside(value):
        return lax.ppermute(value, "tensor", [(i, tp - 1 - i) for i in range(tp)])

    def across_beside(value, distance):
        pairs = [(i * tp + t, (i ^ distance) * tp + tp - 1 - t) for i in range(dp) for t in range(tp)]
        return lax.ppermute(value, ("dp", "tensor"), pairs)

    quarter = me & 3

    def part(weight, axis=0):
        count = weight.shape[axis] // 4
        return lax.dynamic_slice_in_dim(weight, quarter * count, count, axis)

    wo_part = part(w_output)
    wo_part = jnp.concatenate([wo_part[:, :cols], wo_part[:, cols:]], axis=0)
    table = jnp.pad(relative_bias_table.T, ((0, 16 - heads), (0, 128 - BUCKETS)))
    qk_part = jnp.concatenate(
        [jnp.concatenate([part(w_query), part(w_key)], axis=1), jnp.pad(table, ((0, 0), (0, 2 * cols - 128)))], axis=0)
    vo_part = jnp.concatenate([part(w_value), wo_part], axis=1)
    qk_got, vo_got = beside(qk_part), beside(vo_part)
    inner_part = part(after(w_inner, qk_part, vo_part))
    numbers = jnp.concatenate([lengths, jnp.stack([me, side * passages]).astype(jnp.int32)])
    info = groups
    gains = jnp.stack([gain_attn, gain_ffn])

    smem = pl.BlockSpec(memory_space=pltpu.SMEM)
    anywhere = pl.BlockSpec(memory_space=pltpu.HBM)
    by_passage = lambda c: pl.BlockSpec((seq, c), lambda p: (p, 0))
    by_passage_t = pl.BlockSpec((width, seq), lambda p: (0, p))
    lse_spec = pl.BlockSpec((1, 8, seq), lambda p: (p, 0, 0))
    weight_spec = whole_spec((width, cols))
    table_spec = whole_spec((16, 128))
    gain_spec = whole_spec((2, width))
    perm_spec = whole_spec((width, width))
    small_rows = -(-width // 1024) * 8
    small_out = ((small_rows, 128), F32, whole_spec((small_rows, 128)))
    wo_spec = whole_spec((cols, width))
    qkv_outs = [((rows_n, cols), BF16, by_passage(cols))] * 4 + [((passages, 8, seq), F32, lse_spec)]
    bias_scratch = pltpu.VMEM((heads, seq, seq), F32)
    qkv_scratch = [pltpu.VMEM((width, cols), BF16)] * 3
    wo_scratch = pltpu.VMEM((cols, width), BF16)
    dma = pltpu.SemaphoreType.DMA
    cols_vmem = pltpu.VMEM((rows_n, cols), BF16)
    acc_hbm = ((rows_n, width), F32, anywhere)
    rows_hbm = ((rows_n, width), BF16, anywhere)
    turned_hbm = ((width, rows_n), BF16, anywhere)
    acc_vmem = pltpu.VMEM((rows_n, width), F32)
    rows_vmem = pltpu.VMEM((rows_n, width), BF16)
    turned_vmem = pltpu.VMEM((width, rows_n), BF16)
    attn_cost = 2 * rows_n * (width * 3 * cols + seq * 4 * cols)

    bits = [2**n for n in range(1, dp.bit_length() - 1)]
    upper = bits[1:]
    bits_in = upper[:2] + bits[:1] + upper[2:]
    rows_one, q_near, k_near, v_near, ctx_near, lse_near = call(
        functools.partial(attn_first_kernel, info=info), (passages,),
        [(after(numbers, qk_part, vo_part, inner_part), smem), (inputs, by_passage(width)), (gains, gain_spec),
         (w_query, weight_spec), (w_key, weight_spec), (w_value, weight_spec), (table, table_spec)],
        [((rows_n, width), BF16, by_passage(width))] + qkv_outs, [bias_scratch], attn_cost, "attn_first",
    )
    qk_got, vo_got = after(qk_got, rows_one), after(vo_got, rows_one)
    qk_second, vo_second = across(qk_got, 2), across(vo_got, 2)
    qk_core, vo_core = across(qk_got, 1), across(vo_got, 1)
    outer_part = part(after(w_outer, qk_got, vo_got))
    inner_got = beside(after(inner_part, qk_got, vo_got))
    rows_one_t, cot_t, perm, perm_in = call(
        functools.partial(turn_kernel, dp=dp, info=info, orders=([1] + bits, [1] + bits_in)), (passages,),
        [(after(numbers, qk_got, vo_got, outer_part), smem), (rows_one, by_passage(width)), (cotangent, by_passage(width))],
        [((width, rows_n), BF16, by_passage_t)] * 2 + [((width, width), BF16, perm_spec)] * 2,
        [], 4 * rows_n * width * width, "turn",
    )
    attn_pieces = [qk_got, qk_core, qk_second, across(after(qk_second, perm), 1)]
    attn_pieces += [vo_got, vo_core, vo_second, across(after(vo_second, perm), 1)]
    outer_got = beside(outer_part)
    inner_got = after(inner_got, perm)
    inner_second = across(inner_got, 2)
    inner_core = across(inner_got, 1)
    q_far, k_far, v_far, ctx_far, lse_far, residual, rows_two, rows_two_t, table_far = call(
        functools.partial(attn_second_kernel, seq=seq, info=info), (1,),
        [(after(numbers, inner_got), smem), (gains, gain_spec), (rows_one, anywhere), (inputs, anywhere),
         (ctx_near, anywhere), (perm_in, anywhere)] + [(a, anywhere) for a in attn_pieces]
        + [(w_output, anywhere)],
        [((rows_n, cols), BF16, anywhere)] * 4 + [((passages, 8, seq), F32, whole_spec((passages, 8, seq)))]
        + [acc_hbm, rows_hbm, turned_hbm, ((16, 128), BF16, table_spec)],
        [bias_scratch] + qkv_scratch + [wo_scratch, wo_scratch, rows_vmem, rows_vmem, cols_vmem]
        + [pltpu.VMEM((width, width), BF16)] + [cols_vmem] * 4 + [acc_vmem, rows_vmem, turned_vmem]
        + [dma((2,)), dma((6,)), dma((7 * passages,))], attn_cost, "attn_second",
    )

    block_hidden = 768 if hidden % 768 == 0 else hidden
    steps = hidden // block_hidden
    chunk_first, chunk_second, chunk_late = min(512, rows_n), rows_n, rows_n
    grad_out = ((width // 2, hidden), BF16, anywhere)
    hidden_vmem = pltpu.VMEM((rows_n, hidden), BF16)
    work_scratch = [rows_vmem] * 2 + [pltpu.VMEM((width, hidden), BF16), pltpu.VMEM((hidden, width), BF16)]
    work_scratch += [turned_vmem] * 2 + [acc_vmem] * 2 + [hidden_vmem] * 2
    work_scratch += [pltpu.VMEM((width // 2, hidden), BF16)] * 4
    ffn_cost = 12 * rows_n * width * hidden
    outer_got = after(outer_got, rows_two)
    outer_second = across(outer_got, 2)
    outer_core = across(outer_got, 1)
    inner_last = across(after(inner_second, rows_two), 1)
    ffn_near, back_near, in_send_near, out_send_near, in_keep_near, out_keep_near = call(
        functools.partial(ffn_first_kernel, chunk=chunk_first, block=block_hidden), (1,),
        [(after(rows_two, outer_got, inner_second, inner_core), anywhere), (cotangent, anywhere),
         (w_inner, anywhere), (w_outer, anywhere), (rows_two_t, anywhere), (cot_t, anywhere)],
        [acc_hbm, acc_hbm] + [grad_out] * 4,
        work_scratch + [dma((2 * (rows_n // chunk_first) + 2 * steps + 2,)), dma((4 * steps + 2,))], ffn_cost, "ffn_first",
    )
    ffn_pieces = [inner_got, inner_core, inner_second, inner_last]
    ffn_pieces += [outer_got, outer_core, outer_second, across(after(outer_second, ffn_near), 1)]

    def whole(array):
        return (array, 0, array.shape[0])

    def part_of(term, n, ways):
        array, which, rows = term
        return (array, which * ways + n, rows // ways)

    def cut(terms, ways=2):
        return [part_of(t, 0, ways) for t in terms], [[part_of(t, n, ways) for t in terms] for n in range(1, ways)]

    def total(terms):
        return sum(array[which * rows : (which + 1) * rows].astype(F32) for array, which, rows in terms)

    def add_up(*groups):
        return [total(terms).astype(BF16) for terms in groups]

    def distances(low_bits):
        return low_bits if len(low_bits) < 2 else [low_bits[1], low_bits[0], low_bits[0] + low_bits[1]]

    out_got_near = across(after(out_send_near, outer_second, inner_last, outer_core), 1)
    in_got_near = across(after(in_send_near, outer_second, inner_last, outer_core), 1)
    outer_near, sent = cut([whole(out_keep_near), whole(out_got_near)])
    inner_near, sent_in = cut([whole(in_keep_near), whole(in_got_near)])
    (outer_near_sent,) = add_up(sent[0])
    (inner_near_sent,) = add_up(sent_in[0])
    outer_near_got = across(outer_near_sent, 2)
    inner_near_got = across(inner_near_sent, bits_in[0])
    (
        layer_out, grad_residual, grad_attn, grad_attn_t, gain_two_part,
        in_send_far, out_send_far, in_keep_far, out_keep_far,
    ) = call(
        functools.partial(
            ffn_second_kernel, chunk=chunk_second, late_chunk=chunk_late, block=block_hidden, info=info), (1,),
        [(after(numbers, outer_near_sent, inner_near_sent), smem), (gains, gain_spec), (rows_two, anywhere),
         (cotangent, anywhere), (rows_two_t, anywhere), (cot_t, anywhere)]
        + [(a, anywhere) for a in ffn_pieces]
        + [(ffn_near, anywhere), (back_near, anywhere), (residual, anywhere), (perm, anywhere)],
        [rows_hbm, acc_hbm, rows_hbm, turned_hbm, small_out] + [grad_out] * 4,
        work_scratch + [acc_vmem] * 3 + [pltpu.VMEM((width, width), BF16)]
        + [rows_vmem, acc_vmem, rows_vmem, turned_vmem]
        + [dma((steps + 1,)), dma((2 * (rows_n // chunk_second) + 6,)),
           dma((4 * steps + 3 * (rows_n // chunk_late) + 1,))],
        ffn_cost, "ffn_second",
    )

    def attn_back(weights, q, k, v, lse, ctx, tab, order, name, vectors=()):
        half_shape = (width // 2, 4 * cols)
        far = not vectors
        sent_shape = half_shape if far else (width // 2, 4 * cols + 256)
        vector_spec = whole_spec((small_rows, 128))
        more_out = [] if far else [((4 * small_rows, 128), F32, whole_spec((4 * small_rows, 128)))]
        more_scratch = [] if far else [pltpu.VMEM((8 * small_rows, 256), BF16)]
        return call(
            functools.partial(attn_back_kernel, seq=seq, info=info, bits=[1] + bits, far=far), (1,),
            [(after(numbers, *order), smem)] + [(w, anywhere) for w in weights] + [(v, vector_spec) for v in vectors]
            + [(grad_attn, anywhere), (q, anywhere), (k, anywhere), (v, anywhere),
               (lse, whole_spec((passages, 8, seq))), (tab, table_spec), (rows_one_t, anywhere),
               (grad_attn_t, anywhere), (ctx, anywhere), (perm, anywhere), (gains, gain_spec)],
            [((rows_n, 3 * cols), BF16, anywhere), (sent_shape, BF16, anywhere)] + more_out
            + [(half_shape, BF16, anywhere), ((8, 128), F32, whole_spec((8, 128))), small_out],
            qkv_scratch + [wo_scratch, rows_vmem] + [cols_vmem] * 3 + [turned_vmem] * 2
            + [cols_vmem, pltpu.VMEM((width, width), BF16), pltpu.VMEM((rows_n, 3 * cols), BF16)]
            + [pltpu.VMEM(half_shape, BF16)] * 2 + [bias_scratch, pltpu.VMEM((heads, seq, seq), F32)]
            + [pltpu.VMEM((width, 3 * cols), F32), dma((4,)), dma((4 * passages + 4,)), dma((passages + 3,))]
            + more_scratch, 2 * rows_n * cols * (5 * width + 5 * seq), name,
        )

    def pack(values):
        high = lax.reduce_precision(values, 8, 7)
        middle = lax.reduce_precision(values - high, 8, 7)
        low = values - high - middle
        return jnp.concatenate(
            [jnp.concatenate([high, middle], axis=1), jnp.concatenate([low, jnp.zeros_like(low)], axis=1)],
            axis=0).astype(BF16)

    def unpack(block):
        count = block.shape[0] // 2
        block = block.astype(F32)
        return block[:count, :128] + block[:count, 128:] + block[count:, :128]

    def finish(terms, left, *order):
        for bit in left:
            terms, sent = cut(terms)
            terms = terms + [whole(after(across(total(sent[0]).astype(BF16), bit), *order))]
        return total(terms)

    outer_near_got = after(outer_near_got, grad_attn)
    inner_near_got = after(inner_near_got, grad_attn)
    outer_near = outer_near + [whole(outer_near_got)]
    out_got_far = across(after(out_send_far, outer_near_got, inner_near_got), 1)
    in_got_far = across(after(in_send_far, outer_near_got, inner_near_got), 1)
    inner_near, sent_near = cut(inner_near + [whole(inner_near_got)])
    (inner_near_sent,) = add_up(sent_near[0])
    out_got_far = after(out_got_far, inner_near_sent)
    outer_far, sent = cut([whole(out_keep_far), whole(out_got_far)])
    inner_far, sent_in = cut([whole(in_keep_far), whole(in_got_far)])
    outer_far_sent, inner_far_sent = add_up(sent[0], sent_in[0])
    outer_far_got = across(outer_far_sent, 2)
    inner_far_got = across(inner_far_sent, bits_in[0])
    inner_near_got = across(inner_near_sent, bits_in[1])
    d_far, ag_send_far, ag_keep_far, table_part_far, gain_part_far = attn_back(
        attn_pieces, q_far, k_far, v_far, lse_far, ctx_far, table_far,
        [outer_far_sent, inner_far_sent, inner_near_sent], "attn_back_far",
    )
    outer_far_got = after(outer_far_got, d_far)
    inner_far_got = after(inner_far_got, d_far)
    inner_near_got = after(inner_near_got, d_far)
    ag_got_far = across(after(ag_send_far, outer_far_got, inner_far_got, inner_near_got), 1)
    outer_far = outer_far + [whole(outer_far_got)]
    inner_near = inner_near + [whole(inner_near_got)]
    inner_far, sent_in = cut(inner_far + [whole(inner_far_got)])
    outer_far_x, inner_far_sent = add_up(outer_far, sent_in[0])
    outer_x_got = beside(outer_far_x)
    inner_far_got = across(inner_far_sent, bits_in[1])
    attn_far, sent = cut([whole(ag_keep_far), whole(ag_got_far)])
    (attn_far_sent,) = add_up(sent[0])
    attn_far_got = across(attn_far_sent, 2)
    order = [outer_far_x, inner_far_sent, attn_far_sent]
    d_near, ag_send_near, vectors_own, ag_keep_near, _, _ = attn_back(
        [w_query, w_key, w_value, w_output], q_near, k_near, v_near, lse_near, ctx_near, table, order,
        "attn_back_near", (gain_two_part, gain_part_far, table_part_far),
    )
    attn_far_got = after(attn_far_got, d_near)
    inner_far_got = after(inner_far_got, d_near)
    outer_x_got = after(outer_x_got, d_near)
    ag_got_near = across(after(ag_send_near, attn_far_got, inner_far_got, outer_x_got), 1)
    table_at = 2 * small_rows
    vectors = vectors_own + unpack(ag_got_near[: 8 * small_rows, 4 * cols :])
    same = vectors + across(vectors, 2)
    other = beside(vectors) + across_beside(vectors, 2)
    small = jnp.concatenate(
        [same[:table_at] + other[:table_at], same[table_at : table_at + 8] + other[table_at + 8 :]], axis=0)
    block = pack(small)
    outer, sent = cut(outer_near + [whole(outer_x_got)], 2 ** len(upper[:2]))
    outer_sent = [jnp.concatenate([v, block], axis=1) for v in add_up(*sent)]
    outer_got = [across(v, d) for v, d in zip(outer_sent, distances(upper[:2]), strict=True)]
    far_x = jnp.concatenate(
        [total(attn_far + [whole(attn_far_got)]), total(inner_far + [whole(inner_far_got)])], axis=0).astype(BF16)
    far_x_got = beside(after(far_x, same, other))
    attn_near, sent = cut([whole(ag_keep_near), whole(ag_got_near[:, : 4 * cols])])
    (attn_near_sent,) = add_up(sent[0])
    attn_near_got = across(attn_near_sent, 2)
    order = [far_x, attn_near_sent] + outer_sent
    (grad_input,) = call(
        functools.partial(input_back_kernel, info=info), (passages,),
        [(after(numbers, *order), smem),
         (inputs, by_passage(width)), (gains, gain_spec), (grad_residual, by_passage(width)),
         (d_near, by_passage(3 * cols)), (d_far, by_passage(3 * cols)),
         (w_query, weight_spec), (w_key, weight_spec), (w_value, weight_spec)]
        + [(a, anywhere) for a in attn_pieces],
        [((rows_n, width), F32, by_passage(width))],
        qkv_scratch + [dma], 12 * rows_n * width * cols, "input_back",
    )
    far_x_got = after(far_x_got, grad_input)
    rows = attn_near_sent.shape[0]
    attn_near_got = after(attn_near_got, grad_input, far_x_got, *outer_got)
    attn, sent = cut(attn_near + [whole(attn_near_got), whole(far_x_got[:rows])], 2 ** len(upper[:2]))
    attn_sent = add_up(*sent)
    attn_got = [across(v, d) for v, d in zip(attn_sent, distances(upper[:2]), strict=True)]
    inner = inner_near + [whole(after(far_x_got, *attn_sent)[rows:])]
    grad_inner = finish(inner, bits_in[2:])
    outer_got = [after(got, *attn_sent) for got in outer_got]
    outer = outer + [whole(got[:, :hidden]) for got in outer_got]
    small = small + unpack(sum(got[:, hidden:].astype(F32) for got in outer_got))
    for bit in upper[2:]:
        small = small + across(small, bit)
    grad_outer = finish(outer, upper[2:]).T
    attn_grads = finish(attn + [whole(after(got, grad_inner, grad_outer)) for got in attn_got], upper[2:])
    grad_query, grad_key, grad_value = (attn_grads[:, n * cols : (n + 1) * cols] for n in range(3))
    grad_output = attn_grads[:, 3 * cols :].T

    grad_gain_one = small[: width // 128].reshape(width)
    grad_gain_two = small[small_rows : small_rows + width // 128].reshape(width)
    grad_table = small[table_at : table_at + heads, :BUCKETS].T
    return (
        layer_out, grad_input, grad_gain_one, grad_query, grad_key, grad_value, grad_output,
        grad_table, grad_gain_two, grad_inner, grad_outer,
    )


def solution(mesh):
    both = ("dp", "tensor")
    in_specs = (
        P(both, None), P(), P(None, "tensor"), P(None, "tensor"), P(None, "tensor"), P("tensor", None),
        P(None, "tensor"), P(), P(None, "tensor"), P("tensor", None), P("dp"), P(both, None),
    )
    out_specs = (
        P(both, None), P(both, None), P(), P("dp", "tensor"), P("dp", "tensor"), P("dp", "tensor"),
        P("tensor", "dp"), P(None, "tensor"), P(), P("dp", "tensor"), P("tensor", "dp"),
    )
    body = functools.partial(shards, dp=mesh.shape["dp"], tp=mesh.shape["tensor"])
    return jax.shard_map(body, mesh=mesh, in_specs=in_specs, out_specs=out_specs, check_vma=False)
```

```python
import functools

import jax
import jax.numpy as jnp
from jax import lax
from jax.experimental import pallas as pl
from jax.experimental.pallas import tpu as pltpu
from jax.sharding import PartitionSpec as P

HEAD_DIM = 64
BUCKETS = 32
EPS = 1e-6
MASKED = -1e9
GELU_C = 0.7978845608028654
VMEM_BYTES = 60 * 1024 * 1024
F32 = jnp.float32
BF16 = jnp.bfloat16


def dot(left, right):
    return lax.dot_general(left, right, (((1,), (0,)), ((), ())), preferred_element_type=F32)


def dot_t(left, right):
    return lax.dot_general(left, right, (((1,), (1,)), ((), ())), preferred_element_type=F32)


def dot_l(left, right):
    return lax.dot_general(left, right, (((0,), (0,)), ((), ())), preferred_element_type=F32)


def staggered(count, first, second, third):
    for n in range(count + 2):
        if n < count:
            first(n)
        if 0 <= n - 1 < count:
            second(n - 1)
        if 0 <= n - 2 < count:
            third(n - 2)


def bucket_of(offsets):
    distance = jnp.abs(offsets)
    far = jnp.full_like(distance, 8)
    for power in range(1, 8):
        far = far + (distance * distance >= 64 * 2**power).astype(jnp.int32)
    near = jnp.where(distance < 8, distance, far)
    return near + jnp.where(offsets > 0, 16, 0)


def bucket_indicator(seq, count=BUCKETS):
    lane = lax.broadcasted_iota(jnp.int32, (count, 2 * seq), 1)
    offsets = jnp.where(lane < seq, -lane, 2 * seq - lane)
    ids = lax.broadcasted_iota(jnp.int32, (count, 2 * seq), 0)
    return (bucket_of(offsets) == ids).astype(F32)


def fill_bias(table_ref, bias_ref):
    heads, seq, _ = bias_ref.shape
    base = dot(table_ref[:, :BUCKETS], bucket_indicator(seq).astype(BF16))
    for h in range(heads):
        wide = jnp.broadcast_to(base[h : h + 1, :], (seq, 2 * seq))
        bias_ref[h] = pltpu.roll(wide, 0, 1, stride=1, stride_axis=0)[:, :seq]


def head_mask(columns, parity):
    lane = lax.broadcasted_iota(jnp.int32, columns.shape, 1)
    keep = (lane < HEAD_DIM) if parity == 0 else (lane >= HEAD_DIM)
    return jnp.where(keep, columns, jnp.zeros_like(columns))


def rms_rows(values, gain):
    return values * lax.rsqrt(jnp.mean(values * values, axis=-1, keepdims=True) + EPS) * gain


def add_row(ref, row):
    for n in range(row.shape[1] // 128):
        ref[n : n + 1, :] += row[:, n * 128 : (n + 1) * 128]


def rms_back(values, gain, grads):
    scale = lax.rsqrt(jnp.mean(values * values, axis=-1, keepdims=True) + EPS)
    scaled = grads * gain
    mean = jnp.mean(scaled * values, axis=-1, keepdims=True)
    back = scale * scaled - values * (scale * scale * scale * mean)
    return back, jnp.sum(grads * values * scale, axis=0, keepdims=True)


def fill_perm(perm_ref, me, dp, bits):
    width = perm_ref.shape[0]
    block = width // dp
    index = lax.broadcasted_iota(jnp.int32, (width, 128), 0)
    rel = lax.div(index, block)
    target = jnp.zeros_like(rel)
    for n, bit in enumerate(bits):
        target = target + ((rel >> (len(bits) - 1 - n)) & 1) * bit
    source = (target ^ me) * block + (index - rel * block)
    lane = lax.broadcasted_iota(jnp.int32, (width, 128), 1)
    for n in range(0, width, 128):
        perm_ref[:, n : n + 128] = jnp.where(source == lane + n, 1.0, 0.0).astype(BF16)


def piece_copies(packets, quarter, sem, routes):
    copies = []
    for pieces, ways in zip(packets, routes, strict=True):
        for n, piece in enumerate(pieces):
            for rows, cols, target, count, at in ways:
                start = pl.multiple_of((quarter ^ n) * count, 16)
                copies.append((piece.at[rows, cols], target.at[pl.ds(start, count), at], sem))
    return copies


def start_all(copies):
    for copy in copies:
        pltpu.make_async_copy(*copy).start()


def wait_all(copies):
    for copy in copies:
        pltpu.make_async_copy(*copy).wait()


def gather_pieces(packets, quarter, sem, routes):
    copies = piece_copies(packets, quarter, sem, routes)
    start_all(copies)
    wait_all(copies)


class Heads:
    def __init__(self, seq, heads, lengths, bias_ref, q_ref, k_ref, v_ref, ctx_ref, lse_ref):
        self.seq, self.heads, self.lengths = seq, heads, lengths
        self.bias_ref, self.lse_ref = bias_ref, lse_ref
        self.q_ref, self.k_ref, self.v_ref, self.ctx_ref = q_ref, k_ref, v_ref, ctx_ref
        self.first_head = lax.broadcasted_iota(jnp.int32, (seq, 2 * HEAD_DIM), 1) < HEAD_DIM
        self.key_slot = lax.broadcasted_iota(jnp.int32, (seq, 1), 0)
        self.query_t, self.logits, self.probs, self.parts = {}, {}, {}, {}

    def rows_of(self, p):
        return slice(p * self.seq, (p + 1) * self.seq)

    def pair_of(self, h):
        lo = (h // 2) * 2 * HEAD_DIM
        return slice(lo, lo + 2 * HEAD_DIM)

    def project(self, p, rows, wq_ref, wk_ref, wv_ref):
        query = dot(rows, wq_ref[...]).astype(BF16)
        self.q_ref[self.rows_of(p), :] = query
        self.k_ref[self.rows_of(p), :] = dot(rows, wk_ref[...]).astype(BF16)
        self.v_ref[self.rows_of(p), :] = dot(rows, wv_ref[...]).astype(BF16)
        self.query_t[p] = query.T

    def score(self, n):
        p, h = divmod(n, self.heads)
        both = self.pair_of(h)
        keys = head_mask(self.k_ref[self.rows_of(p), both], h % 2)
        self.logits[n] = dot(keys, self.query_t[p][both, :])

    def normalise(self, n):
        p, h = divmod(n, self.heads)
        valid = self.key_slot < self.lengths[p]
        biased = jnp.where(valid, self.logits.pop(n) + self.bias_ref[h], MASKED)
        peak = jnp.max(biased, axis=0, keepdims=True)
        terms = jnp.exp(biased - peak)
        total = jnp.sum(terms, axis=0, keepdims=True)
        self.probs[n] = (terms * (1.0 / total)).astype(BF16)
        self.lse_ref[p, h : h + 1, :] = peak + jnp.log(total)

    def combine(self, n):
        p, h = divmod(n, self.heads)
        self.parts[n] = dot_l(self.probs.pop(n), self.v_ref[self.rows_of(p), self.pair_of(h)])
        if h % 2:
            both = jnp.where(self.first_head, self.parts.pop(n - 1), self.parts.pop(n))
            self.ctx_ref[self.rows_of(p), self.pair_of(h)] = both.astype(BF16)


def attn_first_kernel(
    len_ref, x_ref, gain_ref, wq_ref, wk_ref, wv_ref, table_ref,
    rows_ref, q_ref, k_ref, v_ref, ctx_ref, lse_ref, bias_ref, *, info,
):
    p = pl.program_id(0)
    seq = rows_ref.shape[0]

    @pl.when(p == 0)
    def _():
        fill_bias(table_ref, bias_ref)

    rows = rms_rows(x_ref[...].astype(F32), gain_ref[0:1, :].astype(F32)).astype(BF16)
    rows_ref[...] = rows
    lengths = [len_ref[len_ref[info + 1] + p]]
    work = Heads(seq, bias_ref.shape[0], lengths, bias_ref, q_ref, k_ref, v_ref, ctx_ref, lse_ref)
    work.project(0, rows, wq_ref, wk_ref, wv_ref)
    staggered(work.heads, work.score, work.normalise, work.combine)


def turn_kernel(
    len_ref, rows_ref, cot_ref, rows_t_ref, cot_t_ref, perm_ref, perm_in_ref, *, dp, info, orders,
):
    @pl.when(pl.program_id(0) == 0)
    def _():
        fill_perm(perm_ref, len_ref[info], dp, orders[0])
        fill_perm(perm_in_ref, len_ref[info], dp, orders[1])

    rows_t_ref[...] = dot_t(perm_ref[...], rows_ref[...]).astype(BF16)
    cot_t_ref[...] = dot_t(perm_ref[...], cot_ref[...]).astype(BF16)


def projection_routes(piece_rows, cols, targets):
    rows = slice(0, piece_rows)
    return [
        (rows, slice(n * cols, (n + 1) * cols), target, piece_rows, slice(0, cols))
        for n, target in enumerate(targets)
    ]


def output_routes(piece_rows, cols, target):
    half, lanes = piece_rows // 2, slice(cols, 2 * cols)
    return [
        (slice(0, half), lanes, target, half, slice(0, cols)),
        (slice(half, piece_rows), lanes, target, half, slice(cols, 2 * cols)),
    ]


def attn_second_kernel(len_ref, gain_ref, rows_hbm, x_hbm, ctx_first_hbm, perm_hbm, *refs, seq, info):
    qk_pieces, vo_pieces = refs[:4], refs[4:8]
    (
        wo_first_hbm, q_hbm, k_hbm, v_hbm, ctx_hbm, lse_ref, resid_hbm, rows_two_hbm, rows_two_t_hbm, table_ref,
        bias_ref, wq_ref, wk_ref, wv_ref, wo_ref, wo_first_ref, rows_ref, x_ref, ctx_first_ref, perm_ref,
        q_ref, k_ref, v_ref, ctx_ref, resid_ref, rows_two_ref, rows_two_t_ref, piece_sem, in_sems, out_sems,
    ) = refs[8:]
    rows, cols = wq_ref.shape[0] // 4, wq_ref.shape[1]
    heads = bias_ref.shape[0]
    passages = q_ref.shape[0] // seq
    quarter = len_ref[info] & 3
    get_table = [(qk_pieces[0].at[rows : rows + 16, :128], table_ref, in_sems.at[0])]
    projections = piece_copies(
        (qk_pieces, vo_pieces), quarter, piece_sem.at[0],
        [projection_routes(rows, cols, (wq_ref, wk_ref)), projection_routes(rows, cols, (wv_ref,))],
    )
    get_rows = [(rows_hbm, rows_ref, in_sems.at[1])]
    output = piece_copies((vo_pieces,), quarter, piece_sem.at[1], [output_routes(rows, cols, wo_ref)])
    output += [
        (wo_first_hbm, wo_first_ref, in_sems.at[2]), (ctx_first_hbm, ctx_first_ref, in_sems.at[3]),
        (x_hbm, x_ref, in_sems.at[4]), (perm_hbm, perm_ref, in_sems.at[5]),
    ]
    start_all(get_table + get_rows + projections + output)
    wait_all(get_table)
    fill_bias(table_ref, bias_ref)
    wait_all(get_rows + projections)
    lengths = [len_ref[len_ref[info + 1] + p] for p in range(passages)]
    work = Heads(seq, heads, lengths, bias_ref, q_ref, k_ref, v_ref, ctx_ref, lse_ref)
    out = []

    def put(ref, hbm, at, sem):
        copy = (ref.at[at], hbm.at[at], out_sems.at[sem])
        out.append(copy)
        start_all([copy])

    def project(p):
        here = work.rows_of(p)
        work.project(p, rows_ref[here, :], wq_ref, wk_ref, wv_ref)
        for n, (ref, hbm) in enumerate(((q_ref, q_hbm), (k_ref, k_hbm), (v_ref, v_hbm))):
            put(ref, hbm, (here, slice(None)), 7 * p + n)

    def branch(p):
        here = work.rows_of(p)
        if p == 0:
            wait_all(output)
        total = dot(ctx_first_ref[here, :], wo_first_ref[...]) + dot(ctx_ref[here, :], wo_ref[...])
        residual = x_ref[here, :].astype(F32) + total
        resid_ref[here, :] = residual
        rows_two_ref[here, :] = rms_rows(residual, gain_ref[1:2, :].astype(F32)).astype(BF16)
        pairs = ((ctx_ref, ctx_hbm), (resid_ref, resid_hbm), (rows_two_ref, rows_two_hbm))
        for n, (ref, hbm) in enumerate(pairs):
            put(ref, hbm, (here, slice(None)), 7 * p + 3 + n)

    def turn(p):
        here = work.rows_of(p)
        rows_two_t_ref[:, here] = dot_t(perm_ref[...], rows_two_ref[here, :]).astype(BF16)
        put(rows_two_t_ref, rows_two_t_hbm, (slice(None), here), 7 * p + 6)

    for p in range(passages):
        project(p)
    count = passages * heads
    for n in range(count + 2):
        if n < count:
            work.score(n)
        if 0 <= n - 1 < count:
            work.normalise(n - 1)
        if 0 <= n - 2 < count:
            work.combine(n - 2)
        done = (n - 2) // heads
    for p in range(passages):
        branch(p)
    for p in range(passages):
        turn(p)
    wait_all(out)


class Hidden:
    def __init__(self, refs, weight_refs, weight_hbms, sems, chunk, block):
        (
            self.rows_ref, self.cot_ref, self.wi_ref, self.wo_ref, self.rows_t_ref, self.cot_t_ref, self.ffn_ref,
            self.back_ref, self.act_ref, self.grad_ref,
        ) = refs
        self.weight_refs, self.weight_hbms, self.sems = weight_refs, weight_hbms, sems
        self.chunk, self.block = chunk, block
        self.chunks = self.rows_ref.shape[0] // chunk
        self.blocks = self.wi_ref.shape[1] // block
        self.out = []

    def rows_of(self, i):
        return slice(i * self.chunk, (i + 1) * self.chunk)

    def hidden(self, b, ready):
        units = slice(b * self.block, (b + 1) * self.block)

        def first(i):
            at = self.rows_of(i)
            ready(b, i, 0)
            v = dot(self.rows_ref[at, :], self.wi_ref[:, units])
            ready(b, i, 1)
            grad_act = dot_t(self.cot_ref[at, :], self.wo_ref[units, :])
            square = v * v
            tanh = jnp.tanh(GELU_C * v * (1.0 + 0.044715 * square))
            half = 0.5 + 0.5 * tanh
            self.act_ref[at, units] = (v * half).astype(BF16)
            slope = half + (0.5 * GELU_C) * v * (1.0 - tanh * tanh) * (1.0 + 0.134145 * square)
            self.grad_ref[at, units] = (grad_act * slope).astype(BF16)

        def second(i):
            at = self.rows_of(i)
            forward = dot(self.act_ref[at, units], self.wo_ref[units, :])
            backward = dot_t(self.grad_ref[at, units], self.wi_ref[:, units])
            if b:
                self.ffn_ref[at, :] += forward
                self.back_ref[at, :] += backward
            else:
                self.ffn_ref[at, :] = forward
                self.back_ref[at, :] = backward

        staggered(self.chunks, first, second, lambda i: None)

    def weights(self, b, which):
        units = slice(b * self.block, (b + 1) * self.block)
        ref = self.weight_refs[which]
        half_rows = ref.shape[0]
        at = slice(half_rows, None) if which < 2 else slice(half_rows)
        left, right = ((self.rows_t_ref, self.grad_ref), (self.cot_t_ref, self.act_ref))[which % 2]
        ref[:, units] = dot(left[at, :], right[:, units]).astype(BF16)
        self.put(ref, self.weight_hbms[which], (slice(None), units))

    def put(self, ref, hbm, at):
        self.out.append((ref.at[at], hbm.at[at], self.sems.at[len(self.out)]))
        start_all(self.out[-1:])


def ffn_first_kernel(rows_hbm, cot_hbm, wi_hbm, wo_hbm, rows_t_hbm, cot_t_hbm, ffn_hbm, back_hbm, *refs, chunk, block):
    weight_hbms, work_refs, weight_refs, in_sems, out_sems = refs[:4], refs[4:14], refs[14:18], refs[18], refs[19]
    work = Hidden(work_refs, weight_refs, weight_hbms, out_sems, chunk, block)
    copies = {}

    def get(key, hbm, ref, at):
        copies[key] = [(hbm.at[at], ref.at[at], in_sems.at[len(copies)])]
        start_all(copies[key])

    everything = slice(None)

    def get_weights(b):
        units = slice(b * block, (b + 1) * block)
        get(("weight", b, 0), wi_hbm, work.wi_ref, (everything, units))
        get(("weight", b, 1), wo_hbm, work.wo_ref, (units, everything))

    def get_rows(i):
        get(("rows", i, 0), rows_hbm, work.rows_ref, (work.rows_of(i), everything))
        get(("rows", i, 1), cot_hbm, work.cot_ref, (work.rows_of(i), everything))

    def ready(b, i, which):
        if i == 0:
            wait_all(copies["weight", b, which])
        if b == 0:
            wait_all(copies["rows", i, which])
        if b == 0 and i == 0 and which == 1:
            for n in range(1, work.blocks):
                get_weights(n)
            get("turned rows", rows_t_hbm, work.rows_t_ref, (everything, everything))
            get("turned cot", cot_t_hbm, work.cot_t_ref, (everything, everything))

    get_rows(0)
    get_weights(0)
    for i in range(1, work.chunks):
        get_rows(i)
    for b in range(work.blocks):
        work.hidden(b, ready)
        if b == 0:
            wait_all(copies["turned rows"] + copies["turned cot"])
        if b == work.blocks - 1:
            work.put(work.ffn_ref, ffn_hbm, (everything, everything))
            work.put(work.back_ref, back_hbm, (everything, everything))
        for which in range(4):
            work.weights(b, which)
    wait_all(work.out)


def ffn_second_kernel(
    info_ref, gain_ref, rows_hbm, cot_hbm, rows_t_hbm, cot_t_hbm, *refs, chunk, late_chunk, block, info,
):
    inner_pieces, outer_pieces = refs[:4], refs[4:8]
    (
        ffn_in_hbm, back_in_hbm, resid_hbm, perm_hbm,
        layer_hbm, grad_resid_hbm, grad_attn_hbm, grad_attn_t_hbm, gain_grad_ref,
    ) = refs[8:17]
    weight_hbms, work_refs, weight_refs = refs[17:21], refs[21:31], refs[31:35]
    (
        ffn_in_ref, back_in_ref, resid_ref, perm_ref, layer_ref, grad_resid_ref, grad_attn_ref, grad_attn_t_ref,
        piece_sems, in_sems, out_sems,
    ) = refs[35:]
    work = Hidden(work_refs, weight_refs, weight_hbms, out_sems, chunk, block)
    width, hidden = work.wi_ref.shape
    wi_rows, wo_rows = width // 4, hidden // 4
    quarter = info_ref[info] & 3
    everything = slice(None)
    inner = [
        piece_copies(
            (inner_pieces,), quarter, piece_sems.at[b],
            [[(slice(0, wi_rows), slice(b * block, (b + 1) * block), work.wi_ref, wi_rows,
               slice(b * block, (b + 1) * block))]],
        )
        for b in range(work.blocks)
    ]
    outer = piece_copies(
        (outer_pieces,), quarter, piece_sems.at[work.blocks],
        [[(slice(0, wo_rows), slice(0, width), work.wo_ref, wo_rows, slice(0, width))]],
    )
    rows_in = []
    for i in range(work.chunks):
        at = (work.rows_of(i), everything)
        rows_in.append([
            (rows_hbm.at[at], work.rows_ref.at[at], in_sems.at[2 * i]),
            (cot_hbm.at[at], work.cot_ref.at[at], in_sems.at[2 * i + 1]),
        ])
    base = 2 * work.chunks
    turned = [(rows_t_hbm, work.rows_t_ref, in_sems.at[base]), (cot_t_hbm, work.cot_t_ref, in_sems.at[base + 1])]
    late = [
        (back_in_hbm, back_in_ref, in_sems.at[base + 2]), (resid_hbm, resid_ref, in_sems.at[base + 3]),
        (ffn_in_hbm, ffn_in_ref, in_sems.at[base + 4]), (perm_hbm, perm_ref, in_sems.at[base + 5]),
    ]

    def ready(b, i, which):
        if i == 0 and which == 0:
            wait_all(inner[b])
        if i == 0 and b == 0 and which == 1:
            wait_all(outer)
        if b == 0:
            wait_all(rows_in[i][which : which + 1])
        if b == 0 and i == 0 and which == 1:
            for n in range(1, work.blocks):
                start_all(inner[n])
            start_all(turned)

    start_all(rows_in[0][:1] + inner[0] + rows_in[0][1:] + outer)
    for i in range(1, work.chunks):
        start_all(rows_in[i])
    last = work.blocks - 1
    for b in range(work.blocks):
        if b == last:
            start_all(late)
        work.hidden(b, ready)
        if b == 0:
            wait_all(turned)
        if b < last:
            for which in range(4):
                work.weights(b, which)
    wait_all(late)
    gain_grad_ref[...] = jnp.zeros_like(gain_grad_ref)
    count = resid_ref.shape[0] // late_chunk
    for i in range(count):
        at = slice(i * late_chunk, (i + 1) * late_chunk)
        residual = resid_ref[at, :]
        back, gain_part = rms_back(residual, gain_ref[1:2, :].astype(F32), work.back_ref[at, :] + back_in_ref[at, :])
        add_row(gain_grad_ref, gain_part)
        grad_resid = work.cot_ref[at, :].astype(F32) + back
        grad_resid_ref[at, :] = grad_resid
        grad_attn_ref[at, :] = grad_resid.astype(BF16)
        layer_ref[at, :] = (residual + (work.ffn_ref[at, :] + ffn_in_ref[at, :])).astype(BF16)
        if i < 3:
            work.weights(last, i)
        for ref, hbm in ((grad_attn_ref, grad_attn_hbm), (grad_resid_ref, grad_resid_hbm), (layer_ref, layer_hbm)):
            work.put(ref, hbm, (at, everything))
    grad_attn_t_ref[...] = dot_t(perm_ref[...], grad_attn_ref[...]).astype(BF16)
    work.put(grad_attn_t_ref, grad_attn_t_hbm, (everything, everything))
    for which in range(min(count, 3), 4):
        work.weights(last, which)
    wait_all(work.out)


def gain_from_weights(me, bits, w_refs, grads, perm_ref, gain_ref, out_ref):
    width, cols = w_refs[0].shape
    block = width // (2 ** len(bits))
    if block % 16:
        weights = [dot(perm_ref[...], ref[...]) for ref in w_refs]
    else:
        weights = []
        for ref in w_refs:
            rows = []
            for n in range(width // block):
                target = sum(bit for m, bit in enumerate(bits) if (n >> (len(bits) - 1 - m)) & 1)
                rows.append(ref[pl.ds(pl.multiple_of((me ^ target) * block, 16), block), :])
            weights.append(jnp.concatenate(rows, axis=0).astype(F32))
    folded = None
    for n, weight in enumerate(weights):
        for lo in range(0, cols, 128):
            term = weight[:, lo : lo + 128] * grads[:, n * cols + lo : n * cols + lo + 128]
            folded = term if folded is None else folded + term
    ordered = jnp.sum(folded.T, axis=0, keepdims=True)
    high = ordered.astype(BF16)
    middle = (ordered - high.astype(F32)).astype(BF16)
    low = (ordered - high.astype(F32) - middle.astype(F32)).astype(BF16)
    parts = jnp.concatenate([high, middle, low, jnp.zeros((13, width), BF16)], axis=0)
    natural = jnp.sum(dot(parts, perm_ref[...]), axis=0, keepdims=True) / gain_ref[0:1, :].astype(F32)
    out_ref[...] = jnp.zeros_like(out_ref)
    add_row(out_ref, natural)


def attn_back_kernel(len_ref, *refs, seq, info, bits, far):
    if far:
        qk_pieces, vo_pieces, refs = refs[:4], refs[4:8], refs[8:]
    else:
        weights_hbm, vector_refs, own_ref, block_ref = refs[:4], refs[4:7], refs[20], refs[-1]
        refs = refs[7:20] + refs[21:-1]
    (
        grad_attn_hbm, q_hbm, k_hbm, v_hbm, lse_ref, table_ref, rows_t_hbm, grad_attn_t_hbm, ctx_hbm, perm_hbm,
        gain_ref, dqkv_hbm, send_hbm, keep_hbm, table_grad_ref, gain_grad_ref,
        wq_ref, wk_ref, wv_ref, wo_ref, grad_attn_ref, q_ref, k_ref, v_ref, rows_t_ref, grad_attn_t_ref, ctx_ref,
        perm_ref, dqkv_ref, send_ref, keep_ref, bias_ref, sums_ref, grads_ref, piece_sem, in_sems, out_sems,
    ) = refs
    heads = bias_ref.shape[0]
    cols = heads * HEAD_DIM
    passages = q_ref.shape[0] // seq
    half_rows = keep_ref.shape[0]

    def rows_of(p):
        return slice(p * seq, (p + 1) * seq)

    if far:
        rows = wq_ref.shape[0] // 4
        quarter = len_ref[info] & 3
        late_weights = piece_copies(
            (qk_pieces, vo_pieces), quarter, piece_sem.at[0],
            [projection_routes(rows, cols, (wq_ref, wk_ref)), projection_routes(rows, cols, (wv_ref,))],
        )
        output = piece_copies((vo_pieces,), quarter, piece_sem.at[1], [output_routes(rows, cols, wo_ref)])
    else:
        late_weights = [
            (hbm, ref, piece_sem.at[n])
            for n, (hbm, ref) in enumerate(zip(weights_hbm, (wq_ref, wk_ref, wv_ref), strict=False))
        ]
        output = [(weights_hbm[3], wo_ref, piece_sem.at[3])]
    start_all(output)
    by_passage = []
    for p in range(passages):
        pairs = ((grad_attn_hbm, grad_attn_ref), (q_hbm, q_ref), (k_hbm, k_ref), (v_hbm, v_ref))
        by_passage.append(
            [(hbm.at[rows_of(p), :], ref.at[rows_of(p), :], in_sems.at[4 * p + n]) for n, (hbm, ref) in enumerate(pairs)]
        )
    start_all(by_passage[0])
    at = 4 * passages
    turned = [(ctx_hbm, ctx_ref, in_sems.at[at]), (grad_attn_t_hbm, grad_attn_t_ref, in_sems.at[at + 1])]
    last = [(rows_t_hbm, rows_t_ref, in_sems.at[at + 2]), (perm_hbm, perm_ref, in_sems.at[at + 3])]
    fill_bias(table_ref, bias_ref)
    sums_ref[...] = jnp.zeros_like(sums_ref)
    wait_all(output)
    first_head = lax.broadcasted_iota(jnp.int32, (seq, 2 * HEAD_DIM), 1) < HEAD_DIM
    key_slot = lax.broadcasted_iota(jnp.int32, (seq, 1), 0)
    ready, scores, weights, dq, dk, dv = {}, {}, {}, {}, {}, {}

    def pair_of(h, offset=0):
        lo = (h // 2) * 2 * HEAD_DIM + offset
        return slice(lo, lo + 2 * HEAD_DIM)

    def prepare(p):
        wait_all(by_passage[p])
        grad_ctx = dot_t(grad_attn_ref[rows_of(p), :], wo_ref[...]).astype(BF16)
        valid = key_slot < len_ref[len_ref[info + 1] + p]
        ready[p] = (
            grad_ctx, grad_ctx.T, q_ref[rows_of(p), :].T, k_ref[rows_of(p), :].T, valid,
        )

    def score(n):
        p, h = divmod(n, heads)
        _, grad_ctx_t, query_t, _, _ = ready[p]
        both = pair_of(h)
        scores[n] = (
            dot(head_mask(k_ref[rows_of(p), both], h % 2), query_t[both, :]),
            dot(head_mask(v_ref[rows_of(p), both], h % 2), grad_ctx_t[both, :]),
        )

    def soften(n):
        p, h = divmod(n, heads)
        logits, grad_probs = scores.pop(n)
        probs = jnp.exp(logits + bias_ref[h] - lse_ref[p, h : h + 1, :])
        probs = jnp.where(ready[p][4], probs, 0.0)
        mixed = jnp.sum(probs * grad_probs, axis=0, keepdims=True)
        grads = (probs * (grad_probs - mixed)).astype(BF16)
        sums_ref[h] += grads.astype(F32)
        weights[n] = (probs.astype(BF16), grads)

    def combine(n):
        p, h = divmod(n, heads)
        grad_ctx, _, _, keys_t, _ = ready[p]
        probs, grads = weights.pop(n)
        dq[n] = dot(keys_t[h * HEAD_DIM : (h + 1) * HEAD_DIM, :], grads)
        dk[n] = dot(grads, q_ref[rows_of(p), pair_of(h)])
        dv[n] = dot(probs, grad_ctx[:, pair_of(h)])
        if h % 2:
            dqkv_ref[rows_of(p), pair_of(h, cols)] = jnp.where(first_head, dk.pop(n - 1), dk.pop(n)).astype(BF16)
            dqkv_ref[rows_of(p), pair_of(h, 2 * cols)] = jnp.where(first_head, dv.pop(n - 1), dv.pop(n)).astype(BF16)
        if h == heads - 1:
            parts = jnp.concatenate([dq.pop(m) for m in range(n - h, n + 1)], axis=0)
            dqkv_ref[rows_of(p), :cols] = parts.astype(BF16).T
            copy = (dqkv_ref.at[rows_of(p), :], dqkv_hbm.at[rows_of(p), :], out_sems.at[p])
            out.append(copy)
            start_all([copy])

    out = []
    count = passages * heads
    for p in range(1, passages):
        start_all(by_passage[p])
    start_all(turned)
    for p in range(passages):
        prepare(p)
    for n in range(count + 2):
        if n == heads:
            start_all(last + late_weights)
        if n < count:
            score(n)
        if 0 <= n - 1 < count:
            soften(n - 1)
        if 0 <= n - 2 < count:
            combine(n - 2)
        if n == heads:
            wait_all(turned)
            send_ref[:, 3 * cols :] = dot(grad_attn_t_ref[half_rows:, :], ctx_ref[...]).astype(BF16)
        if n == heads + 2:
            keep_ref[:, 3 * cols :] = dot(grad_attn_t_ref[:half_rows, :], ctx_ref[...]).astype(BF16)
    wait_all(last)
    for ref, hbm, at, sem in (
        (send_ref, send_hbm, slice(half_rows, None), passages), (keep_ref, keep_hbm, slice(half_rows), passages + 1),
    ):
        grads_ref[at, :] = dot(rows_t_ref[at, :], dqkv_ref[...])
        ref[:, : 3 * cols] = grads_ref[at, :].astype(BF16)
        copy = (ref, hbm.at[:, : 4 * cols], out_sems.at[sem])
        out.append(copy)
        start_all([copy])
    wait_all(late_weights)
    gain_from_weights(
        len_ref[info], bits, (wq_ref, wk_ref, wv_ref), grads_ref, perm_ref, gain_ref, gain_grad_ref
    )
    rows = []
    for h in range(heads):
        folded = jnp.zeros((8, 2 * seq), F32)
        for a in range(0, seq, 8):
            wide = jnp.concatenate([sums_ref[h, a : a + 8, :], jnp.zeros((8, seq), F32)], axis=1)
            folded = folded + (pltpu.roll(wide, 2 * seq - a, 1) if a else wide)
        diagonals = folded[0:1, :]
        for b in range(1, 8):
            diagonals = diagonals + pltpu.roll(folded[b : b + 1, :], 2 * seq - b, 1)
        rows.append(diagonals)
    rows.append(jnp.zeros((8 - heads, 2 * seq), F32))
    table_grad_ref[...] = lax.dot_general(
        jnp.concatenate(rows, axis=0), bucket_indicator(seq, 128), (((1,), (1,)), ((), ())),
        precision=lax.Precision.HIGHEST, preferred_element_type=F32,
    )
    if not far:
        gain_two_ref, gain_far_ref, table_far_ref = vector_refs
        own = jnp.concatenate(
            [gain_grad_ref[...] + gain_far_ref[...], gain_two_ref[...], table_grad_ref[...], table_far_ref[...]], axis=0)
        own_ref[...] = own
        high = own.astype(BF16)
        middle = (own - high.astype(F32)).astype(BF16)
        block_ref[...] = jnp.concatenate([high, middle], axis=1)
        rows, lanes = block_ref.shape
        out.append(
            (block_ref, send_hbm.at[:rows, 4 * cols : 4 * cols + lanes], out_sems.at[passages + 2])
        )
        start_all(out[-1:])
    wait_all(out)


def input_back_kernel(
    info_ref, x_ref, gain_ref, grad_resid_ref, d_first_ref, d_second_ref,
    wq_first_ref, wk_first_ref, wv_first_ref, *refs, info,
):
    qk_pieces, vo_pieces = refs[:4], refs[4:8]
    grad_input_ref, wq_ref, wk_ref, wv_ref, sem = refs[8:]

    @pl.when(pl.program_id(0) == 0)
    def _():
        rows, cols = wq_ref.shape[0] // 4, wq_ref.shape[1]
        gather_pieces(
            (qk_pieces, vo_pieces), info_ref[info] & 3, sem,
            [projection_routes(rows, cols, (wq_ref, wk_ref)), projection_routes(rows, cols, (wv_ref,))],
        )

    width = wq_ref.shape[1]
    total = None
    for d_ref, refs in (
        (d_first_ref, (wq_first_ref, wk_first_ref, wv_first_ref)),
        (d_second_ref, (wq_ref, wk_ref, wv_ref)),
    ):
        for n, ref in enumerate(refs):
            term = dot_t(d_ref[:, n * width : (n + 1) * width], ref[...])
            total = term if total is None else total + term
    back, _ = rms_back(x_ref[...].astype(F32), gain_ref[0:1, :].astype(F32), total)
    grad_input_ref[...] = grad_resid_ref[...] + back


def whole_spec(array_shape):
    return pl.BlockSpec(array_shape, lambda i: (0,) * len(array_shape), pipeline_mode=pl.Buffered(1))


def call(kernel, grid, ins, outs, scratch, cost, name):
    arrays = [a for a, _ in ins]
    return pl.pallas_call(
        kernel,
        grid=grid,
        in_specs=[s for _, s in ins],
        out_specs=[s for _, _, s in outs],
        out_shape=[jax.ShapeDtypeStruct(s, d) for s, d, _ in outs],
        scratch_shapes=scratch,
        compiler_params=pltpu.CompilerParams(
            dimension_semantics=("arbitrary",), vmem_limit_bytes=VMEM_BYTES
        ),
        cost_estimate=pl.CostEstimate(flops=1, bytes_accessed=1, transcendentals=0),
        name=name,
    )(*arrays)


def after(value, *others):
    return lax.optimization_barrier((value,) + others)[0]


def shards(
    inputs, gain_attn, w_query, w_key, w_value, w_output, relative_bias_table,
    gain_ffn, w_inner, w_outer, lengths, cotangent, *, dp, tp,
):
    rows_n, width = inputs.shape
    groups = lengths.shape[0]
    passages = groups // tp
    seq = rows_n // passages
    cols = w_query.shape[1]
    heads = cols // HEAD_DIM
    hidden = w_inner.shape[1]
    me = lax.axis_index("dp")
    side = lax.axis_index("tensor")
    rest = dp // 4

    def across(value, distance):
        return lax.ppermute(value, "dp", [(i, i ^ distance) for i in range(dp)])

    def beside(value):
        return lax.ppermute(value, "tensor", [(i, tp - 1 - i) for i in range(tp)])

    def across_beside(value, distance):
        pairs = [(i * tp + t, (i ^ distance) * tp + tp - 1 - t) for i in range(dp) for t in range(tp)]
        return lax.ppermute(value, ("dp", "tensor"), pairs)

    quarter = me & 3

    def part(weight, axis=0):
        count = weight.shape[axis] // 4
        return lax.dynamic_slice_in_dim(weight, quarter * count, count, axis)

    wo_part = part(w_output)
    wo_part = jnp.concatenate([wo_part[:, :cols], wo_part[:, cols:]], axis=0)
    table = jnp.pad(relative_bias_table.T, ((0, 16 - heads), (0, 128 - BUCKETS)))
    qk_part = jnp.concatenate(
        [jnp.concatenate([part(w_query), part(w_key)], axis=1), jnp.pad(table, ((0, 0), (0, 2 * cols - 128)))], axis=0)
    vo_part = jnp.concatenate([part(w_value), wo_part], axis=1)
    qk_got, vo_got = beside(qk_part), beside(vo_part)
    inner_part = part(after(w_inner, qk_part, vo_part))
    numbers = jnp.concatenate([lengths, jnp.stack([me, side * passages]).astype(jnp.int32)])
    info = groups
    gains = jnp.stack([gain_attn, gain_ffn])

    smem = pl.BlockSpec(memory_space=pltpu.SMEM)
    anywhere = pl.BlockSpec(memory_space=pltpu.HBM)
    by_passage = lambda c: pl.BlockSpec((seq, c), lambda p: (p, 0))
    by_passage_t = pl.BlockSpec((width, seq), lambda p: (0, p))
    lse_spec = pl.BlockSpec((1, 8, seq), lambda p: (p, 0, 0))
    weight_spec = whole_spec((width, cols))
    table_spec = whole_spec((16, 128))
    gain_spec = whole_spec((2, width))
    perm_spec = whole_spec((width, width))
    small_rows = -(-width // 1024) * 8
    small_out = ((small_rows, 128), F32, whole_spec((small_rows, 128)))
    wo_spec = whole_spec((cols, width))
    qkv_outs = [((rows_n, cols), BF16, by_passage(cols))] * 4 + [((passages, 8, seq), F32, lse_spec)]
    bias_scratch = pltpu.VMEM((heads, seq, seq), F32)
    qkv_scratch = [pltpu.VMEM((width, cols), BF16)] * 3
    wo_scratch = pltpu.VMEM((cols, width), BF16)
    dma = pltpu.SemaphoreType.DMA
    cols_vmem = pltpu.VMEM((rows_n, cols), BF16)
    acc_hbm = ((rows_n, width), F32, anywhere)
    rows_hbm = ((rows_n, width), BF16, anywhere)
    turned_hbm = ((width, rows_n), BF16, anywhere)
    acc_vmem = pltpu.VMEM((rows_n, width), F32)
    rows_vmem = pltpu.VMEM((rows_n, width), BF16)
    turned_vmem = pltpu.VMEM((width, rows_n), BF16)
    attn_cost = 2 * rows_n * (width * 3 * cols + seq * 4 * cols)

    bits = [2**n for n in range(1, dp.bit_length() - 1)]
    upper = bits[1:]
    bits_in = upper[:2] + bits[:1] + upper[2:]
    rows_one, q_near, k_near, v_near, ctx_near, lse_near = call(
        functools.partial(attn_first_kernel, info=info), (passages,),
        [(after(numbers, qk_part, vo_part, inner_part), smem), (inputs, by_passage(width)), (gains, gain_spec),
         (w_query, weight_spec), (w_key, weight_spec), (w_value, weight_spec), (table, table_spec)],
        [((rows_n, width), BF16, by_passage(width))] + qkv_outs, [bias_scratch], attn_cost, "attn_first",
    )
    qk_got, vo_got = after(qk_got, rows_one), after(vo_got, rows_one)
    qk_second, vo_second = across(qk_got, 2), across(vo_got, 2)
    qk_core, vo_core = across(qk_got, 1), across(vo_got, 1)
    outer_part = part(after(w_outer, qk_got, vo_got))
    inner_got = beside(after(inner_part, qk_got, vo_got))
    rows_one_t, cot_t, perm, perm_in = call(
        functools.partial(turn_kernel, dp=dp, info=info, orders=([1] + bits, [1] + bits_in)), (passages,),
        [(after(numbers, qk_got, vo_got, outer_part), smem), (rows_one, by_passage(width)), (cotangent, by_passage(width))],
        [((width, rows_n), BF16, by_passage_t)] * 2 + [((width, width), BF16, perm_spec)] * 2,
        [], 4 * rows_n * width * width, "turn",
    )
    attn_pieces = [qk_got, qk_core, qk_second, across(after(qk_second, perm), 1)]
    attn_pieces += [vo_got, vo_core, vo_second, across(after(vo_second, perm), 1)]
    outer_got = beside(outer_part)
    inner_got = after(inner_got, perm)
    inner_second = across(inner_got, 2)
    inner_core = across(inner_got, 1)
    q_far, k_far, v_far, ctx_far, lse_far, residual, rows_two, rows_two_t, table_far = call(
        functools.partial(attn_second_kernel, seq=seq, info=info), (1,),
        [(after(numbers, inner_got), smem), (gains, gain_spec), (rows_one, anywhere), (inputs, anywhere),
         (ctx_near, anywhere), (perm_in, anywhere)] + [(a, anywhere) for a in attn_pieces]
        + [(w_output, anywhere)],
        [((rows_n, cols), BF16, anywhere)] * 4 + [((passages, 8, seq), F32, whole_spec((passages, 8, seq)))]
        + [acc_hbm, rows_hbm, turned_hbm, ((16, 128), BF16, table_spec)],
        [bias_scratch] + qkv_scratch + [wo_scratch, wo_scratch, rows_vmem, rows_vmem, cols_vmem]
        + [pltpu.VMEM((width, width), BF16)] + [cols_vmem] * 4 + [acc_vmem, rows_vmem, turned_vmem]
        + [dma((2,)), dma((6,)), dma((7 * passages,))], attn_cost, "attn_second",
    )

    block_hidden = 768 if hidden % 768 == 0 else hidden
    steps = hidden // block_hidden
    chunk_first, chunk_second, chunk_late = min(512, rows_n), rows_n, rows_n
    grad_out = ((width // 2, hidden), BF16, anywhere)
    hidden_vmem = pltpu.VMEM((rows_n, hidden), BF16)
    work_scratch = [rows_vmem] * 2 + [pltpu.VMEM((width, hidden), BF16), pltpu.VMEM((hidden, width), BF16)]
    work_scratch += [turned_vmem] * 2 + [acc_vmem] * 2 + [hidden_vmem] * 2
    work_scratch += [pltpu.VMEM((width // 2, hidden), BF16)] * 4
    ffn_cost = 12 * rows_n * width * hidden
    outer_got = after(outer_got, rows_two)
    outer_second = across(outer_got, 2)
    outer_core = across(outer_got, 1)
    inner_last = across(after(inner_second, rows_two), 1)
    ffn_near, back_near, in_send_near, out_send_near, in_keep_near, out_keep_near = call(
        functools.partial(ffn_first_kernel, chunk=chunk_first, block=block_hidden), (1,),
        [(after(rows_two, outer_got, inner_second, inner_core), anywhere), (cotangent, anywhere),
         (w_inner, anywhere), (w_outer, anywhere), (rows_two_t, anywhere), (cot_t, anywhere)],
        [acc_hbm, acc_hbm] + [grad_out] * 4,
        work_scratch + [dma((2 * (rows_n // chunk_first) + 2 * steps + 2,)), dma((4 * steps + 2,))], ffn_cost, "ffn_first",
    )
    ffn_pieces = [inner_got, inner_core, inner_second, inner_last]
    ffn_pieces += [outer_got, outer_core, outer_second, across(after(outer_second, ffn_near), 1)]

    def whole(array):
        return (array, 0, array.shape[0])

    def part_of(term, n, ways):
        array, which, rows = term
        return (array, which * ways + n, rows // ways)

    def cut(terms, ways=2):
        return [part_of(t, 0, ways) for t in terms], [[part_of(t, n, ways) for t in terms] for n in range(1, ways)]

    def total(terms):
        return sum(array[which * rows : (which + 1) * rows].astype(F32) for array, which, rows in terms)

    def add_up(*groups):
        return [total(terms).astype(BF16) for terms in groups]

    def distances(low_bits):
        return low_bits if len(low_bits) < 2 else [low_bits[1], low_bits[0], low_bits[0] + low_bits[1]]

    out_got_near = across(after(out_send_near, outer_second, inner_last, outer_core), 1)
    in_got_near = across(after(in_send_near, outer_second, inner_last, outer_core), 1)
    outer_near, sent = cut([whole(out_keep_near), whole(out_got_near)])
    inner_near, sent_in = cut([whole(in_keep_near), whole(in_got_near)])
    (outer_near_sent,) = add_up(sent[0])
    (inner_near_sent,) = add_up(sent_in[0])
    outer_near_got = across(outer_near_sent, 2)
    inner_near_got = across(inner_near_sent, bits_in[0])
    (
        layer_out, grad_residual, grad_attn, grad_attn_t, gain_two_part,
        in_send_far, out_send_far, in_keep_far, out_keep_far,
    ) = call(
        functools.partial(
            ffn_second_kernel, chunk=chunk_second, late_chunk=chunk_late, block=block_hidden, info=info), (1,),
        [(after(numbers, outer_near_sent, inner_near_sent), smem), (gains, gain_spec), (rows_two, anywhere),
         (cotangent, anywhere), (rows_two_t, anywhere), (cot_t, anywhere)]
        + [(a, anywhere) for a in ffn_pieces]
        + [(ffn_near, anywhere), (back_near, anywhere), (residual, anywhere), (perm, anywhere)],
        [rows_hbm, acc_hbm, rows_hbm, turned_hbm, small_out] + [grad_out] * 4,
        work_scratch + [acc_vmem] * 3 + [pltpu.VMEM((width, width), BF16)]
        + [rows_vmem, acc_vmem, rows_vmem, turned_vmem]
        + [dma((steps + 1,)), dma((2 * (rows_n // chunk_second) + 6,)),
           dma((4 * steps + 3 * (rows_n // chunk_late) + 1,))],
        ffn_cost, "ffn_second",
    )

    def attn_back(weights, q, k, v, lse, ctx, tab, order, name, vectors=()):
        half_shape = (width // 2, 4 * cols)
        far = not vectors
        sent_shape = half_shape if far else (width // 2, 4 * cols + 256)
        vector_spec = whole_spec((small_rows, 128))
        more_out = [] if far else [((4 * small_rows, 128), F32, whole_spec((4 * small_rows, 128)))]
        more_scratch = [] if far else [pltpu.VMEM((4 * small_rows, 256), BF16)]
        return call(
            functools.partial(attn_back_kernel, seq=seq, info=info, bits=[1] + bits, far=far), (1,),
            [(after(numbers, *order), smem)] + [(w, anywhere) for w in weights] + [(v, vector_spec) for v in vectors]
            + [(grad_attn, anywhere), (q, anywhere), (k, anywhere), (v, anywhere),
               (lse, whole_spec((passages, 8, seq))), (tab, table_spec), (rows_one_t, anywhere),
               (grad_attn_t, anywhere), (ctx, anywhere), (perm, anywhere), (gains, gain_spec)],
            [((rows_n, 3 * cols), BF16, anywhere), (sent_shape, BF16, anywhere)] + more_out
            + [(half_shape, BF16, anywhere), ((8, 128), F32, whole_spec((8, 128))), small_out],
            qkv_scratch + [wo_scratch, rows_vmem] + [cols_vmem] * 3 + [turned_vmem] * 2
            + [cols_vmem, pltpu.VMEM((width, width), BF16), pltpu.VMEM((rows_n, 3 * cols), BF16)]
            + [pltpu.VMEM(half_shape, BF16)] * 2 + [bias_scratch, pltpu.VMEM((heads, seq, seq), F32)]
            + [pltpu.VMEM((width, 3 * cols), F32), dma((4,)), dma((4 * passages + 4,)), dma((passages + 3,))]
            + more_scratch, 2 * rows_n * cols * (5 * width + 5 * seq), name,
        )

    def pack(values, rows):
        high = lax.reduce_precision(values, 8, 7)
        middle = lax.reduce_precision(values - high, 8, 7)
        parts = jnp.concatenate([high, middle], axis=1).astype(BF16)
        return jnp.pad(parts, ((0, rows - parts.shape[0]), (0, 0)))

    def unpack(block):
        return block[:, :128].astype(F32) + block[:, 128:].astype(F32)

    def finish(terms, left, *order):
        for bit in left:
            terms, sent = cut(terms)
            terms = terms + [whole(after(across(total(sent[0]).astype(BF16), bit), *order))]
        return total(terms)

    outer_near_got = after(outer_near_got, grad_attn)
    inner_near_got = after(inner_near_got, grad_attn)
    outer_near = outer_near + [whole(outer_near_got)]
    out_got_far = across(after(out_send_far, outer_near_got, inner_near_got), 1)
    in_got_far = across(after(in_send_far, outer_near_got, inner_near_got), 1)
    inner_near, sent_near = cut(inner_near + [whole(inner_near_got)])
    (inner_near_sent,) = add_up(sent_near[0])
    out_got_far = after(out_got_far, inner_near_sent)
    outer_far, sent = cut([whole(out_keep_far), whole(out_got_far)])
    inner_far, sent_in = cut([whole(in_keep_far), whole(in_got_far)])
    outer_far_sent, inner_far_sent = add_up(sent[0], sent_in[0])
    outer_far_got = across(outer_far_sent, 2)
    inner_far_got = across(inner_far_sent, bits_in[0])
    inner_near_got = across(inner_near_sent, bits_in[1])
    d_far, ag_send_far, ag_keep_far, table_part_far, gain_part_far = attn_back(
        attn_pieces, q_far, k_far, v_far, lse_far, ctx_far, table_far,
        [outer_far_sent, inner_far_sent, inner_near_sent], "attn_back_far",
    )
    outer_far_got = after(outer_far_got, d_far)
    inner_far_got = after(inner_far_got, d_far)
    inner_near_got = after(inner_near_got, d_far)
    ag_got_far = across(after(ag_send_far, outer_far_got, inner_far_got, inner_near_got), 1)
    outer_far = outer_far + [whole(outer_far_got)]
    inner_near = inner_near + [whole(inner_near_got)]
    inner_far, sent_in = cut(inner_far + [whole(inner_far_got)])
    outer_far_x, inner_far_sent = add_up(outer_far, sent_in[0])
    outer_x_got = beside(outer_far_x)
    inner_far_got = across(inner_far_sent, bits_in[1])
    attn_far, sent = cut([whole(ag_keep_far), whole(ag_got_far)])
    (attn_far_sent,) = add_up(sent[0])
    attn_far_got = across(attn_far_sent, 2)
    order = [outer_far_x, inner_far_sent, attn_far_sent]
    d_near, ag_send_near, vectors_own, ag_keep_near, _, _ = attn_back(
        [w_query, w_key, w_value, w_output], q_near, k_near, v_near, lse_near, ctx_near, table, order,
        "attn_back_near", (gain_two_part, gain_part_far, table_part_far),
    )
    attn_far_got = after(attn_far_got, d_near)
    inner_far_got = after(inner_far_got, d_near)
    outer_x_got = after(outer_x_got, d_near)
    ag_got_near = across(after(ag_send_near, attn_far_got, inner_far_got, outer_x_got), 1)
    vectors = vectors_own + unpack(ag_got_near[: 4 * small_rows, 4 * cols :])
    same = vectors + across(vectors, 2)
    outer, sent = cut(outer_near + [whole(outer_x_got)], 2 ** len(upper[:2]))
    outer_sent = add_up(*sent)
    block = pack(same, outer_sent[0].shape[0])
    outer_sent = [jnp.concatenate([v, block], axis=1) for v in outer_sent]
    outer_got = [across(v, d) for v, d in zip(outer_sent, distances(upper[:2]), strict=True)]
    far_x = jnp.concatenate(
        [total(attn_far + [whole(attn_far_got)]), total(inner_far + [whole(inner_far_got)])], axis=0).astype(BF16)
    far_x_got = beside(far_x)
    attn_near, sent = cut([whole(ag_keep_near), whole(ag_got_near[:, : 4 * cols])])
    (attn_near_sent,) = add_up(sent[0])
    attn_near_got = across(after(attn_near_sent, same), 2)
    order = [far_x, attn_near_sent] + outer_sent
    (grad_input,) = call(
        functools.partial(input_back_kernel, info=info), (passages,),
        [(after(numbers, *order), smem),
         (inputs, by_passage(width)), (gains, gain_spec), (grad_residual, by_passage(width)),
         (d_near, by_passage(3 * cols)), (d_far, by_passage(3 * cols)),
         (w_query, weight_spec), (w_key, weight_spec), (w_value, weight_spec)]
        + [(a, anywhere) for a in attn_pieces],
        [((rows_n, width), F32, by_passage(width))],
        qkv_scratch + [dma], 12 * rows_n * width * cols, "input_back",
    )
    far_x_got = after(far_x_got, grad_input)
    rows = attn_near_sent.shape[0]
    attn_near_got = after(attn_near_got, grad_input, far_x_got, *outer_got)
    attn, sent = cut(attn_near + [whole(attn_near_got), whole(far_x_got[:rows])], 2 ** len(upper[:2]))
    attn_sent = add_up(*sent)
    attn_got = [across(v, d) for v, d in zip(attn_sent, distances(upper[:2]), strict=True)]
    inner = inner_near + [whole(after(far_x_got, *attn_sent)[rows:])]
    grad_inner = finish(inner, bits_in[2:])
    outer_got = [after(got, *attn_sent) for got in outer_got]
    outer = outer + [whole(got[:, :hidden]) for got in outer_got]
    small = same + unpack(sum(got[: 4 * small_rows, hidden:].astype(F32) for got in outer_got))
    for bit in upper[2:]:
        small = small + across(small, bit)
    other = beside(small)
    table_at = 2 * small_rows
    small = jnp.concatenate(
        [small[:table_at] + other[:table_at], small[table_at : table_at + 8] + other[table_at + 8 :]], axis=0)
    grad_outer = finish(outer, upper[2:]).T
    attn_grads = finish(attn + [whole(after(got, grad_inner, grad_outer)) for got in attn_got], upper[2:])
    grad_query, grad_key, grad_value = (attn_grads[:, n * cols : (n + 1) * cols] for n in range(3))
    grad_output = attn_grads[:, 3 * cols :].T

    grad_gain_one = small[: width // 128].reshape(width)
    grad_gain_two = small[small_rows : small_rows + width // 128].reshape(width)
    grad_table = small[table_at : table_at + heads, :BUCKETS].T
    return (
        layer_out, grad_input, grad_gain_one, grad_query, grad_key, grad_value, grad_output,
        grad_table, grad_gain_two, grad_inner, grad_outer,
    )


def solution(mesh):
    both = ("dp", "tensor")
    in_specs = (
        P(both, None), P(), P(None, "tensor"), P(None, "tensor"), P(None, "tensor"), P("tensor", None),
        P(None, "tensor"), P(), P(None, "tensor"), P("tensor", None), P("dp"), P(both, None),
    )
    out_specs = (
        P(both, None), P(both, None), P(), P("dp", "tensor"), P("dp", "tensor"), P("dp", "tensor"),
        P("tensor", "dp"), P(None, "tensor"), P(), P("dp", "tensor"), P("tensor", "dp"),
    )
    body = functools.partial(shards, dp=mesh.shape["dp"], tp=mesh.shape["tensor"])
    return jax.shard_map(body, mesh=mesh, in_specs=in_specs, out_specs=out_specs, check_vma=False)
```

```python
import functools

import jax
import jax.numpy as jnp
from jax import lax
from jax.experimental import pallas as pl
from jax.experimental.pallas import tpu as pltpu
from jax.sharding import PartitionSpec as P

HEAD_DIM = 64
BUCKETS = 32
EPS = 1e-6
MASKED = -1e9
GELU_C = 0.7978845608028654
VMEM_BYTES = 51 * 1024 * 1024
F32 = jnp.float32
BF16 = jnp.bfloat16


def dot(left, right):
    return lax.dot_general(left, right, (((1,), (0,)), ((), ())), preferred_element_type=F32)


def dot_t(left, right):
    return lax.dot_general(left, right, (((1,), (1,)), ((), ())), preferred_element_type=F32)


def dot_l(left, right):
    return lax.dot_general(left, right, (((0,), (0,)), ((), ())), preferred_element_type=F32)


def staggered(count, first, second, third):
    for n in range(count + 2):
        if n < count:
            first(n)
        if 0 <= n - 1 < count:
            second(n - 1)
        if 0 <= n - 2 < count:
            third(n - 2)


def bucket_of(offsets):
    distance = jnp.abs(offsets)
    far = jnp.full_like(distance, 8)
    for power in range(1, 8):
        far = far + (distance * distance >= 64 * 2**power).astype(jnp.int32)
    near = jnp.where(distance < 8, distance, far)
    return near + jnp.where(offsets > 0, 16, 0)


def bucket_indicator(seq, count=BUCKETS):
    lane = lax.broadcasted_iota(jnp.int32, (count, 2 * seq), 1)
    offsets = jnp.where(lane < seq, -lane, 2 * seq - lane)
    ids = lax.broadcasted_iota(jnp.int32, (count, 2 * seq), 0)
    return (bucket_of(offsets) == ids).astype(F32)


def fill_bias(table_ref, bias_ref):
    heads, seq, _ = bias_ref.shape
    base = dot(table_ref[:, :BUCKETS], bucket_indicator(seq).astype(BF16))
    for h in range(heads):
        wide = jnp.broadcast_to(base[h : h + 1, :], (seq, 2 * seq))
        bias_ref[h] = pltpu.roll(wide, 0, 1, stride=1, stride_axis=0)[:, :seq]


def head_mask(columns, parity):
    lane = lax.broadcasted_iota(jnp.int32, columns.shape, 1)
    keep = (lane < HEAD_DIM) if parity == 0 else (lane >= HEAD_DIM)
    return jnp.where(keep, columns, jnp.zeros_like(columns))


def rms_rows(values, gain):
    return values * lax.rsqrt(jnp.mean(values * values, axis=-1, keepdims=True) + EPS) * gain


def add_row(ref, row):
    for n in range(row.shape[1] // 128):
        ref[n : n + 1, :] += row[:, n * 128 : (n + 1) * 128]


def rms_back(values, gain, grads):
    scale = lax.rsqrt(jnp.mean(values * values, axis=-1, keepdims=True) + EPS)
    scaled = grads * gain
    mean = jnp.mean(scaled * values, axis=-1, keepdims=True)
    back = scale * scaled - values * (scale * scale * scale * mean)
    return back, jnp.sum(grads * values * scale, axis=0, keepdims=True)


def fill_perm(perm_ref, me, dp, bits):
    width = perm_ref.shape[0]
    block = width // dp
    index = lax.broadcasted_iota(jnp.int32, (width, 128), 0)
    rel = lax.div(index, block)
    target = jnp.zeros_like(rel)
    for n, bit in enumerate(bits):
        target = target + ((rel >> (len(bits) - 1 - n)) & 1) * bit
    source = (target ^ me) * block + (index - rel * block)
    lane = lax.broadcasted_iota(jnp.int32, (width, 128), 1)
    for n in range(0, width, 128):
        perm_ref[:, n : n + 128] = jnp.where(source == lane + n, 1.0, 0.0).astype(BF16)


def piece_copies(packets, quarter, sem, routes):
    copies = []
    for pieces, ways in zip(packets, routes, strict=True):
        for n, piece in enumerate(pieces):
            for rows, cols, target, count, at in ways:
                start = pl.multiple_of((quarter ^ n) * count, 16)
                copies.append((piece.at[rows, cols], target.at[pl.ds(start, count), at], sem))
    return copies


def start_all(copies):
    for copy in copies:
        pltpu.make_async_copy(*copy).start()


def wait_all(copies):
    for copy in copies:
        pltpu.make_async_copy(*copy).wait()


def gather_pieces(packets, quarter, sem, routes):
    copies = piece_copies(packets, quarter, sem, routes)
    start_all(copies)
    wait_all(copies)


class Heads:
    def __init__(self, seq, heads, lengths, bias_ref, q_ref, k_ref, v_ref, ctx_ref, lse_ref):
        self.seq, self.heads, self.lengths = seq, heads, lengths
        self.bias_ref, self.lse_ref = bias_ref, lse_ref
        self.q_ref, self.k_ref, self.v_ref, self.ctx_ref = q_ref, k_ref, v_ref, ctx_ref
        self.first_head = lax.broadcasted_iota(jnp.int32, (seq, 2 * HEAD_DIM), 1) < HEAD_DIM
        self.key_slot = lax.broadcasted_iota(jnp.int32, (seq, 1), 0)
        self.query_t, self.logits, self.probs, self.parts = {}, {}, {}, {}

    def rows_of(self, p):
        return slice(p * self.seq, (p + 1) * self.seq)

    def pair_of(self, h):
        lo = (h // 2) * 2 * HEAD_DIM
        return slice(lo, lo + 2 * HEAD_DIM)

    def project(self, p, rows, wq_ref, wk_ref, wv_ref):
        query = dot(rows, wq_ref[...]).astype(BF16)
        self.q_ref[self.rows_of(p), :] = query
        self.k_ref[self.rows_of(p), :] = dot(rows, wk_ref[...]).astype(BF16)
        self.v_ref[self.rows_of(p), :] = dot(rows, wv_ref[...]).astype(BF16)
        self.query_t[p] = query.T

    def score(self, n):
        p, h = divmod(n, self.heads)
        both = self.pair_of(h)
        keys = head_mask(self.k_ref[self.rows_of(p), both], h % 2)
        self.logits[n] = dot(keys, self.query_t[p][both, :])

    def normalise(self, n):
        p, h = divmod(n, self.heads)
        valid = self.key_slot < self.lengths[p]
        biased = jnp.where(valid, self.logits.pop(n) + self.bias_ref[h], MASKED)
        peak = jnp.max(biased, axis=0, keepdims=True)
        terms = jnp.exp(biased - peak)
        total = jnp.sum(terms, axis=0, keepdims=True)
        self.probs[n] = (terms * (1.0 / total)).astype(BF16)
        self.lse_ref[p, h : h + 1, :] = peak + jnp.log(total)

    def combine(self, n):
        p, h = divmod(n, self.heads)
        self.parts[n] = dot_l(self.probs.pop(n), self.v_ref[self.rows_of(p), self.pair_of(h)])
        if h % 2:
            both = jnp.where(self.first_head, self.parts.pop(n - 1), self.parts.pop(n))
            self.ctx_ref[self.rows_of(p), self.pair_of(h)] = both.astype(BF16)


def attn_first_kernel(
    len_ref, x_ref, gain_ref, wq_ref, wk_ref, wv_ref, table_ref,
    rows_ref, q_ref, k_ref, v_ref, ctx_ref, lse_ref, bias_ref, *, info,
):
    p = pl.program_id(0)
    seq = rows_ref.shape[0]

    @pl.when(p == 0)
    def _():
        fill_bias(table_ref, bias_ref)

    rows = rms_rows(x_ref[...].astype(F32), gain_ref[0:1, :].astype(F32)).astype(BF16)
    rows_ref[...] = rows
    lengths = [len_ref[len_ref[info + 1] + p]]
    work = Heads(seq, bias_ref.shape[0], lengths, bias_ref, q_ref, k_ref, v_ref, ctx_ref, lse_ref)
    work.project(0, rows, wq_ref, wk_ref, wv_ref)
    staggered(work.heads, work.score, work.normalise, work.combine)


def turn_kernel(
    len_ref, rows_ref, cot_ref, rows_t_ref, cot_t_ref, perm_ref, perm_in_ref, *, dp, info, orders,
):
    @pl.when(pl.program_id(0) == 0)
    def _():
        fill_perm(perm_ref, len_ref[info], dp, orders[0])
        fill_perm(perm_in_ref, len_ref[info], dp, orders[1])

    rows_t_ref[...] = dot_t(perm_ref[...], rows_ref[...]).astype(BF16)
    cot_t_ref[...] = dot_t(perm_ref[...], cot_ref[...]).astype(BF16)


def projection_routes(piece_rows, cols, targets):
    rows = slice(0, piece_rows)
    return [
        (rows, slice(n * cols, (n + 1) * cols), target, piece_rows, slice(0, cols))
        for n, target in enumerate(targets)
    ]


def output_routes(piece_rows, cols, target):
    half, lanes = piece_rows // 2, slice(cols, 2 * cols)
    return [
        (slice(0, half), lanes, target, half, slice(0, cols)),
        (slice(half, piece_rows), lanes, target, half, slice(cols, 2 * cols)),
    ]


def attn_second_kernel(len_ref, gain_ref, rows_hbm, x_hbm, ctx_first_hbm, perm_hbm, *refs, seq, info):
    qk_pieces, vo_pieces = refs[:4], refs[4:8]
    (
        wo_first_hbm, q_hbm, k_hbm, v_hbm, ctx_hbm, lse_ref, resid_hbm, rows_two_hbm, rows_two_t_hbm, table_ref,
        bias_ref, wq_ref, wk_ref, wv_ref, wo_ref, wo_first_ref, rows_ref, x_ref, ctx_first_ref, perm_ref,
        q_ref, k_ref, v_ref, ctx_ref, resid_ref, rows_two_ref, rows_two_t_ref, piece_sem, in_sems, out_sems,
    ) = refs[8:]
    rows, cols = wq_ref.shape[0] // 4, wq_ref.shape[1]
    heads = bias_ref.shape[0]
    passages = q_ref.shape[0] // seq
    quarter = len_ref[info] & 3
    get_table = [(qk_pieces[0].at[rows : rows + 16, :128], table_ref, in_sems.at[0])]
    projections = piece_copies(
        (qk_pieces, vo_pieces), quarter, piece_sem.at[0],
        [projection_routes(rows, cols, (wq_ref, wk_ref)), projection_routes(rows, cols, (wv_ref,))],
    )
    get_rows = [(rows_hbm, rows_ref, in_sems.at[1])]
    output = piece_copies((vo_pieces,), quarter, piece_sem.at[1], [output_routes(rows, cols, wo_ref)])
    output += [
        (wo_first_hbm, wo_first_ref, in_sems.at[2]), (ctx_first_hbm, ctx_first_ref, in_sems.at[3]),
        (x_hbm, x_ref, in_sems.at[4]), (perm_hbm, perm_ref, in_sems.at[5]),
    ]
    start_all(get_table + get_rows + projections + output)
    wait_all(get_table)
    fill_bias(table_ref, bias_ref)
    wait_all(get_rows + projections)
    lengths = [len_ref[len_ref[info + 1] + p] for p in range(passages)]
    work = Heads(seq, heads, lengths, bias_ref, q_ref, k_ref, v_ref, ctx_ref, lse_ref)
    out = []

    def put(ref, hbm, at, sem):
        copy = (ref.at[at], hbm.at[at], out_sems.at[sem])
        out.append(copy)
        start_all([copy])

    def project(p):
        here = work.rows_of(p)
        work.project(p, rows_ref[here, :], wq_ref, wk_ref, wv_ref)
        for n, (ref, hbm) in enumerate(((q_ref, q_hbm), (k_ref, k_hbm), (v_ref, v_hbm))):
            put(ref, hbm, (here, slice(None)), 7 * p + n)

    def branch(p):
        here = work.rows_of(p)
        if p == 0:
            wait_all(output)
        total = dot(ctx_first_ref[here, :], wo_first_ref[...]) + dot(ctx_ref[here, :], wo_ref[...])
        residual = x_ref[here, :].astype(F32) + total
        resid_ref[here, :] = residual
        rows_two_ref[here, :] = rms_rows(residual, gain_ref[1:2, :].astype(F32)).astype(BF16)
        pairs = ((ctx_ref, ctx_hbm), (resid_ref, resid_hbm), (rows_two_ref, rows_two_hbm))
        for n, (ref, hbm) in enumerate(pairs):
            put(ref, hbm, (here, slice(None)), 7 * p + 3 + n)

    def turn(p):
        here = work.rows_of(p)
        rows_two_t_ref[:, here] = dot_t(perm_ref[...], rows_two_ref[here, :]).astype(BF16)
        put(rows_two_t_ref, rows_two_t_hbm, (slice(None), here), 7 * p + 6)

    for p in range(passages):
        project(p)
    count = passages * heads
    for n in range(count + 2):
        if n < count:
            work.score(n)
        if 0 <= n - 1 < count:
            work.normalise(n - 1)
        if 0 <= n - 2 < count:
            work.combine(n - 2)
        done = (n - 2) // heads
    for p in range(passages):
        branch(p)
    for p in range(passages):
        turn(p)
    wait_all(out)


class Hidden:
    def __init__(self, refs, weight_refs, weight_hbms, sems, chunk, block):
        (
            self.rows_ref, self.cot_ref, self.wi_ref, self.wo_ref, self.rows_t_ref, self.cot_t_ref, self.ffn_ref,
            self.back_ref, self.act_ref, self.grad_ref,
        ) = refs
        self.weight_refs, self.weight_hbms, self.sems = weight_refs, weight_hbms, sems
        self.chunk, self.block = chunk, block
        self.chunks = self.rows_ref.shape[0] // chunk
        self.blocks = self.wi_ref.shape[1] // block
        self.out = []

    def rows_of(self, i):
        return slice(i * self.chunk, (i + 1) * self.chunk)

    def hidden(self, b, ready):
        units = slice(b * self.block, (b + 1) * self.block)

        def first(i):
            at = self.rows_of(i)
            ready(b, i, 0)
            v = dot(self.rows_ref[at, :], self.wi_ref[:, units])
            ready(b, i, 1)
            grad_act = dot_t(self.cot_ref[at, :], self.wo_ref[units, :])
            square = v * v
            tanh = jnp.tanh(GELU_C * v * (1.0 + 0.044715 * square))
            half = 0.5 + 0.5 * tanh
            self.act_ref[at, units] = (v * half).astype(BF16)
            slope = half + (0.5 * GELU_C) * v * (1.0 - tanh * tanh) * (1.0 + 0.134145 * square)
            self.grad_ref[at, units] = (grad_act * slope).astype(BF16)

        def second(i):
            at = self.rows_of(i)
            forward = dot(self.act_ref[at, units], self.wo_ref[units, :])
            backward = dot_t(self.grad_ref[at, units], self.wi_ref[:, units])
            if b:
                self.ffn_ref[at, :] += forward
                self.back_ref[at, :] += backward
            else:
                self.ffn_ref[at, :] = forward
                self.back_ref[at, :] = backward

        staggered(self.chunks, first, second, lambda i: None)

    def weights(self, b, which):
        units = slice(b * self.block, (b + 1) * self.block)
        ref = self.weight_refs[which]
        half_rows = ref.shape[0]
        at = slice(half_rows, None) if which < 2 else slice(half_rows)
        left, right = ((self.rows_t_ref, self.grad_ref), (self.cot_t_ref, self.act_ref))[which % 2]
        ref[:, units] = dot(left[at, :], right[:, units]).astype(BF16)
        self.put(ref, self.weight_hbms[which], (slice(None), units))

    def put(self, ref, hbm, at):
        self.out.append((ref.at[at], hbm.at[at], self.sems.at[len(self.out)]))
        start_all(self.out[-1:])


def ffn_first_kernel(rows_hbm, cot_hbm, wi_hbm, wo_hbm, rows_t_hbm, cot_t_hbm, ffn_hbm, back_hbm, *refs, chunk, block):
    weight_hbms, work_refs, weight_refs, in_sems, out_sems = refs[:4], refs[4:14], refs[14:18], refs[18], refs[19]
    work = Hidden(work_refs, weight_refs, weight_hbms, out_sems, chunk, block)
    copies = {}

    def get(key, hbm, ref, at):
        copies[key] = [(hbm.at[at], ref.at[at], in_sems.at[len(copies)])]
        start_all(copies[key])

    everything = slice(None)

    def get_weights(b):
        units = slice(b * block, (b + 1) * block)
        get(("weight", b, 0), wi_hbm, work.wi_ref, (everything, units))
        get(("weight", b, 1), wo_hbm, work.wo_ref, (units, everything))

    def get_rows(i):
        get(("rows", i, 0), rows_hbm, work.rows_ref, (work.rows_of(i), everything))
        get(("rows", i, 1), cot_hbm, work.cot_ref, (work.rows_of(i), everything))

    def ready(b, i, which):
        if i == 0:
            wait_all(copies["weight", b, which])
        if b == 0:
            wait_all(copies["rows", i, which])
        if b == 0 and i == 0 and which == 1:
            for n in range(1, work.blocks):
                get_weights(n)
            get("turned rows", rows_t_hbm, work.rows_t_ref, (everything, everything))
            get("turned cot", cot_t_hbm, work.cot_t_ref, (everything, everything))

    get_rows(0)
    get_weights(0)
    for i in range(1, work.chunks):
        get_rows(i)
    for b in range(work.blocks):
        work.hidden(b, ready)
        if b == 0:
            wait_all(copies["turned rows"] + copies["turned cot"])
        if b == work.blocks - 1:
            work.put(work.ffn_ref, ffn_hbm, (everything, everything))
            work.put(work.back_ref, back_hbm, (everything, everything))
        for which in range(4):
            work.weights(b, which)
    wait_all(work.out)


def ffn_second_kernel(
    info_ref, gain_ref, rows_hbm, cot_hbm, rows_t_hbm, cot_t_hbm, *refs, chunk, late_chunk, block, info,
):
    inner_pieces, outer_pieces = refs[:4], refs[4:8]
    (
        ffn_in_hbm, back_in_hbm, resid_hbm, perm_hbm,
        layer_hbm, grad_resid_hbm, grad_attn_hbm, grad_attn_t_hbm, gain_grad_ref,
    ) = refs[8:17]
    weight_hbms, work_refs, weight_refs = refs[17:21], refs[21:31], refs[31:35]
    (
        ffn_in_ref, back_in_ref, resid_ref, perm_ref, layer_ref, grad_resid_ref, grad_attn_ref, grad_attn_t_ref,
        piece_sems, in_sems, out_sems,
    ) = refs[35:]
    work = Hidden(work_refs, weight_refs, weight_hbms, out_sems, chunk, block)
    width, hidden = work.wi_ref.shape
    wi_rows, wo_rows = width // 4, hidden // 4
    quarter = info_ref[info] & 3
    everything = slice(None)
    inner = [
        piece_copies(
            (inner_pieces,), quarter, piece_sems.at[b],
            [[(slice(0, wi_rows), slice(b * block, (b + 1) * block), work.wi_ref, wi_rows,
               slice(b * block, (b + 1) * block))]],
        )
        for b in range(work.blocks)
    ]
    outer = piece_copies(
        (outer_pieces,), quarter, piece_sems.at[work.blocks],
        [[(slice(0, wo_rows), slice(0, width), work.wo_ref, wo_rows, slice(0, width))]],
    )
    rows_in = []
    for i in range(work.chunks):
        at = (work.rows_of(i), everything)
        rows_in.append([
            (rows_hbm.at[at], work.rows_ref.at[at], in_sems.at[2 * i]),
            (cot_hbm.at[at], work.cot_ref.at[at], in_sems.at[2 * i + 1]),
        ])
    base = 2 * work.chunks
    turned = [(rows_t_hbm, work.rows_t_ref, in_sems.at[base]), (cot_t_hbm, work.cot_t_ref, in_sems.at[base + 1])]
    late = [
        (back_in_hbm, back_in_ref, in_sems.at[base + 2]), (resid_hbm, resid_ref, in_sems.at[base + 3]),
        (ffn_in_hbm, ffn_in_ref, in_sems.at[base + 4]), (perm_hbm, perm_ref, in_sems.at[base + 5]),
    ]

    def ready(b, i, which):
        if i == 0 and which == 0:
            wait_all(inner[b])
        if i == 0 and b == 0 and which == 1:
            wait_all(outer)
        if b == 0:
            wait_all(rows_in[i][which : which + 1])
        if b == 0 and i == 0 and which == 1:
            for n in range(1, work.blocks):
                start_all(inner[n])
            start_all(turned)

    start_all(rows_in[0][:1] + inner[0] + rows_in[0][1:] + outer)
    for i in range(1, work.chunks):
        start_all(rows_in[i])
    last = work.blocks - 1
    for b in range(work.blocks):
        if b == last:
            start_all(late)
        work.hidden(b, ready)
        if b == 0:
            wait_all(turned)
        if b < last:
            for which in range(4):
                work.weights(b, which)
    wait_all(late)
    gain_grad_ref[...] = jnp.zeros_like(gain_grad_ref)
    count = resid_ref.shape[0] // late_chunk
    for i in range(count):
        at = slice(i * late_chunk, (i + 1) * late_chunk)
        residual = resid_ref[at, :]
        back, gain_part = rms_back(residual, gain_ref[1:2, :].astype(F32), work.back_ref[at, :] + back_in_ref[at, :])
        add_row(gain_grad_ref, gain_part)
        grad_resid = work.cot_ref[at, :].astype(F32) + back
        grad_resid_ref[at, :] = grad_resid
        grad_attn_ref[at, :] = grad_resid.astype(BF16)
        layer_ref[at, :] = (residual + (work.ffn_ref[at, :] + ffn_in_ref[at, :])).astype(BF16)
        if i < 3:
            work.weights(last, i)
        for ref, hbm in ((grad_attn_ref, grad_attn_hbm), (grad_resid_ref, grad_resid_hbm), (layer_ref, layer_hbm)):
            work.put(ref, hbm, (at, everything))
    grad_attn_t_ref[...] = dot_t(perm_ref[...], grad_attn_ref[...]).astype(BF16)
    work.put(grad_attn_t_ref, grad_attn_t_hbm, (everything, everything))
    for which in range(min(count, 3), 4):
        work.weights(last, which)
    wait_all(work.out)


def gain_from_weights(me, bits, w_refs, grads, perm_ref, gain_ref, out_ref):
    width, cols = w_refs[0].shape
    block = width // (2 ** len(bits))
    if block % 16:
        weights = [dot(perm_ref[...], ref[...]) for ref in w_refs]
    else:
        weights = []
        for ref in w_refs:
            rows = []
            for n in range(width // block):
                target = sum(bit for m, bit in enumerate(bits) if (n >> (len(bits) - 1 - m)) & 1)
                rows.append(ref[pl.ds(pl.multiple_of((me ^ target) * block, 16), block), :])
            weights.append(jnp.concatenate(rows, axis=0).astype(F32))
    folded = None
    for n, weight in enumerate(weights):
        for lo in range(0, cols, 128):
            term = weight[:, lo : lo + 128] * grads[:, n * cols + lo : n * cols + lo + 128]
            folded = term if folded is None else folded + term
    ordered = jnp.sum(folded.T, axis=0, keepdims=True)
    high = ordered.astype(BF16)
    middle = (ordered - high.astype(F32)).astype(BF16)
    low = (ordered - high.astype(F32) - middle.astype(F32)).astype(BF16)
    parts = jnp.concatenate([high, middle, low, jnp.zeros((13, width), BF16)], axis=0)
    natural = jnp.sum(dot(parts, perm_ref[...]), axis=0, keepdims=True) / gain_ref[0:1, :].astype(F32)
    out_ref[...] = jnp.zeros_like(out_ref)
    add_row(out_ref, natural)


def attn_back_kernel(len_ref, *refs, seq, info, bits, far):
    if far:
        qk_pieces, vo_pieces, refs = refs[:4], refs[4:8], refs[8:]
    else:
        weights_hbm, vector_refs, own_ref, block_ref = refs[:4], refs[4:7], refs[20], refs[-1]
        refs = refs[7:20] + refs[21:-1]
    (
        grad_attn_hbm, q_hbm, k_hbm, v_hbm, lse_ref, table_ref, rows_t_hbm, grad_attn_t_hbm, ctx_hbm, perm_hbm,
        gain_ref, dqkv_hbm, send_hbm, keep_hbm, table_grad_ref, gain_grad_ref,
        wq_ref, wk_ref, wv_ref, wo_ref, grad_attn_ref, q_ref, k_ref, v_ref, rows_t_ref, grad_attn_t_ref, ctx_ref,
        perm_ref, dqkv_ref, send_ref, keep_ref, bias_ref, sums_ref, grads_ref, piece_sem, in_sems, out_sems,
    ) = refs
    heads = bias_ref.shape[0]
    cols = heads * HEAD_DIM
    passages = q_ref.shape[0] // seq
    half_rows = keep_ref.shape[0]

    def rows_of(p):
        return slice(p * seq, (p + 1) * seq)

    if far:
        rows = wq_ref.shape[0] // 4
        quarter = len_ref[info] & 3
        late_weights = piece_copies(
            (qk_pieces, vo_pieces), quarter, piece_sem.at[0],
            [projection_routes(rows, cols, (wq_ref, wk_ref)), projection_routes(rows, cols, (wv_ref,))],
        )
        output = piece_copies((vo_pieces,), quarter, piece_sem.at[1], [output_routes(rows, cols, wo_ref)])
    else:
        late_weights = [
            (hbm, ref, piece_sem.at[n])
            for n, (hbm, ref) in enumerate(zip(weights_hbm, (wq_ref, wk_ref, wv_ref), strict=False))
        ]
        output = [(weights_hbm[3], wo_ref, piece_sem.at[3])]
    start_all(output)
    by_passage = []
    for p in range(passages):
        pairs = ((grad_attn_hbm, grad_attn_ref), (q_hbm, q_ref), (k_hbm, k_ref), (v_hbm, v_ref))
        by_passage.append(
            [(hbm.at[rows_of(p), :], ref.at[rows_of(p), :], in_sems.at[4 * p + n]) for n, (hbm, ref) in enumerate(pairs)]
        )
    start_all(by_passage[0])
    at = 4 * passages
    turned = [(ctx_hbm, ctx_ref, in_sems.at[at]), (grad_attn_t_hbm, grad_attn_t_ref, in_sems.at[at + 1])]
    last = [(rows_t_hbm, rows_t_ref, in_sems.at[at + 2]), (perm_hbm, perm_ref, in_sems.at[at + 3])]
    fill_bias(table_ref, bias_ref)
    sums_ref[...] = jnp.zeros_like(sums_ref)
    wait_all(output)
    first_head = lax.broadcasted_iota(jnp.int32, (seq, 2 * HEAD_DIM), 1) < HEAD_DIM
    key_slot = lax.broadcasted_iota(jnp.int32, (seq, 1), 0)
    ready, scores, weights, dq, dk, dv = {}, {}, {}, {}, {}, {}

    def pair_of(h, offset=0):
        lo = (h // 2) * 2 * HEAD_DIM + offset
        return slice(lo, lo + 2 * HEAD_DIM)

    def prepare(p):
        wait_all(by_passage[p])
        grad_ctx = dot_t(grad_attn_ref[rows_of(p), :], wo_ref[...]).astype(BF16)
        valid = key_slot < len_ref[len_ref[info + 1] + p]
        ready[p] = (
            grad_ctx, grad_ctx.T, q_ref[rows_of(p), :].T, k_ref[rows_of(p), :].T, valid,
        )

    def score(n):
        p, h = divmod(n, heads)
        _, grad_ctx_t, query_t, _, _ = ready[p]
        both = pair_of(h)
        scores[n] = (
            dot(head_mask(k_ref[rows_of(p), both], h % 2), query_t[both, :]),
            dot(head_mask(v_ref[rows_of(p), both], h % 2), grad_ctx_t[both, :]),
        )

    def soften(n):
        p, h = divmod(n, heads)
        logits, grad_probs = scores.pop(n)
        probs = jnp.exp(logits + bias_ref[h] - lse_ref[p, h : h + 1, :])
        probs = jnp.where(ready[p][4], probs, 0.0)
        mixed = jnp.sum(probs * grad_probs, axis=0, keepdims=True)
        grads = (probs * (grad_probs - mixed)).astype(BF16)
        sums_ref[h] += grads.astype(F32)
        weights[n] = (probs.astype(BF16), grads)

    def combine(n):
        p, h = divmod(n, heads)
        grad_ctx, _, _, keys_t, _ = ready[p]
        probs, grads = weights.pop(n)
        dq[n] = dot(keys_t[h * HEAD_DIM : (h + 1) * HEAD_DIM, :], grads)
        dk[n] = dot(grads, q_ref[rows_of(p), pair_of(h)])
        dv[n] = dot(probs, grad_ctx[:, pair_of(h)])
        if h % 2:
            dqkv_ref[rows_of(p), pair_of(h, cols)] = jnp.where(first_head, dk.pop(n - 1), dk.pop(n)).astype(BF16)
            dqkv_ref[rows_of(p), pair_of(h, 2 * cols)] = jnp.where(first_head, dv.pop(n - 1), dv.pop(n)).astype(BF16)
        if h == heads - 1:
            parts = jnp.concatenate([dq.pop(m) for m in range(n - h, n + 1)], axis=0)
            dqkv_ref[rows_of(p), :cols] = parts.astype(BF16).T
            copy = (dqkv_ref.at[rows_of(p), :], dqkv_hbm.at[rows_of(p), :], out_sems.at[p])
            out.append(copy)
            start_all([copy])

    out = []
    count = passages * heads
    for p in range(1, passages):
        start_all(by_passage[p])
    start_all(turned)
    for p in range(passages):
        prepare(p)
    for n in range(count + 2):
        if n == heads:
            start_all(last + late_weights)
        if n < count:
            score(n)
        if 0 <= n - 1 < count:
            soften(n - 1)
        if 0 <= n - 2 < count:
            combine(n - 2)
        if n == heads:
            wait_all(turned)
            send_ref[:, 3 * cols :] = dot(grad_attn_t_ref[half_rows:, :], ctx_ref[...]).astype(BF16)
        if n == heads + 2:
            keep_ref[:, 3 * cols :] = dot(grad_attn_t_ref[:half_rows, :], ctx_ref[...]).astype(BF16)
    wait_all(last)
    for ref, hbm, at, sem in (
        (send_ref, send_hbm, slice(half_rows, None), passages), (keep_ref, keep_hbm, slice(half_rows), passages + 1),
    ):
        grads_ref[at, :] = dot(rows_t_ref[at, :], dqkv_ref[...])
        ref[:, : 3 * cols] = grads_ref[at, :].astype(BF16)
        copy = (ref, hbm.at[:, : 4 * cols], out_sems.at[sem])
        out.append(copy)
        start_all([copy])
    wait_all(late_weights)
    gain_from_weights(
        len_ref[info], bits, (wq_ref, wk_ref, wv_ref), grads_ref, perm_ref, gain_ref, gain_grad_ref
    )
    rows = []
    for h in range(heads):
        folded = jnp.zeros((8, 2 * seq), F32)
        for a in range(0, seq, 8):
            wide = jnp.concatenate([sums_ref[h, a : a + 8, :], jnp.zeros((8, seq), F32)], axis=1)
            folded = folded + (pltpu.roll(wide, 2 * seq - a, 1) if a else wide)
        diagonals = folded[0:1, :]
        for b in range(1, 8):
            diagonals = diagonals + pltpu.roll(folded[b : b + 1, :], 2 * seq - b, 1)
        rows.append(diagonals)
    rows.append(jnp.zeros((8 - heads, 2 * seq), F32))
    table_grad_ref[...] = lax.dot_general(
        jnp.concatenate(rows, axis=0), bucket_indicator(seq, 128), (((1,), (1,)), ((), ())),
        precision=lax.Precision.HIGHEST, preferred_element_type=F32,
    )
    if not far:
        gain_two_ref, gain_far_ref, table_far_ref = vector_refs
        own = jnp.concatenate(
            [gain_grad_ref[...] + gain_far_ref[...], gain_two_ref[...], table_grad_ref[...], table_far_ref[...]], axis=0)
        own_ref[...] = own
        high = own.astype(BF16)
        middle = (own - high.astype(F32)).astype(BF16)
        block_ref[...] = jnp.concatenate([high, middle], axis=1)
        rows, lanes = block_ref.shape
        out.append(
            (block_ref, send_hbm.at[:rows, 4 * cols : 4 * cols + lanes], out_sems.at[passages + 2])
        )
        start_all(out[-1:])
    wait_all(out)


def input_back_kernel(
    info_ref, x_ref, gain_ref, grad_resid_ref, d_first_ref, d_second_ref,
    wq_first_ref, wk_first_ref, wv_first_ref, *refs, info,
):
    qk_pieces, vo_pieces = refs[:4], refs[4:8]
    grad_input_ref, wq_ref, wk_ref, wv_ref, sem = refs[8:]

    @pl.when(pl.program_id(0) == 0)
    def _():
        rows, cols = wq_ref.shape[0] // 4, wq_ref.shape[1]
        gather_pieces(
            (qk_pieces, vo_pieces), info_ref[info] & 3, sem,
            [projection_routes(rows, cols, (wq_ref, wk_ref)), projection_routes(rows, cols, (wv_ref,))],
        )

    width = wq_ref.shape[1]
    total = None
    for d_ref, refs in (
        (d_first_ref, (wq_first_ref, wk_first_ref, wv_first_ref)),
        (d_second_ref, (wq_ref, wk_ref, wv_ref)),
    ):
        for n, ref in enumerate(refs):
            term = dot_t(d_ref[:, n * width : (n + 1) * width], ref[...])
            total = term if total is None else total + term
    back, _ = rms_back(x_ref[...].astype(F32), gain_ref[0:1, :].astype(F32), total)
    grad_input_ref[...] = grad_resid_ref[...] + back


def whole_spec(array_shape):
    return pl.BlockSpec(array_shape, lambda i: (0,) * len(array_shape), pipeline_mode=pl.Buffered(1))


def call(kernel, grid, ins, outs, scratch, cost, name):
    arrays = [a for a, _ in ins]
    return pl.pallas_call(
        kernel,
        grid=grid,
        in_specs=[s for _, s in ins],
        out_specs=[s for _, _, s in outs],
        out_shape=[jax.ShapeDtypeStruct(s, d) for s, d, _ in outs],
        scratch_shapes=scratch,
        compiler_params=pltpu.CompilerParams(
            dimension_semantics=("arbitrary",), vmem_limit_bytes=VMEM_BYTES
        ),
        cost_estimate=pl.CostEstimate(flops=1, bytes_accessed=1, transcendentals=0),
        name=name,
    )(*arrays)


def after(value, *others):
    return lax.optimization_barrier((value,) + others)[0]


def shards(
    inputs, gain_attn, w_query, w_key, w_value, w_output, relative_bias_table,
    gain_ffn, w_inner, w_outer, lengths, cotangent, *, dp, tp,
):
    rows_n, width = inputs.shape
    groups = lengths.shape[0]
    passages = groups // tp
    seq = rows_n // passages
    cols = w_query.shape[1]
    heads = cols // HEAD_DIM
    hidden = w_inner.shape[1]
    me = lax.axis_index("dp")
    side = lax.axis_index("tensor")
    rest = dp // 4

    def across(value, distance):
        return lax.ppermute(value, "dp", [(i, i ^ distance) for i in range(dp)])

    def beside(value):
        return lax.ppermute(value, "tensor", [(i, tp - 1 - i) for i in range(tp)])

    def across_beside(value, distance):
        pairs = [(i * tp + t, (i ^ distance) * tp + tp - 1 - t) for i in range(dp) for t in range(tp)]
        return lax.ppermute(value, ("dp", "tensor"), pairs)

    quarter = me & 3

    def part(weight, axis=0):
        count = weight.shape[axis] // 4
        return lax.dynamic_slice_in_dim(weight, quarter * count, count, axis)

    wo_part = part(w_output)
    wo_part = jnp.concatenate([wo_part[:, :cols], wo_part[:, cols:]], axis=0)
    table = jnp.pad(relative_bias_table.T, ((0, 16 - heads), (0, 128 - BUCKETS)))
    qk_part = jnp.concatenate(
        [jnp.concatenate([part(w_query), part(w_key)], axis=1), jnp.pad(table, ((0, 0), (0, 2 * cols - 128)))], axis=0)
    vo_part = jnp.concatenate([part(w_value), wo_part], axis=1)
    qk_got, vo_got = beside(qk_part), beside(vo_part)
    inner_part = part(after(w_inner, qk_part, vo_part))
    numbers = jnp.concatenate([lengths, jnp.stack([me, side * passages]).astype(jnp.int32)])
    info = groups
    gains = jnp.stack([gain_attn, gain_ffn])

    smem = pl.BlockSpec(memory_space=pltpu.SMEM)
    anywhere = pl.BlockSpec(memory_space=pltpu.HBM)
    by_passage = lambda c: pl.BlockSpec((seq, c), lambda p: (p, 0))
    by_passage_t = pl.BlockSpec((width, seq), lambda p: (0, p))
    lse_spec = pl.BlockSpec((1, 8, seq), lambda p: (p, 0, 0))
    weight_spec = whole_spec((width, cols))
    table_spec = whole_spec((16, 128))
    gain_spec = whole_spec((2, width))
    perm_spec = whole_spec((width, width))
    small_rows = -(-width // 1024) * 8
    small_out = ((small_rows, 128), F32, whole_spec((small_rows, 128)))
    wo_spec = whole_spec((cols, width))
    qkv_outs = [((rows_n, cols), BF16, by_passage(cols))] * 4 + [((passages, 8, seq), F32, lse_spec)]
    bias_scratch = pltpu.VMEM((heads, seq, seq), F32)
    qkv_scratch = [pltpu.VMEM((width, cols), BF16)] * 3
    wo_scratch = pltpu.VMEM((cols, width), BF16)
    dma = pltpu.SemaphoreType.DMA
    cols_vmem = pltpu.VMEM((rows_n, cols), BF16)
    acc_hbm = ((rows_n, width), F32, anywhere)
    rows_hbm = ((rows_n, width), BF16, anywhere)
    turned_hbm = ((width, rows_n), BF16, anywhere)
    acc_vmem = pltpu.VMEM((rows_n, width), F32)
    rows_vmem = pltpu.VMEM((rows_n, width), BF16)
    turned_vmem = pltpu.VMEM((width, rows_n), BF16)
    attn_cost = 2 * rows_n * (width * 3 * cols + seq * 4 * cols)

    bits = [2**n for n in range(1, dp.bit_length() - 1)]
    upper = bits[1:]
    bits_in = upper[:2] + bits[:1] + upper[2:]
    rows_one, q_near, k_near, v_near, ctx_near, lse_near = call(
        functools.partial(attn_first_kernel, info=info), (passages,),
        [(after(numbers, qk_part, vo_part, inner_part), smem), (inputs, by_passage(width)), (gains, gain_spec),
         (w_query, weight_spec), (w_key, weight_spec), (w_value, weight_spec), (table, table_spec)],
        [((rows_n, width), BF16, by_passage(width))] + qkv_outs, [bias_scratch], attn_cost, "attn_first",
    )
    qk_got, vo_got = after(qk_got, rows_one), after(vo_got, rows_one)
    qk_second, vo_second = across(qk_got, 2), across(vo_got, 2)
    qk_core, vo_core = across(qk_got, 1), across(vo_got, 1)
    outer_part = part(after(w_outer, qk_got, vo_got))
    inner_got = beside(after(inner_part, qk_got, vo_got))
    rows_one_t, cot_t, perm, perm_in = call(
        functools.partial(turn_kernel, dp=dp, info=info, orders=([1] + bits, [1] + bits_in)), (passages,),
        [(after(numbers, qk_got, vo_got, outer_part), smem), (rows_one, by_passage(width)), (cotangent, by_passage(width))],
        [((width, rows_n), BF16, by_passage_t)] * 2 + [((width, width), BF16, perm_spec)] * 2,
        [], 4 * rows_n * width * width, "turn",
    )
    attn_pieces = [qk_got, qk_core, qk_second, across(after(qk_second, perm), 1)]
    attn_pieces += [vo_got, vo_core, vo_second, across(after(vo_second, perm), 1)]
    outer_got = beside(outer_part)
    inner_got = after(inner_got, perm)
    inner_second = across(inner_got, 2)
    inner_core = across(inner_got, 1)
    q_far, k_far, v_far, ctx_far, lse_far, residual, rows_two, rows_two_t, table_far = call(
        functools.partial(attn_second_kernel, seq=seq, info=info), (1,),
        [(after(numbers, inner_got), smem), (gains, gain_spec), (rows_one, anywhere), (inputs, anywhere),
         (ctx_near, anywhere), (perm_in, anywhere)] + [(a, anywhere) for a in attn_pieces]
        + [(w_output, anywhere)],
        [((rows_n, cols), BF16, anywhere)] * 4 + [((passages, 8, seq), F32, whole_spec((passages, 8, seq)))]
        + [acc_hbm, rows_hbm, turned_hbm, ((16, 128), BF16, table_spec)],
        [bias_scratch] + qkv_scratch + [wo_scratch, wo_scratch, rows_vmem, rows_vmem, cols_vmem]
        + [pltpu.VMEM((width, width), BF16)] + [cols_vmem] * 4 + [acc_vmem, rows_vmem, turned_vmem]
        + [dma((2,)), dma((6,)), dma((7 * passages,))], attn_cost, "attn_second",
    )

    block_hidden = 768 if hidden % 768 == 0 else hidden
    steps = hidden // block_hidden
    chunk_first, chunk_second, chunk_late = min(512, rows_n), rows_n, rows_n
    grad_out = ((width // 2, hidden), BF16, anywhere)
    hidden_vmem = pltpu.VMEM((rows_n, hidden), BF16)
    work_scratch = [rows_vmem] * 2 + [pltpu.VMEM((width, hidden), BF16), pltpu.VMEM((hidden, width), BF16)]
    work_scratch += [turned_vmem] * 2 + [acc_vmem] * 2 + [hidden_vmem] * 2
    work_scratch += [pltpu.VMEM((width // 2, hidden), BF16)] * 4
    ffn_cost = 12 * rows_n * width * hidden
    outer_got = after(outer_got, rows_two)
    outer_second = across(outer_got, 2)
    outer_core = across(outer_got, 1)
    inner_last = across(after(inner_second, rows_two), 1)
    ffn_near, back_near, in_send_near, out_send_near, in_keep_near, out_keep_near = call(
        functools.partial(ffn_first_kernel, chunk=chunk_first, block=block_hidden), (1,),
        [(after(rows_two, outer_got, inner_second, inner_core), anywhere), (cotangent, anywhere),
         (w_inner, anywhere), (w_outer, anywhere), (rows_two_t, anywhere), (cot_t, anywhere)],
        [acc_hbm, acc_hbm] + [grad_out] * 4,
        work_scratch + [dma((2 * (rows_n // chunk_first) + 2 * steps + 2,)), dma((4 * steps + 2,))], ffn_cost, "ffn_first",
    )
    ffn_pieces = [inner_got, inner_core, inner_second, inner_last]
    ffn_pieces += [outer_got, outer_core, outer_second, across(after(outer_second, ffn_near), 1)]

    def whole(array):
        return (array, 0, array.shape[0])

    def part_of(term, n, ways):
        array, which, rows = term
        return (array, which * ways + n, rows // ways)

    def cut(terms, ways=2):
        return [part_of(t, 0, ways) for t in terms], [[part_of(t, n, ways) for t in terms] for n in range(1, ways)]

    def total(terms):
        return sum(array[which * rows : (which + 1) * rows].astype(F32) for array, which, rows in terms)

    def add_up(*groups):
        return [total(terms).astype(BF16) for terms in groups]

    def distances(low_bits):
        return low_bits if len(low_bits) < 2 else [low_bits[1], low_bits[0], low_bits[0] + low_bits[1]]

    out_got_near = across(after(out_send_near, outer_second, inner_last, outer_core), 1)
    in_got_near = across(after(in_send_near, outer_second, inner_last, outer_core), 1)
    outer_near, sent = cut([whole(out_keep_near), whole(out_got_near)])
    inner_near, sent_in = cut([whole(in_keep_near), whole(in_got_near)])
    (outer_near_sent,) = add_up(sent[0])
    (inner_near_sent,) = add_up(sent_in[0])
    outer_near_got = across(outer_near_sent, 2)
    inner_near_got = across(inner_near_sent, bits_in[0])
    (
        layer_out, grad_residual, grad_attn, grad_attn_t, gain_two_part,
        in_send_far, out_send_far, in_keep_far, out_keep_far,
    ) = call(
        functools.partial(
            ffn_second_kernel, chunk=chunk_second, late_chunk=chunk_late, block=block_hidden, info=info), (1,),
        [(after(numbers, outer_near_sent, inner_near_sent), smem), (gains, gain_spec), (rows_two, anywhere),
         (cotangent, anywhere), (rows_two_t, anywhere), (cot_t, anywhere)]
        + [(a, anywhere) for a in ffn_pieces]
        + [(ffn_near, anywhere), (back_near, anywhere), (residual, anywhere), (perm, anywhere)],
        [rows_hbm, acc_hbm, rows_hbm, turned_hbm, small_out] + [grad_out] * 4,
        work_scratch + [acc_vmem] * 3 + [pltpu.VMEM((width, width), BF16)]
        + [rows_vmem, acc_vmem, rows_vmem, turned_vmem]
        + [dma((steps + 1,)), dma((2 * (rows_n // chunk_second) + 6,)),
           dma((4 * steps + 3 * (rows_n // chunk_late) + 1,))],
        ffn_cost, "ffn_second",
    )

    def attn_back(weights, q, k, v, lse, ctx, tab, order, name, vectors=()):
        half_shape = (width // 2, 4 * cols)
        far = not vectors
        sent_shape = half_shape if far else (width // 2, 4 * cols + 256)
        vector_spec = whole_spec((small_rows, 128))
        more_out = [] if far else [((4 * small_rows, 128), F32, whole_spec((4 * small_rows, 128)))]
        more_scratch = [] if far else [pltpu.VMEM((4 * small_rows, 256), BF16)]
        return call(
            functools.partial(attn_back_kernel, seq=seq, info=info, bits=[1] + bits, far=far), (1,),
            [(after(numbers, *order), smem)] + [(w, anywhere) for w in weights] + [(v, vector_spec) for v in vectors]
            + [(grad_attn, anywhere), (q, anywhere), (k, anywhere), (v, anywhere),
               (lse, whole_spec((passages, 8, seq))), (tab, table_spec), (rows_one_t, anywhere),
               (grad_attn_t, anywhere), (ctx, anywhere), (perm, anywhere), (gains, gain_spec)],
            [((rows_n, 3 * cols), BF16, anywhere), (sent_shape, BF16, anywhere)] + more_out
            + [(half_shape, BF16, anywhere), ((8, 128), F32, whole_spec((8, 128))), small_out],
            qkv_scratch + [wo_scratch, rows_vmem] + [cols_vmem] * 3 + [turned_vmem] * 2
            + [cols_vmem, pltpu.VMEM((width, width), BF16), pltpu.VMEM((rows_n, 3 * cols), BF16)]
            + [pltpu.VMEM(half_shape, BF16)] * 2 + [bias_scratch, pltpu.VMEM((heads, seq, seq), F32)]
            + [pltpu.VMEM((width, 3 * cols), F32), dma((4,)), dma((4 * passages + 4,)), dma((passages + 3,))]
            + more_scratch, 2 * rows_n * cols * (5 * width + 5 * seq), name,
        )

    def pack(values, rows):
        high = lax.reduce_precision(values, 8, 7)
        middle = lax.reduce_precision(values - high, 8, 7)
        parts = jnp.concatenate([high, middle], axis=1).astype(BF16)
        return jnp.pad(parts, ((0, rows - parts.shape[0]), (0, 0)))

    def unpack(block):
        return block[:, :128].astype(F32) + block[:, 128:].astype(F32)

    def finish(terms, left, *order):
        for bit in left:
            terms, sent = cut(terms)
            terms = terms + [whole(after(across(total(sent[0]).astype(BF16), bit), *order))]
        return total(terms)

    outer_near_got = after(outer_near_got, grad_attn)
    inner_near_got = after(inner_near_got, grad_attn)
    outer_near = outer_near + [whole(outer_near_got)]
    out_got_far = across(after(out_send_far, outer_near_got, inner_near_got), 1)
    in_got_far = across(after(in_send_far, outer_near_got, inner_near_got), 1)
    inner_near, sent_near = cut(inner_near + [whole(inner_near_got)])
    (inner_near_sent,) = add_up(sent_near[0])
    out_got_far = after(out_got_far, inner_near_sent)
    outer_far, sent = cut([whole(out_keep_far), whole(out_got_far)])
    inner_far, sent_in = cut([whole(in_keep_far), whole(in_got_far)])
    outer_far_sent, inner_far_sent = add_up(sent[0], sent_in[0])
    outer_far_got = across(outer_far_sent, 2)
    inner_far_got = across(inner_far_sent, bits_in[0])
    inner_near_got = across(inner_near_sent, bits_in[1])
    d_far, ag_send_far, ag_keep_far, table_part_far, gain_part_far = attn_back(
        attn_pieces, q_far, k_far, v_far, lse_far, ctx_far, table_far,
        [outer_far_sent, inner_far_sent, inner_near_sent], "attn_back_far",
    )
    outer_far_got = after(outer_far_got, d_far)
    inner_far_got = after(inner_far_got, d_far)
    inner_near_got = after(inner_near_got, d_far)
    ag_got_far = across(after(ag_send_far, outer_far_got, inner_far_got, inner_near_got), 1)
    outer_far = outer_far + [whole(outer_far_got)]
    inner_near = inner_near + [whole(inner_near_got)]
    inner_far, sent_in = cut(inner_far + [whole(inner_far_got)])
    outer_far_x, inner_far_sent = add_up(outer_far, sent_in[0])
    outer_x_got = beside(outer_far_x)
    inner_far_got = across(inner_far_sent, bits_in[1])
    attn_far, sent = cut([whole(ag_keep_far), whole(ag_got_far)])
    (attn_far_sent,) = add_up(sent[0])
    attn_far_got = across(attn_far_sent, 2)
    order = [outer_far_x, inner_far_sent, attn_far_sent]
    d_near, ag_send_near, vectors_own, ag_keep_near, _, _ = attn_back(
        [w_query, w_key, w_value, w_output], q_near, k_near, v_near, lse_near, ctx_near, table, order,
        "attn_back_near", (gain_two_part, gain_part_far, table_part_far),
    )
    attn_far_got = after(attn_far_got, d_near)
    inner_far_got = after(inner_far_got, d_near)
    outer_x_got = after(outer_x_got, d_near)
    ag_got_near = across(after(ag_send_near, attn_far_got, inner_far_got, outer_x_got), 1)
    vectors = vectors_own + unpack(ag_got_near[: 4 * small_rows, 4 * cols :])
    same = vectors + across(vectors, 2)
    outer, sent = cut(outer_near + [whole(outer_x_got)], 2 ** len(upper[:2]))
    outer_sent = add_up(*sent)
    block = pack(same, outer_sent[0].shape[0])
    outer_sent = [jnp.concatenate([v, block], axis=1) for v in outer_sent]
    outer_got = [across(v, d) for v, d in zip(outer_sent, distances(upper[:2]), strict=True)]
    far_x = jnp.concatenate(
        [total(attn_far + [whole(attn_far_got)]), total(inner_far + [whole(inner_far_got)])], axis=0).astype(BF16)
    far_x_got = beside(far_x)
    attn_near, sent = cut([whole(ag_keep_near), whole(ag_got_near[:, : 4 * cols])])
    (attn_near_sent,) = add_up(sent[0])
    attn_near_got = across(after(attn_near_sent, same), 2)
    order = [far_x, attn_near_sent] + outer_sent
    (grad_input,) = call(
        functools.partial(input_back_kernel, info=info), (passages,),
        [(after(numbers, *order), smem),
         (inputs, by_passage(width)), (gains, gain_spec), (grad_residual, by_passage(width)),
         (d_near, by_passage(3 * cols)), (d_far, by_passage(3 * cols)),
         (w_query, weight_spec), (w_key, weight_spec), (w_value, weight_spec)]
        + [(a, anywhere) for a in attn_pieces],
        [((rows_n, width), F32, by_passage(width))],
        qkv_scratch + [dma], 12 * rows_n * width * cols, "input_back",
    )
    far_x_got = after(far_x_got, grad_input)
    rows = attn_near_sent.shape[0]
    attn_near_got = after(attn_near_got, grad_input, far_x_got, *outer_got)
    attn, sent = cut(attn_near + [whole(attn_near_got), whole(far_x_got[:rows])], 2 ** len(upper[:2]))
    attn_sent = add_up(*sent)
    attn_got = [across(v, d) for v, d in zip(attn_sent, distances(upper[:2]), strict=True)]
    inner = inner_near + [whole(after(far_x_got, *attn_sent)[rows:])]
    grad_inner = finish(inner, bits_in[2:])
    outer_got = [after(got, *attn_sent) for got in outer_got]
    outer = outer + [whole(got[:, :hidden]) for got in outer_got]
    small = same + unpack(sum(got[: 4 * small_rows, hidden:].astype(F32) for got in outer_got))
    for bit in upper[2:]:
        small = small + across(small, bit)
    other = beside(small)
    table_at = 2 * small_rows
    small = jnp.concatenate(
        [small[:table_at] + other[:table_at], small[table_at : table_at + 8] + other[table_at + 8 :]], axis=0)
    grad_outer = finish(outer, upper[2:]).T
    attn_grads = finish(attn + [whole(after(got, grad_inner, grad_outer)) for got in attn_got], upper[2:])
    grad_query, grad_key, grad_value = (attn_grads[:, n * cols : (n + 1) * cols] for n in range(3))
    grad_output = attn_grads[:, 3 * cols :].T

    grad_gain_one = small[: width // 128].reshape(width)
    grad_gain_two = small[small_rows : small_rows + width // 128].reshape(width)
    grad_table = small[table_at : table_at + heads, :BUCKETS].T
    return (
        layer_out, grad_input, grad_gain_one, grad_query, grad_key, grad_value, grad_output,
        grad_table, grad_gain_two, grad_inner, grad_outer,
    )


def solution(mesh):
    both = ("dp", "tensor")
    in_specs = (
        P(both, None), P(), P(None, "tensor"), P(None, "tensor"), P(None, "tensor"), P("tensor", None),
        P(None, "tensor"), P(), P(None, "tensor"), P("tensor", None), P("dp"), P(both, None),
    )
    out_specs = (
        P(both, None), P(both, None), P(), P("dp", "tensor"), P("dp", "tensor"), P("dp", "tensor"),
        P("tensor", "dp"), P(None, "tensor"), P(), P("dp", "tensor"), P("tensor", "dp"),
    )
    body = functools.partial(shards, dp=mesh.shape["dp"], tp=mesh.shape["tensor"])
    return jax.shard_map(body, mesh=mesh, in_specs=in_specs, out_specs=out_specs, check_vma=False)
```

```python
import functools

import jax
import jax.numpy as jnp
from jax import lax
from jax.experimental import pallas as pl
from jax.experimental.pallas import tpu as pltpu
from jax.sharding import PartitionSpec as P

HEAD_DIM = 64
BUCKETS = 32
EPS = 1e-6
MASKED = -1e9
GELU_C = 0.7978845608028654
VMEM_BYTES = 50 * 1024 * 1024
F32 = jnp.float32
BF16 = jnp.bfloat16


def dot(left, right):
    return lax.dot_general(left, right, (((1,), (0,)), ((), ())), preferred_element_type=F32)


def dot_t(left, right):
    return lax.dot_general(left, right, (((1,), (1,)), ((), ())), preferred_element_type=F32)


def dot_l(left, right):
    return lax.dot_general(left, right, (((0,), (0,)), ((), ())), preferred_element_type=F32)


def staggered(count, first, second, third):
    for n in range(count + 2):
        if n < count:
            first(n)
        if 0 <= n - 1 < count:
            second(n - 1)
        if 0 <= n - 2 < count:
            third(n - 2)


def bucket_of(offsets):
    distance = jnp.abs(offsets)
    far = jnp.full_like(distance, 8)
    for power in range(1, 8):
        far = far + (distance * distance >= 64 * 2**power).astype(jnp.int32)
    near = jnp.where(distance < 8, distance, far)
    return near + jnp.where(offsets > 0, 16, 0)


def bucket_indicator(seq, count=BUCKETS):
    lane = lax.broadcasted_iota(jnp.int32, (count, 2 * seq), 1)
    offsets = jnp.where(lane < seq, -lane, 2 * seq - lane)
    ids = lax.broadcasted_iota(jnp.int32, (count, 2 * seq), 0)
    return (bucket_of(offsets) == ids).astype(F32)


def fill_bias(table_ref, bias_ref):
    heads, seq, _ = bias_ref.shape
    base = dot(table_ref[:, :BUCKETS], bucket_indicator(seq).astype(BF16))
    for h in range(heads):
        wide = jnp.broadcast_to(base[h : h + 1, :], (seq, 2 * seq))
        bias_ref[h] = pltpu.roll(wide, 0, 1, stride=1, stride_axis=0)[:, :seq]


def head_mask(columns, parity):
    lane = lax.broadcasted_iota(jnp.int32, columns.shape, 1)
    keep = (lane < HEAD_DIM) if parity == 0 else (lane >= HEAD_DIM)
    return jnp.where(keep, columns, jnp.zeros_like(columns))


def rms_rows(values, gain):
    return values * lax.rsqrt(jnp.mean(values * values, axis=-1, keepdims=True) + EPS) * gain


def add_row(ref, row):
    for n in range(row.shape[1] // 128):
        ref[n : n + 1, :] += row[:, n * 128 : (n + 1) * 128]


def rms_back(values, gain, grads):
    scale = lax.rsqrt(jnp.mean(values * values, axis=-1, keepdims=True) + EPS)
    scaled = grads * gain
    mean = jnp.mean(scaled * values, axis=-1, keepdims=True)
    back = scale * scaled - values * (scale * scale * scale * mean)
    return back, jnp.sum(grads * values * scale, axis=0, keepdims=True)


def fill_perm(perm_ref, me, dp, bits):
    width = perm_ref.shape[0]
    block = width // dp
    index = lax.broadcasted_iota(jnp.int32, (width, 128), 0)
    rel = lax.div(index, block)
    target = jnp.zeros_like(rel)
    for n, bit in enumerate(bits):
        target = target + ((rel >> (len(bits) - 1 - n)) & 1) * bit
    source = (target ^ me) * block + (index - rel * block)
    lane = lax.broadcasted_iota(jnp.int32, (width, 128), 1)
    for n in range(0, width, 128):
        perm_ref[:, n : n + 128] = jnp.where(source == lane + n, 1.0, 0.0).astype(BF16)


def piece_copies(packets, quarter, sem, routes):
    copies = []
    for pieces, ways in zip(packets, routes, strict=True):
        for n, piece in enumerate(pieces):
            for rows, cols, target, count, at in ways:
                start = pl.multiple_of((quarter ^ n) * count, 16)
                copies.append((piece.at[rows, cols], target.at[pl.ds(start, count), at], sem))
    return copies


def start_all(copies):
    for copy in copies:
        pltpu.make_async_copy(*copy).start()


def wait_all(copies):
    for copy in copies:
        pltpu.make_async_copy(*copy).wait()


def gather_pieces(packets, quarter, sem, routes):
    copies = piece_copies(packets, quarter, sem, routes)
    start_all(copies)
    wait_all(copies)


class Heads:
    def __init__(self, seq, heads, lengths, bias_ref, q_ref, k_ref, v_ref, ctx_ref, lse_ref):
        self.seq, self.heads, self.lengths = seq, heads, lengths
        self.bias_ref, self.lse_ref = bias_ref, lse_ref
        self.q_ref, self.k_ref, self.v_ref, self.ctx_ref = q_ref, k_ref, v_ref, ctx_ref
        self.first_head = lax.broadcasted_iota(jnp.int32, (seq, 2 * HEAD_DIM), 1) < HEAD_DIM
        self.key_slot = lax.broadcasted_iota(jnp.int32, (seq, 1), 0)
        self.query_t, self.logits, self.probs, self.parts = {}, {}, {}, {}

    def rows_of(self, p):
        return slice(p * self.seq, (p + 1) * self.seq)

    def pair_of(self, h):
        lo = (h // 2) * 2 * HEAD_DIM
        return slice(lo, lo + 2 * HEAD_DIM)

    def project(self, p, rows, wq_ref, wk_ref, wv_ref):
        query = dot(rows, wq_ref[...]).astype(BF16)
        self.q_ref[self.rows_of(p), :] = query
        self.k_ref[self.rows_of(p), :] = dot(rows, wk_ref[...]).astype(BF16)
        self.v_ref[self.rows_of(p), :] = dot(rows, wv_ref[...]).astype(BF16)
        self.query_t[p] = query.T

    def score(self, n):
        p, h = divmod(n, self.heads)
        both = self.pair_of(h)
        keys = head_mask(self.k_ref[self.rows_of(p), both], h % 2)
        self.logits[n] = dot(keys, self.query_t[p][both, :])

    def normalise(self, n):
        p, h = divmod(n, self.heads)
        valid = self.key_slot < self.lengths[p]
        biased = jnp.where(valid, self.logits.pop(n) + self.bias_ref[h], MASKED)
        peak = jnp.max(biased, axis=0, keepdims=True)
        terms = jnp.exp(biased - peak)
        total = jnp.sum(terms, axis=0, keepdims=True)
        self.probs[n] = (terms * (1.0 / total)).astype(BF16)
        self.lse_ref[p, h : h + 1, :] = peak + jnp.log(total)

    def combine(self, n):
        p, h = divmod(n, self.heads)
        self.parts[n] = dot_l(self.probs.pop(n), self.v_ref[self.rows_of(p), self.pair_of(h)])
        if h % 2:
            both = jnp.where(self.first_head, self.parts.pop(n - 1), self.parts.pop(n))
            self.ctx_ref[self.rows_of(p), self.pair_of(h)] = both.astype(BF16)


def attn_first_kernel(
    len_ref, x_ref, gain_ref, wq_ref, wk_ref, wv_ref, table_ref,
    rows_ref, q_ref, k_ref, v_ref, ctx_ref, lse_ref, bias_ref, *, info,
):
    p = pl.program_id(0)
    seq = rows_ref.shape[0]

    @pl.when(p == 0)
    def _():
        fill_bias(table_ref, bias_ref)

    rows = rms_rows(x_ref[...].astype(F32), gain_ref[0:1, :].astype(F32)).astype(BF16)
    rows_ref[...] = rows
    lengths = [len_ref[len_ref[info + 1] + p]]
    work = Heads(seq, bias_ref.shape[0], lengths, bias_ref, q_ref, k_ref, v_ref, ctx_ref, lse_ref)
    work.project(0, rows, wq_ref, wk_ref, wv_ref)
    staggered(work.heads, work.score, work.normalise, work.combine)


def turn_kernel(
    len_ref, rows_ref, cot_ref, rows_t_ref, cot_t_ref, perm_ref, perm_in_ref, *, dp, info, orders,
):
    @pl.when(pl.program_id(0) == 0)
    def _():
        fill_perm(perm_ref, len_ref[info], dp, orders[0])
        fill_perm(perm_in_ref, len_ref[info], dp, orders[1])

    rows_t_ref[...] = dot_t(perm_ref[...], rows_ref[...]).astype(BF16)
    cot_t_ref[...] = dot_t(perm_ref[...], cot_ref[...]).astype(BF16)


def projection_routes(piece_rows, cols, targets):
    rows = slice(0, piece_rows)
    return [
        (rows, slice(n * cols, (n + 1) * cols), target, piece_rows, slice(0, cols))
        for n, target in enumerate(targets)
    ]


def output_routes(piece_rows, cols, target):
    half, lanes = piece_rows // 2, slice(cols, 2 * cols)
    return [
        (slice(0, half), lanes, target, half, slice(0, cols)),
        (slice(half, piece_rows), lanes, target, half, slice(cols, 2 * cols)),
    ]


def attn_second_kernel(len_ref, gain_ref, rows_hbm, x_hbm, ctx_first_hbm, perm_hbm, *refs, seq, info):
    qk_pieces, vo_pieces = refs[:4], refs[4:8]
    (
        wo_first_hbm, q_hbm, k_hbm, v_hbm, ctx_hbm, lse_ref, resid_hbm, rows_two_hbm, rows_two_t_hbm, table_ref,
        bias_ref, wq_ref, wk_ref, wv_ref, wo_ref, wo_first_ref, rows_ref, x_ref, ctx_first_ref, perm_ref,
        q_ref, k_ref, v_ref, ctx_ref, resid_ref, rows_two_ref, rows_two_t_ref, piece_sem, in_sems, out_sems,
    ) = refs[8:]
    rows, cols = wq_ref.shape[0] // 4, wq_ref.shape[1]
    heads = bias_ref.shape[0]
    passages = q_ref.shape[0] // seq
    quarter = len_ref[info] & 3
    get_table = [(qk_pieces[0].at[rows : rows + 16, :128], table_ref, in_sems.at[0])]
    projections = piece_copies(
        (qk_pieces, vo_pieces), quarter, piece_sem.at[0],
        [projection_routes(rows, cols, (wq_ref, wk_ref)), projection_routes(rows, cols, (wv_ref,))],
    )
    get_rows = [(rows_hbm, rows_ref, in_sems.at[1])]
    output = piece_copies((vo_pieces,), quarter, piece_sem.at[1], [output_routes(rows, cols, wo_ref)])
    output += [
        (wo_first_hbm, wo_first_ref, in_sems.at[2]), (ctx_first_hbm, ctx_first_ref, in_sems.at[3]),
        (x_hbm, x_ref, in_sems.at[4]), (perm_hbm, perm_ref, in_sems.at[5]),
    ]
    start_all(get_table + get_rows + projections + output)
    wait_all(get_table)
    fill_bias(table_ref, bias_ref)
    wait_all(get_rows + projections)
    lengths = [len_ref[len_ref[info + 1] + p] for p in range(passages)]
    work = Heads(seq, heads, lengths, bias_ref, q_ref, k_ref, v_ref, ctx_ref, lse_ref)
    out = []

    def put(ref, hbm, at, sem):
        copy = (ref.at[at], hbm.at[at], out_sems.at[sem])
        out.append(copy)
        start_all([copy])

    def project(p):
        here = work.rows_of(p)
        work.project(p, rows_ref[here, :], wq_ref, wk_ref, wv_ref)
        for n, (ref, hbm) in enumerate(((q_ref, q_hbm), (k_ref, k_hbm), (v_ref, v_hbm))):
            put(ref, hbm, (here, slice(None)), 7 * p + n)

    def branch(p):
        here = work.rows_of(p)
        if p == 0:
            wait_all(output)
        total = dot(ctx_first_ref[here, :], wo_first_ref[...]) + dot(ctx_ref[here, :], wo_ref[...])
        residual = x_ref[here, :].astype(F32) + total
        resid_ref[here, :] = residual
        rows_two_ref[here, :] = rms_rows(residual, gain_ref[1:2, :].astype(F32)).astype(BF16)
        pairs = ((ctx_ref, ctx_hbm), (resid_ref, resid_hbm), (rows_two_ref, rows_two_hbm))
        for n, (ref, hbm) in enumerate(pairs):
            put(ref, hbm, (here, slice(None)), 7 * p + 3 + n)

    def turn(p):
        here = work.rows_of(p)
        rows_two_t_ref[:, here] = dot_t(perm_ref[...], rows_two_ref[here, :]).astype(BF16)
        put(rows_two_t_ref, rows_two_t_hbm, (slice(None), here), 7 * p + 6)

    for p in range(passages):
        project(p)
    count = passages * heads
    for n in range(count + 2):
        if n < count:
            work.score(n)
        if 0 <= n - 1 < count:
            work.normalise(n - 1)
        if 0 <= n - 2 < count:
            work.combine(n - 2)
        done = (n - 2) // heads
    for p in range(passages):
        branch(p)
    for p in range(passages):
        turn(p)
    wait_all(out)


class Hidden:
    def __init__(self, refs, weight_refs, weight_hbms, sems, chunk, block):
        (
            self.rows_ref, self.cot_ref, self.wi_ref, self.wo_ref, self.rows_t_ref, self.cot_t_ref, self.ffn_ref,
            self.back_ref, self.act_ref, self.grad_ref,
        ) = refs
        self.weight_refs, self.weight_hbms, self.sems = weight_refs, weight_hbms, sems
        self.chunk, self.block = chunk, block
        self.chunks = self.rows_ref.shape[0] // chunk
        self.blocks = self.wi_ref.shape[1] // block
        self.out = []

    def rows_of(self, i):
        return slice(i * self.chunk, (i + 1) * self.chunk)

    def hidden(self, b, ready):
        units = slice(b * self.block, (b + 1) * self.block)

        def first(i):
            at = self.rows_of(i)
            ready(b, i, 0)
            v = dot(self.rows_ref[at, :], self.wi_ref[:, units])
            ready(b, i, 1)
            grad_act = dot_t(self.cot_ref[at, :], self.wo_ref[units, :])
            square = v * v
            tanh = jnp.tanh(GELU_C * v * (1.0 + 0.044715 * square))
            half = 0.5 + 0.5 * tanh
            self.act_ref[at, units] = (v * half).astype(BF16)
            slope = half + (0.5 * GELU_C) * v * (1.0 - tanh * tanh) * (1.0 + 0.134145 * square)
            self.grad_ref[at, units] = (grad_act * slope).astype(BF16)

        def second(i):
            at = self.rows_of(i)
            forward = dot(self.act_ref[at, units], self.wo_ref[units, :])
            backward = dot_t(self.grad_ref[at, units], self.wi_ref[:, units])
            if b:
                self.ffn_ref[at, :] += forward
                self.back_ref[at, :] += backward
            else:
                self.ffn_ref[at, :] = forward
                self.back_ref[at, :] = backward

        staggered(self.chunks, first, second, lambda i: None)

    def weights(self, b, which):
        units = slice(b * self.block, (b + 1) * self.block)
        ref = self.weight_refs[which]
        half_rows = ref.shape[0]
        at = slice(half_rows, None) if which < 2 else slice(half_rows)
        left, right = ((self.rows_t_ref, self.grad_ref), (self.cot_t_ref, self.act_ref))[which % 2]
        ref[:, units] = dot(left[at, :], right[:, units]).astype(BF16)
        self.put(ref, self.weight_hbms[which], (slice(None), units))

    def put(self, ref, hbm, at):
        self.out.append((ref.at[at], hbm.at[at], self.sems.at[len(self.out)]))
        start_all(self.out[-1:])


def ffn_first_kernel(rows_hbm, cot_hbm, wi_hbm, wo_hbm, rows_t_hbm, cot_t_hbm, ffn_hbm, back_hbm, *refs, chunk, block):
    weight_hbms, work_refs, weight_refs, in_sems, out_sems = refs[:4], refs[4:14], refs[14:18], refs[18], refs[19]
    work = Hidden(work_refs, weight_refs, weight_hbms, out_sems, chunk, block)
    copies = {}

    def get(key, hbm, ref, at):
        copies[key] = [(hbm.at[at], ref.at[at], in_sems.at[len(copies)])]
        start_all(copies[key])

    everything = slice(None)

    def get_weights(b):
        units = slice(b * block, (b + 1) * block)
        get(("weight", b, 0), wi_hbm, work.wi_ref, (everything, units))
        get(("weight", b, 1), wo_hbm, work.wo_ref, (units, everything))

    def get_rows(i):
        get(("rows", i, 0), rows_hbm, work.rows_ref, (work.rows_of(i), everything))
        get(("rows", i, 1), cot_hbm, work.cot_ref, (work.rows_of(i), everything))

    def ready(b, i, which):
        if i == 0:
            wait_all(copies["weight", b, which])
        if b == 0:
            wait_all(copies["rows", i, which])
        if b == 0 and i == 0 and which == 1:
            for n in range(1, work.blocks):
                get_weights(n)
            get("turned rows", rows_t_hbm, work.rows_t_ref, (everything, everything))
            get("turned cot", cot_t_hbm, work.cot_t_ref, (everything, everything))

    get_rows(0)
    get_weights(0)
    for i in range(1, work.chunks):
        get_rows(i)
    for b in range(work.blocks):
        work.hidden(b, ready)
        if b == 0:
            wait_all(copies["turned rows"] + copies["turned cot"])
        if b == work.blocks - 1:
            work.put(work.ffn_ref, ffn_hbm, (everything, everything))
            work.put(work.back_ref, back_hbm, (everything, everything))
        for which in range(4):
            work.weights(b, which)
    wait_all(work.out)


def ffn_second_kernel(
    info_ref, gain_ref, rows_hbm, cot_hbm, rows_t_hbm, cot_t_hbm, *refs, chunk, late_chunk, block, info,
):
    inner_pieces, outer_pieces = refs[:4], refs[4:8]
    (
        ffn_in_hbm, back_in_hbm, resid_hbm, perm_hbm,
        layer_hbm, grad_resid_hbm, grad_attn_hbm, grad_attn_t_hbm, gain_grad_ref,
    ) = refs[8:17]
    weight_hbms, work_refs, weight_refs = refs[17:21], refs[21:31], refs[31:35]
    (
        ffn_in_ref, back_in_ref, resid_ref, perm_ref, layer_ref, grad_resid_ref, grad_attn_ref, grad_attn_t_ref,
        piece_sems, in_sems, out_sems,
    ) = refs[35:]
    work = Hidden(work_refs, weight_refs, weight_hbms, out_sems, chunk, block)
    width, hidden = work.wi_ref.shape
    wi_rows, wo_rows = width // 4, hidden // 4
    quarter = info_ref[info] & 3
    everything = slice(None)
    inner = [
        piece_copies(
            (inner_pieces,), quarter, piece_sems.at[b],
            [[(slice(0, wi_rows), slice(b * block, (b + 1) * block), work.wi_ref, wi_rows,
               slice(b * block, (b + 1) * block))]],
        )
        for b in range(work.blocks)
    ]
    outer = piece_copies(
        (outer_pieces,), quarter, piece_sems.at[work.blocks],
        [[(slice(0, wo_rows), slice(0, width), work.wo_ref, wo_rows, slice(0, width))]],
    )
    rows_in = []
    for i in range(work.chunks):
        at = (work.rows_of(i), everything)
        rows_in.append([
            (rows_hbm.at[at], work.rows_ref.at[at], in_sems.at[2 * i]),
            (cot_hbm.at[at], work.cot_ref.at[at], in_sems.at[2 * i + 1]),
        ])
    base = 2 * work.chunks
    turned = [(rows_t_hbm, work.rows_t_ref, in_sems.at[base]), (cot_t_hbm, work.cot_t_ref, in_sems.at[base + 1])]
    late = [
        (back_in_hbm, back_in_ref, in_sems.at[base + 2]), (resid_hbm, resid_ref, in_sems.at[base + 3]),
        (ffn_in_hbm, ffn_in_ref, in_sems.at[base + 4]), (perm_hbm, perm_ref, in_sems.at[base + 5]),
    ]

    def ready(b, i, which):
        if i == 0 and which == 0:
            wait_all(inner[b])
        if i == 0 and b == 0 and which == 1:
            wait_all(outer)
        if b == 0:
            wait_all(rows_in[i][which : which + 1])
        if b == 0 and i == 0 and which == 1:
            for n in range(1, work.blocks):
                start_all(inner[n])
            start_all(turned)

    start_all(rows_in[0][:1] + inner[0] + rows_in[0][1:] + outer)
    for i in range(1, work.chunks):
        start_all(rows_in[i])
    last = work.blocks - 1
    for b in range(work.blocks):
        if b == last:
            start_all(late)
        work.hidden(b, ready)
        if b == 0:
            wait_all(turned)
        if b < last:
            for which in range(4):
                work.weights(b, which)
    wait_all(late)
    gain_grad_ref[...] = jnp.zeros_like(gain_grad_ref)
    count = resid_ref.shape[0] // late_chunk
    for i in range(count):
        at = slice(i * late_chunk, (i + 1) * late_chunk)
        residual = resid_ref[at, :]
        back, gain_part = rms_back(residual, gain_ref[1:2, :].astype(F32), work.back_ref[at, :] + back_in_ref[at, :])
        add_row(gain_grad_ref, gain_part)
        grad_resid = work.cot_ref[at, :].astype(F32) + back
        grad_resid_ref[at, :] = grad_resid
        grad_attn_ref[at, :] = grad_resid.astype(BF16)
        layer_ref[at, :] = (residual + (work.ffn_ref[at, :] + ffn_in_ref[at, :])).astype(BF16)
        if i < 3:
            work.weights(last, i)
        for ref, hbm in ((grad_attn_ref, grad_attn_hbm), (grad_resid_ref, grad_resid_hbm), (layer_ref, layer_hbm)):
            work.put(ref, hbm, (at, everything))
    grad_attn_t_ref[...] = dot_t(perm_ref[...], grad_attn_ref[...]).astype(BF16)
    work.put(grad_attn_t_ref, grad_attn_t_hbm, (everything, everything))
    for which in range(min(count, 3), 4):
        work.weights(last, which)
    wait_all(work.out)


def gain_from_weights(me, bits, w_refs, grads, perm_ref, gain_ref, out_ref):
    width, cols = w_refs[0].shape
    block = width // (2 ** len(bits))
    if block % 16:
        weights = [dot(perm_ref[...], ref[...]) for ref in w_refs]
    else:
        weights = []
        for ref in w_refs:
            rows = []
            for n in range(width // block):
                target = sum(bit for m, bit in enumerate(bits) if (n >> (len(bits) - 1 - m)) & 1)
                rows.append(ref[pl.ds(pl.multiple_of((me ^ target) * block, 16), block), :])
            weights.append(jnp.concatenate(rows, axis=0).astype(F32))
    folded = None
    for n, weight in enumerate(weights):
        for lo in range(0, cols, 128):
            term = weight[:, lo : lo + 128] * grads[:, n * cols + lo : n * cols + lo + 128]
            folded = term if folded is None else folded + term
    ordered = jnp.sum(folded.T, axis=0, keepdims=True)
    high = ordered.astype(BF16)
    middle = (ordered - high.astype(F32)).astype(BF16)
    low = (ordered - high.astype(F32) - middle.astype(F32)).astype(BF16)
    parts = jnp.concatenate([high, middle, low, jnp.zeros((13, width), BF16)], axis=0)
    natural = jnp.sum(dot(parts, perm_ref[...]), axis=0, keepdims=True) / gain_ref[0:1, :].astype(F32)
    out_ref[...] = jnp.zeros_like(out_ref)
    add_row(out_ref, natural)


def attn_back_kernel(len_ref, *refs, seq, info, bits, far):
    if far:
        qk_pieces, vo_pieces, refs = refs[:4], refs[4:8], refs[8:]
    else:
        weights_hbm, vector_refs, own_ref, block_ref = refs[:4], refs[4:7], refs[20], refs[-1]
        refs = refs[7:20] + refs[21:-1]
    (
        grad_attn_hbm, q_hbm, k_hbm, v_hbm, lse_ref, table_ref, rows_t_hbm, grad_attn_t_hbm, ctx_hbm, perm_hbm,
        gain_ref, dqkv_hbm, send_hbm, keep_hbm, table_grad_ref, gain_grad_ref,
        wq_ref, wk_ref, wv_ref, wo_ref, grad_attn_ref, q_ref, k_ref, v_ref, rows_t_ref, grad_attn_t_ref, ctx_ref,
        perm_ref, dqkv_ref, send_ref, keep_ref, bias_ref, sums_ref, grads_ref, piece_sem, in_sems, out_sems,
    ) = refs
    heads = bias_ref.shape[0]
    cols = heads * HEAD_DIM
    passages = q_ref.shape[0] // seq
    half_rows = keep_ref.shape[0]

    def rows_of(p):
        return slice(p * seq, (p + 1) * seq)

    if far:
        rows = wq_ref.shape[0] // 4
        quarter = len_ref[info] & 3
        late_weights = piece_copies(
            (qk_pieces, vo_pieces), quarter, piece_sem.at[0],
            [projection_routes(rows, cols, (wq_ref, wk_ref)), projection_routes(rows, cols, (wv_ref,))],
        )
        output = piece_copies((vo_pieces,), quarter, piece_sem.at[1], [output_routes(rows, cols, wo_ref)])
    else:
        late_weights = [
            (hbm, ref, piece_sem.at[n])
            for n, (hbm, ref) in enumerate(zip(weights_hbm, (wq_ref, wk_ref, wv_ref), strict=False))
        ]
        output = [(weights_hbm[3], wo_ref, piece_sem.at[3])]
    start_all(output)
    by_passage = []
    for p in range(passages):
        pairs = ((grad_attn_hbm, grad_attn_ref), (q_hbm, q_ref), (k_hbm, k_ref), (v_hbm, v_ref))
        by_passage.append(
            [(hbm.at[rows_of(p), :], ref.at[rows_of(p), :], in_sems.at[4 * p + n]) for n, (hbm, ref) in enumerate(pairs)]
        )
    start_all(by_passage[0])
    at = 4 * passages
    turned = [(ctx_hbm, ctx_ref, in_sems.at[at]), (grad_attn_t_hbm, grad_attn_t_ref, in_sems.at[at + 1])]
    last = [(rows_t_hbm, rows_t_ref, in_sems.at[at + 2]), (perm_hbm, perm_ref, in_sems.at[at + 3])]
    fill_bias(table_ref, bias_ref)
    sums_ref[...] = jnp.zeros_like(sums_ref)
    wait_all(output)
    first_head = lax.broadcasted_iota(jnp.int32, (seq, 2 * HEAD_DIM), 1) < HEAD_DIM
    key_slot = lax.broadcasted_iota(jnp.int32, (seq, 1), 0)
    ready, scores, weights, dq, dk, dv = {}, {}, {}, {}, {}, {}

    def pair_of(h, offset=0):
        lo = (h // 2) * 2 * HEAD_DIM + offset
        return slice(lo, lo + 2 * HEAD_DIM)

    def prepare(p):
        wait_all(by_passage[p])
        grad_ctx = dot_t(grad_attn_ref[rows_of(p), :], wo_ref[...]).astype(BF16)
        valid = key_slot < len_ref[len_ref[info + 1] + p]
        ready[p] = (
            grad_ctx, grad_ctx.T, q_ref[rows_of(p), :].T, k_ref[rows_of(p), :].T, valid,
        )

    def score(n):
        p, h = divmod(n, heads)
        _, grad_ctx_t, query_t, _, _ = ready[p]
        both = pair_of(h)
        scores[n] = (
            dot(head_mask(k_ref[rows_of(p), both], h % 2), query_t[both, :]),
            dot(head_mask(v_ref[rows_of(p), both], h % 2), grad_ctx_t[both, :]),
        )

    def soften(n):
        p, h = divmod(n, heads)
        logits, grad_probs = scores.pop(n)
        probs = jnp.exp(logits + bias_ref[h] - lse_ref[p, h : h + 1, :])
        probs = jnp.where(ready[p][4], probs, 0.0)
        mixed = jnp.sum(probs * grad_probs, axis=0, keepdims=True)
        grads = (probs * (grad_probs - mixed)).astype(BF16)
        sums_ref[h] += grads.astype(F32)
        weights[n] = (probs.astype(BF16), grads)

    def combine(n):
        p, h = divmod(n, heads)
        grad_ctx, _, _, keys_t, _ = ready[p]
        probs, grads = weights.pop(n)
        dq[n] = dot(keys_t[h * HEAD_DIM : (h + 1) * HEAD_DIM, :], grads)
        dk[n] = dot(grads, q_ref[rows_of(p), pair_of(h)])
        dv[n] = dot(probs, grad_ctx[:, pair_of(h)])
        if h % 2:
            dqkv_ref[rows_of(p), pair_of(h, cols)] = jnp.where(first_head, dk.pop(n - 1), dk.pop(n)).astype(BF16)
            dqkv_ref[rows_of(p), pair_of(h, 2 * cols)] = jnp.where(first_head, dv.pop(n - 1), dv.pop(n)).astype(BF16)
        if h == heads - 1:
            parts = jnp.concatenate([dq.pop(m) for m in range(n - h, n + 1)], axis=0)
            dqkv_ref[rows_of(p), :cols] = parts.astype(BF16).T
            copy = (dqkv_ref.at[rows_of(p), :], dqkv_hbm.at[rows_of(p), :], out_sems.at[p])
            out.append(copy)
            start_all([copy])

    out = []
    count = passages * heads
    for p in range(1, passages):
        start_all(by_passage[p])
    start_all(turned)
    for p in range(passages):
        prepare(p)
    for n in range(count + 2):
        if n == heads:
            start_all(last + late_weights)
        if n < count:
            score(n)
        if 0 <= n - 1 < count:
            soften(n - 1)
        if 0 <= n - 2 < count:
            combine(n - 2)
        if n == heads:
            wait_all(turned)
            send_ref[:, 3 * cols :] = dot(grad_attn_t_ref[half_rows:, :], ctx_ref[...]).astype(BF16)
        if n == heads + 2:
            keep_ref[:, 3 * cols :] = dot(grad_attn_t_ref[:half_rows, :], ctx_ref[...]).astype(BF16)
    wait_all(last)
    for ref, hbm, at, sem in (
        (send_ref, send_hbm, slice(half_rows, None), passages), (keep_ref, keep_hbm, slice(half_rows), passages + 1),
    ):
        grads_ref[at, :] = dot(rows_t_ref[at, :], dqkv_ref[...])
        ref[:, : 3 * cols] = grads_ref[at, :].astype(BF16)
        copy = (ref, hbm.at[:, : 4 * cols], out_sems.at[sem])
        out.append(copy)
        start_all([copy])
    wait_all(late_weights)
    gain_from_weights(
        len_ref[info], bits, (wq_ref, wk_ref, wv_ref), grads_ref, perm_ref, gain_ref, gain_grad_ref
    )
    rows = []
    for h in range(heads):
        folded = jnp.zeros((8, 2 * seq), F32)
        for a in range(0, seq, 8):
            wide = jnp.concatenate([sums_ref[h, a : a + 8, :], jnp.zeros((8, seq), F32)], axis=1)
            folded = folded + (pltpu.roll(wide, 2 * seq - a, 1) if a else wide)
        diagonals = folded[0:1, :]
        for b in range(1, 8):
            diagonals = diagonals + pltpu.roll(folded[b : b + 1, :], 2 * seq - b, 1)
        rows.append(diagonals)
    rows.append(jnp.zeros((8 - heads, 2 * seq), F32))
    table_grad_ref[...] = lax.dot_general(
        jnp.concatenate(rows, axis=0), bucket_indicator(seq, 128), (((1,), (1,)), ((), ())),
        precision=lax.Precision.HIGHEST, preferred_element_type=F32,
    )
    if not far:
        gain_two_ref, gain_far_ref, table_far_ref = vector_refs
        own = jnp.concatenate(
            [gain_grad_ref[...] + gain_far_ref[...], gain_two_ref[...], table_grad_ref[...], table_far_ref[...]], axis=0)
        own_ref[...] = own
        high = own.astype(BF16)
        middle = (own - high.astype(F32)).astype(BF16)
        block_ref[...] = jnp.concatenate([high, middle], axis=1)
        rows, lanes = block_ref.shape
        out.append(
            (block_ref, send_hbm.at[:rows, 4 * cols : 4 * cols + lanes], out_sems.at[passages + 2])
        )
        start_all(out[-1:])
    wait_all(out)


def input_back_kernel(
    info_ref, x_ref, gain_ref, grad_resid_ref, d_first_ref, d_second_ref,
    wq_first_ref, wk_first_ref, wv_first_ref, *refs, info,
):
    qk_pieces, vo_pieces = refs[:4], refs[4:8]
    grad_input_ref, wq_ref, wk_ref, wv_ref, sem = refs[8:]

    @pl.when(pl.program_id(0) == 0)
    def _():
        rows, cols = wq_ref.shape[0] // 4, wq_ref.shape[1]
        gather_pieces(
            (qk_pieces, vo_pieces), info_ref[info] & 3, sem,
            [projection_routes(rows, cols, (wq_ref, wk_ref)), projection_routes(rows, cols, (wv_ref,))],
        )

    width = wq_ref.shape[1]
    total = None
    for d_ref, refs in (
        (d_first_ref, (wq_first_ref, wk_first_ref, wv_first_ref)),
        (d_second_ref, (wq_ref, wk_ref, wv_ref)),
    ):
        for n, ref in enumerate(refs):
            term = dot_t(d_ref[:, n * width : (n + 1) * width], ref[...])
            total = term if total is None else total + term
    back, _ = rms_back(x_ref[...].astype(F32), gain_ref[0:1, :].astype(F32), total)
    grad_input_ref[...] = grad_resid_ref[...] + back


def whole_spec(array_shape):
    return pl.BlockSpec(array_shape, lambda i: (0,) * len(array_shape), pipeline_mode=pl.Buffered(1))


def call(kernel, grid, ins, outs, scratch, cost, name):
    arrays = [a for a, _ in ins]
    return pl.pallas_call(
        kernel,
        grid=grid,
        in_specs=[s for _, s in ins],
        out_specs=[s for _, _, s in outs],
        out_shape=[jax.ShapeDtypeStruct(s, d) for s, d, _ in outs],
        scratch_shapes=scratch,
        compiler_params=pltpu.CompilerParams(
            dimension_semantics=("arbitrary",), vmem_limit_bytes=VMEM_BYTES
        ),
        cost_estimate=pl.CostEstimate(flops=1, bytes_accessed=1, transcendentals=0),
        name=name,
    )(*arrays)


def after(value, *others):
    return lax.optimization_barrier((value,) + others)[0]


def shards(
    inputs, gain_attn, w_query, w_key, w_value, w_output, relative_bias_table,
    gain_ffn, w_inner, w_outer, lengths, cotangent, *, dp, tp,
):
    rows_n, width = inputs.shape
    groups = lengths.shape[0]
    passages = groups // tp
    seq = rows_n // passages
    cols = w_query.shape[1]
    heads = cols // HEAD_DIM
    hidden = w_inner.shape[1]
    me = lax.axis_index("dp")
    side = lax.axis_index("tensor")
    rest = dp // 4

    def across(value, distance):
        return lax.ppermute(value, "dp", [(i, i ^ distance) for i in range(dp)])

    def beside(value):
        return lax.ppermute(value, "tensor", [(i, tp - 1 - i) for i in range(tp)])

    def across_beside(value, distance):
        pairs = [(i * tp + t, (i ^ distance) * tp + tp - 1 - t) for i in range(dp) for t in range(tp)]
        return lax.ppermute(value, ("dp", "tensor"), pairs)

    quarter = me & 3

    def part(weight, axis=0):
        count = weight.shape[axis] // 4
        return lax.dynamic_slice_in_dim(weight, quarter * count, count, axis)

    wo_part = part(w_output)
    wo_part = jnp.concatenate([wo_part[:, :cols], wo_part[:, cols:]], axis=0)
    table = jnp.pad(relative_bias_table.T, ((0, 16 - heads), (0, 128 - BUCKETS)))
    qk_part = jnp.concatenate(
        [jnp.concatenate([part(w_query), part(w_key)], axis=1), jnp.pad(table, ((0, 0), (0, 2 * cols - 128)))], axis=0)
    vo_part = jnp.concatenate([part(w_value), wo_part], axis=1)
    qk_got, vo_got = beside(qk_part), beside(vo_part)
    inner_part = part(after(w_inner, qk_part, vo_part))
    numbers = jnp.concatenate([lengths, jnp.stack([me, side * passages]).astype(jnp.int32)])
    info = groups
    gains = jnp.stack([gain_attn, gain_ffn])

    smem = pl.BlockSpec(memory_space=pltpu.SMEM)
    anywhere = pl.BlockSpec(memory_space=pltpu.HBM)
    by_passage = lambda c: pl.BlockSpec((seq, c), lambda p: (p, 0))
    by_passage_t = pl.BlockSpec((width, seq), lambda p: (0, p))
    lse_spec = pl.BlockSpec((1, 8, seq), lambda p: (p, 0, 0))
    weight_spec = whole_spec((width, cols))
    table_spec = whole_spec((16, 128))
    gain_spec = whole_spec((2, width))
    perm_spec = whole_spec((width, width))
    small_rows = -(-width // 1024) * 8
    small_out = ((small_rows, 128), F32, whole_spec((small_rows, 128)))
    wo_spec = whole_spec((cols, width))
    qkv_outs = [((rows_n, cols), BF16, by_passage(cols))] * 4 + [((passages, 8, seq), F32, lse_spec)]
    bias_scratch = pltpu.VMEM((heads, seq, seq), F32)
    qkv_scratch = [pltpu.VMEM((width, cols), BF16)] * 3
    wo_scratch = pltpu.VMEM((cols, width), BF16)
    dma = pltpu.SemaphoreType.DMA
    cols_vmem = pltpu.VMEM((rows_n, cols), BF16)
    acc_hbm = ((rows_n, width), F32, anywhere)
    rows_hbm = ((rows_n, width), BF16, anywhere)
    turned_hbm = ((width, rows_n), BF16, anywhere)
    acc_vmem = pltpu.VMEM((rows_n, width), F32)
    rows_vmem = pltpu.VMEM((rows_n, width), BF16)
    turned_vmem = pltpu.VMEM((width, rows_n), BF16)
    attn_cost = 2 * rows_n * (width * 3 * cols + seq * 4 * cols)

    bits = [2**n for n in range(1, dp.bit_length() - 1)]
    upper = bits[1:]
    bits_in = upper[:2] + bits[:1] + upper[2:]
    rows_one, q_near, k_near, v_near, ctx_near, lse_near = call(
        functools.partial(attn_first_kernel, info=info), (passages,),
        [(after(numbers, qk_part, vo_part, inner_part), smem), (inputs, by_passage(width)), (gains, gain_spec),
         (w_query, weight_spec), (w_key, weight_spec), (w_value, weight_spec), (table, table_spec)],
        [((rows_n, width), BF16, by_passage(width))] + qkv_outs, [bias_scratch], attn_cost, "attn_first",
    )
    qk_got, vo_got = after(qk_got, rows_one), after(vo_got, rows_one)
    qk_second, vo_second = across(qk_got, 2), across(vo_got, 2)
    qk_core, vo_core = across(qk_got, 1), across(vo_got, 1)
    outer_part = part(after(w_outer, qk_got, vo_got))
    inner_got = beside(after(inner_part, qk_got, vo_got))
    rows_one_t, cot_t, perm, perm_in = call(
        functools.partial(turn_kernel, dp=dp, info=info, orders=([1] + bits, [1] + bits_in)), (passages,),
        [(after(numbers, qk_got, vo_got, outer_part), smem), (rows_one, by_passage(width)), (cotangent, by_passage(width))],
        [((width, rows_n), BF16, by_passage_t)] * 2 + [((width, width), BF16, perm_spec)] * 2,
        [], 4 * rows_n * width * width, "turn",
    )
    attn_pieces = [qk_got, qk_core, qk_second, across(after(qk_second, perm), 1)]
    attn_pieces += [vo_got, vo_core, vo_second, across(after(vo_second, perm), 1)]
    outer_got = beside(outer_part)
    inner_got = after(inner_got, perm)
    inner_second = across(inner_got, 2)
    inner_core = across(inner_got, 1)
    q_far, k_far, v_far, ctx_far, lse_far, residual, rows_two, rows_two_t, table_far = call(
        functools.partial(attn_second_kernel, seq=seq, info=info), (1,),
        [(after(numbers, inner_got), smem), (gains, gain_spec), (rows_one, anywhere), (inputs, anywhere),
         (ctx_near, anywhere), (perm_in, anywhere)] + [(a, anywhere) for a in attn_pieces]
        + [(w_output, anywhere)],
        [((rows_n, cols), BF16, anywhere)] * 4 + [((passages, 8, seq), F32, whole_spec((passages, 8, seq)))]
        + [acc_hbm, rows_hbm, turned_hbm, ((16, 128), BF16, table_spec)],
        [bias_scratch] + qkv_scratch + [wo_scratch, wo_scratch, rows_vmem, rows_vmem, cols_vmem]
        + [pltpu.VMEM((width, width), BF16)] + [cols_vmem] * 4 + [acc_vmem, rows_vmem, turned_vmem]
        + [dma((2,)), dma((6,)), dma((7 * passages,))], attn_cost, "attn_second",
    )

    block_hidden = 768 if hidden % 768 == 0 else hidden
    steps = hidden // block_hidden
    chunk_first, chunk_second, chunk_late = min(512, rows_n), rows_n, rows_n
    grad_out = ((width // 2, hidden), BF16, anywhere)
    hidden_vmem = pltpu.VMEM((rows_n, hidden), BF16)
    work_scratch = [rows_vmem] * 2 + [pltpu.VMEM((width, hidden), BF16), pltpu.VMEM((hidden, width), BF16)]
    work_scratch += [turned_vmem] * 2 + [acc_vmem] * 2 + [hidden_vmem] * 2
    work_scratch += [pltpu.VMEM((width // 2, hidden), BF16)] * 4
    ffn_cost = 12 * rows_n * width * hidden
    outer_got = after(outer_got, rows_two)
    outer_second = across(outer_got, 2)
    outer_core = across(outer_got, 1)
    inner_last = across(after(inner_second, rows_two), 1)
    ffn_near, back_near, in_send_near, out_send_near, in_keep_near, out_keep_near = call(
        functools.partial(ffn_first_kernel, chunk=chunk_first, block=block_hidden), (1,),
        [(after(rows_two, outer_got, inner_second, inner_core), anywhere), (cotangent, anywhere),
         (w_inner, anywhere), (w_outer, anywhere), (rows_two_t, anywhere), (cot_t, anywhere)],
        [acc_hbm, acc_hbm] + [grad_out] * 4,
        work_scratch + [dma((2 * (rows_n // chunk_first) + 2 * steps + 2,)), dma((4 * steps + 2,))], ffn_cost, "ffn_first",
    )
    ffn_pieces = [inner_got, inner_core, inner_second, inner_last]
    ffn_pieces += [outer_got, outer_core, outer_second, across(after(outer_second, ffn_near), 1)]

    def whole(array):
        return (array, 0, array.shape[0])

    def part_of(term, n, ways):
        array, which, rows = term
        return (array, which * ways + n, rows // ways)

    def cut(terms, ways=2):
        return [part_of(t, 0, ways) for t in terms], [[part_of(t, n, ways) for t in terms] for n in range(1, ways)]

    def total(terms):
        return sum(array[which * rows : (which + 1) * rows].astype(F32) for array, which, rows in terms)

    def add_up(*groups):
        return [total(terms).astype(BF16) for terms in groups]

    def distances(low_bits):
        return low_bits if len(low_bits) < 2 else [low_bits[1], low_bits[0], low_bits[0] + low_bits[1]]

    out_got_near = across(after(out_send_near, outer_second, inner_last, outer_core), 1)
    in_got_near = across(after(in_send_near, outer_second, inner_last, outer_core), 1)
    outer_near, sent = cut([whole(out_keep_near), whole(out_got_near)])
    inner_near, sent_in = cut([whole(in_keep_near), whole(in_got_near)])
    (outer_near_sent,) = add_up(sent[0])
    (inner_near_sent,) = add_up(sent_in[0])
    outer_near_got = across(outer_near_sent, 2)
    inner_near_got = across(inner_near_sent, bits_in[0])
    (
        layer_out, grad_residual, grad_attn, grad_attn_t, gain_two_part,
        in_send_far, out_send_far, in_keep_far, out_keep_far,
    ) = call(
        functools.partial(
            ffn_second_kernel, chunk=chunk_second, late_chunk=chunk_late, block=block_hidden, info=info), (1,),
        [(after(numbers, outer_near_sent, inner_near_sent), smem), (gains, gain_spec), (rows_two, anywhere),
         (cotangent, anywhere), (rows_two_t, anywhere), (cot_t, anywhere)]
        + [(a, anywhere) for a in ffn_pieces]
        + [(ffn_near, anywhere), (back_near, anywhere), (residual, anywhere), (perm, anywhere)],
        [rows_hbm, acc_hbm, rows_hbm, turned_hbm, small_out] + [grad_out] * 4,
        work_scratch + [acc_vmem] * 3 + [pltpu.VMEM((width, width), BF16)]
        + [rows_vmem, acc_vmem, rows_vmem, turned_vmem]
        + [dma((steps + 1,)), dma((2 * (rows_n // chunk_second) + 6,)),
           dma((4 * steps + 3 * (rows_n // chunk_late) + 1,))],
        ffn_cost, "ffn_second",
    )

    def attn_back(weights, q, k, v, lse, ctx, tab, order, name, vectors=()):
        half_shape = (width // 2, 4 * cols)
        far = not vectors
        sent_shape = half_shape if far else (width // 2, 4 * cols + 256)
        vector_spec = whole_spec((small_rows, 128))
        more_out = [] if far else [((4 * small_rows, 128), F32, whole_spec((4 * small_rows, 128)))]
        more_scratch = [] if far else [pltpu.VMEM((4 * small_rows, 256), BF16)]
        return call(
            functools.partial(attn_back_kernel, seq=seq, info=info, bits=[1] + bits, far=far), (1,),
            [(after(numbers, *order), smem)] + [(w, anywhere) for w in weights] + [(v, vector_spec) for v in vectors]
            + [(grad_attn, anywhere), (q, anywhere), (k, anywhere), (v, anywhere),
               (lse, whole_spec((passages, 8, seq))), (tab, table_spec), (rows_one_t, anywhere),
               (grad_attn_t, anywhere), (ctx, anywhere), (perm, anywhere), (gains, gain_spec)],
            [((rows_n, 3 * cols), BF16, anywhere), (sent_shape, BF16, anywhere)] + more_out
            + [(half_shape, BF16, anywhere), ((8, 128), F32, whole_spec((8, 128))), small_out],
            qkv_scratch + [wo_scratch, rows_vmem] + [cols_vmem] * 3 + [turned_vmem] * 2
            + [cols_vmem, pltpu.VMEM((width, width), BF16), pltpu.VMEM((rows_n, 3 * cols), BF16)]
            + [pltpu.VMEM(half_shape, BF16)] * 2 + [bias_scratch, pltpu.VMEM((heads, seq, seq), F32)]
            + [pltpu.VMEM((width, 3 * cols), F32), dma((4,)), dma((4 * passages + 4,)), dma((passages + 3,))]
            + more_scratch, 2 * rows_n * cols * (5 * width + 5 * seq), name,
        )

    def pack(values, rows):
        high = lax.reduce_precision(values, 8, 7)
        middle = lax.reduce_precision(values - high, 8, 7)
        parts = jnp.concatenate([high, middle], axis=1).astype(BF16)
        return jnp.pad(parts, ((0, rows - parts.shape[0]), (0, 0)))

    def unpack(block):
        return block[:, :128].astype(F32) + block[:, 128:].astype(F32)

    def finish(terms, left, *order):
        for bit in left:
            terms, sent = cut(terms)
            terms = terms + [whole(after(across(total(sent[0]).astype(BF16), bit), *order))]
        return total(terms)

    outer_near_got = after(outer_near_got, grad_attn)
    inner_near_got = after(inner_near_got, grad_attn)
    outer_near = outer_near + [whole(outer_near_got)]
    out_got_far = across(after(out_send_far, outer_near_got, inner_near_got), 1)
    in_got_far = across(after(in_send_far, outer_near_got, inner_near_got), 1)
    inner_near, sent_near = cut(inner_near + [whole(inner_near_got)])
    (inner_near_sent,) = add_up(sent_near[0])
    out_got_far = after(out_got_far, inner_near_sent)
    outer_far, sent = cut([whole(out_keep_far), whole(out_got_far)])
    inner_far, sent_in = cut([whole(in_keep_far), whole(in_got_far)])
    outer_far_sent, inner_far_sent = add_up(sent[0], sent_in[0])
    outer_far_got = across(outer_far_sent, 2)
    inner_far_got = across(inner_far_sent, bits_in[0])
    inner_near_got = across(inner_near_sent, bits_in[1])
    d_far, ag_send_far, ag_keep_far, table_part_far, gain_part_far = attn_back(
        attn_pieces, q_far, k_far, v_far, lse_far, ctx_far, table_far,
        [outer_far_sent, inner_far_sent, inner_near_sent], "attn_back_far",
    )
    outer_far_got = after(outer_far_got, d_far)
    inner_far_got = after(inner_far_got, d_far)
    inner_near_got = after(inner_near_got, d_far)
    ag_got_far = across(after(ag_send_far, outer_far_got, inner_far_got, inner_near_got), 1)
    outer_far = outer_far + [whole(outer_far_got)]
    inner_near = inner_near + [whole(inner_near_got)]
    inner_far, sent_in = cut(inner_far + [whole(inner_far_got)])
    outer_far_x, inner_far_sent = add_up(outer_far, sent_in[0])
    outer_x_got = beside(outer_far_x)
    inner_far_got = across(inner_far_sent, bits_in[1])
    attn_far, sent = cut([whole(ag_keep_far), whole(ag_got_far)])
    (attn_far_sent,) = add_up(sent[0])
    attn_far_got = across(attn_far_sent, 2)
    order = [outer_far_x, inner_far_sent, attn_far_sent]
    d_near, ag_send_near, vectors_own, ag_keep_near, _, _ = attn_back(
        [w_query, w_key, w_value, w_output], q_near, k_near, v_near, lse_near, ctx_near, table, order,
        "attn_back_near", (gain_two_part, gain_part_far, table_part_far),
    )
    attn_far_got = after(attn_far_got, d_near)
    inner_far_got = after(inner_far_got, d_near)
    outer_x_got = after(outer_x_got, d_near)
    ag_got_near = across(after(ag_send_near, attn_far_got, inner_far_got, outer_x_got), 1)
    vectors = vectors_own + unpack(ag_got_near[: 4 * small_rows, 4 * cols :])
    same = vectors + across(vectors, 2)
    outer, sent = cut(outer_near + [whole(outer_x_got)], 2 ** len(upper[:2]))
    outer_sent = add_up(*sent)
    block = pack(same, outer_sent[0].shape[0])
    outer_sent = [jnp.concatenate([v, block], axis=1) for v in outer_sent]
    outer_got = [across(v, d) for v, d in zip(outer_sent, distances(upper[:2]), strict=True)]
    far_x = jnp.concatenate(
        [total(attn_far + [whole(attn_far_got)]), total(inner_far + [whole(inner_far_got)])], axis=0).astype(BF16)
    far_x_got = beside(far_x)
    attn_near, sent = cut([whole(ag_keep_near), whole(ag_got_near[:, : 4 * cols])])
    (attn_near_sent,) = add_up(sent[0])
    attn_near_got = across(after(attn_near_sent, same), 2)
    order = [far_x, attn_near_sent] + outer_sent
    (grad_input,) = call(
        functools.partial(input_back_kernel, info=info), (passages,),
        [(after(numbers, *order), smem),
         (inputs, by_passage(width)), (gains, gain_spec), (grad_residual, by_passage(width)),
         (d_near, by_passage(3 * cols)), (d_far, by_passage(3 * cols)),
         (w_query, weight_spec), (w_key, weight_spec), (w_value, weight_spec)]
        + [(a, anywhere) for a in attn_pieces],
        [((rows_n, width), F32, by_passage(width))],
        qkv_scratch + [dma], 12 * rows_n * width * cols, "input_back",
    )
    far_x_got = after(far_x_got, grad_input)
    rows = attn_near_sent.shape[0]
    attn_near_got = after(attn_near_got, grad_input, far_x_got, *outer_got)
    attn, sent = cut(attn_near + [whole(attn_near_got), whole(far_x_got[:rows])], 2 ** len(upper[:2]))
    attn_sent = add_up(*sent)
    attn_got = [across(v, d) for v, d in zip(attn_sent, distances(upper[:2]), strict=True)]
    inner = inner_near + [whole(after(far_x_got, *attn_sent)[rows:])]
    grad_inner = finish(inner, bits_in[2:])
    outer_got = [after(got, *attn_sent) for got in outer_got]
    outer = outer + [whole(got[:, :hidden]) for got in outer_got]
    small = same + unpack(sum(got[: 4 * small_rows, hidden:].astype(F32) for got in outer_got))
    for bit in upper[2:]:
        small = small + across(small, bit)
    other = beside(small)
    table_at = 2 * small_rows
    small = jnp.concatenate(
        [small[:table_at] + other[:table_at], small[table_at : table_at + 8] + other[table_at + 8 :]], axis=0)
    grad_outer = finish(outer, upper[2:]).T
    attn_grads = finish(attn + [whole(after(got, grad_inner, grad_outer)) for got in attn_got], upper[2:])
    grad_query, grad_key, grad_value = (attn_grads[:, n * cols : (n + 1) * cols] for n in range(3))
    grad_output = attn_grads[:, 3 * cols :].T

    grad_gain_one = small[: width // 128].reshape(width)
    grad_gain_two = small[small_rows : small_rows + width // 128].reshape(width)
    grad_table = small[table_at : table_at + heads, :BUCKETS].T
    return (
        layer_out, grad_input, grad_gain_one, grad_query, grad_key, grad_value, grad_output,
        grad_table, grad_gain_two, grad_inner, grad_outer,
    )


def solution(mesh):
    both = ("dp", "tensor")
    in_specs = (
        P(both, None), P(), P(None, "tensor"), P(None, "tensor"), P(None, "tensor"), P("tensor", None),
        P(None, "tensor"), P(), P(None, "tensor"), P("tensor", None), P("dp"), P(both, None),
    )
    out_specs = (
        P(both, None), P(both, None), P(), P("dp", "tensor"), P("dp", "tensor"), P("dp", "tensor"),
        P("tensor", "dp"), P(None, "tensor"), P(), P("dp", "tensor"), P("tensor", "dp"),
    )
    body = functools.partial(shards, dp=mesh.shape["dp"], tp=mesh.shape["tensor"])
    return jax.shard_map(body, mesh=mesh, in_specs=in_specs, out_specs=out_specs, check_vma=False)
```
